32 devices in a mesh: gx: 2 (over x), gy: 4 (over z), gz: 4 (over y, core).
Axes of the slice: x: 2, y: 2, z: 4, core: 2. Of those that a mesh axis runs over, the one named last changes fastest.
Arguments:
- load_cases: float32 [2, 4, 4, 1158, 128], P('gx', 'gy', 'gz'), may hold values from -6 to 6
- schur_matrix: bfloat16 [2, 4, 4, 1158, 1158], P('gx', 'gy', 'gz'), may hold values from -0.25 to 3.25, as said below
- local_inverse: bfloat16 [2, 4, 4, 1158, 1158], P('gx', 'gy', 'gz'), may hold values from -0.05 to 0.45, as said below
- coarse_basis: bfloat16 [2, 4, 4, 6, 1158], P('gx', 'gy', 'gz'), may hold values from -0.25 to 0.25
- coarse_inverse: float32 [192, 192], P(('gx', 'gy', 'gz')), may hold values from -0.4 to 2.9, as said below
- canon_rows: int32 [2, 4, 4, 1158], P('gx', 'gy', 'gz'), may hold values from 0 to 1157, each once within a row
Outputs:
- solution: float32 [2, 4, 4, 1158, 128], P('gx', 'gy', 'gz')
- residual: float32 [2, 4, 4, 1158, 128], P('gx', 'gy', 'gz')
The draws below stay inside these ranges and needn't reach their ends.
Inputs may be any that keep to these rules, and one draw needn't show every extreme that they name: `schur_matrix`: symmetric for every subdomain. `local_inverse`: symmetric for every subdomain. `coarse_inverse`: symmetric. `canon_rows`: each subdomain's row is a permutation of 0 to 1157.
All inputs are finite; a program needn't handle non-finite values.
Results may differ from the reference program's by a relative error of at most 0.0044.
Values sent between devices are 32-bit elements; how exact they have to be, the bound alone decides.
No kernel may reach another device: no remote copies, remote signals or barrier semaphores. Data moves between devices by JAX's collectives and lax.ppermute only.
A program may use at most 128 MiB of HBM per device.

```python
import math
import jax
import jax.numpy as jnp
from jax import lax

NODES = 7
DOF = 3
MODES = 6
LOADS = 128
ITERS = 3
IFACE = 1158
SUB_X = 2
SUB_Y = 4
SUB_Z = 4
NC = 192


def symmetric_block(key, order, low, high, entry_scale):
    diag_key, noise_key = jax.random.split(key)
    noise = jax.random.truncated_normal(noise_key, -4.0, 4.0, (order, order), jnp.float32)
    diagonal = jax.random.uniform(diag_key, (order,), jnp.float32, low, high)
    mixed = (noise + noise.T) * (entry_scale / math.sqrt(2.0))
    return mixed + jnp.diag(diagonal)


def draw_schur_matrix(key, part):
    subkeys = jax.random.split(jax.random.fold_in(key, 11), SUB_X * SUB_Y * SUB_Z)
    blocks = lax.map(lambda one_key: symmetric_block(one_key, IFACE, 1.5, 3.0, 0.5 / math.sqrt(IFACE)).astype(jnp.bfloat16), subkeys)
    return blocks.reshape(SUB_X, SUB_Y, SUB_Z, IFACE, IFACE)


def draw_local_inverse(key, part):
    subkeys = jax.random.split(jax.random.fold_in(key, 23), SUB_X * SUB_Y * SUB_Z)
    blocks = lax.map(lambda one_key: symmetric_block(one_key, IFACE, 0.2, 0.4, 0.1 / math.sqrt(IFACE)).astype(jnp.bfloat16), subkeys)
    return blocks.reshape(SUB_X, SUB_Y, SUB_Z, IFACE, IFACE)


def draw_coarse_inverse(key, part):
    return symmetric_block(jax.random.fold_in(key, 37), NC, 1.5, 2.5, 0.06)


def level_of(stream_key, shape, cuts, smallest, high):
    def one(axis_at, parts):
        steps = jax.random.uniform(jax.random.fold_in(jax.random.fold_in(stream_key, 6), axis_at), (parts,), jnp.float32, smallest / len(cuts), high / len(cuts))
        return jnp.repeat(jnp.exp(steps), shape[axis_at] // parts).reshape((-1,) + (1,) * (len(shape) - axis_at - 1))

    gain = one(*cuts[0])
    for cut in cuts[1:]:
        gain = gain * one(*cut)
    return gain


def normal_values(own_key, shape, spread, limit, cuts=(), kind=jnp.bfloat16):
    result = jax.random.normal(own_key, shape, jnp.float32) * spread
    if len(cuts) > 0:
        result = level_of(own_key, shape, cuts, -0.22, 0.18) * result
    return jnp.clip(result, min=-limit, max=limit).astype(kind)


def setup_inputs(seed: int = 0) -> dict:
    streams_of = jax.random.split(jax.random.key(seed), 7)
    return {
        "load_cases": normal_values(streams_of[0], (SUB_X, SUB_Y, SUB_Z, IFACE, LOADS), 1.0, 6.0, ((0, 2), (1, 4), (2, 4)), jnp.float32),
        "schur_matrix": draw_schur_matrix(jax.random.fold_in(streams_of[6], 71), 0),
        "local_inverse": draw_local_inverse(jax.random.fold_in(streams_of[6], 71), 0),
        "coarse_basis": normal_values(streams_of[3], (SUB_X, SUB_Y, SUB_Z, MODES, IFACE), (IFACE // 2) ** -0.5, 0.25, ((0, 2), (1, 4), (2, 4))),
        "coarse_inverse": draw_coarse_inverse(jax.random.fold_in(streams_of[6], 71), 0),
        "canon_rows": jax.vmap(lambda own: jax.random.permutation(own, IFACE))(jax.random.split(streams_of[5], SUB_X * SUB_Y * SUB_Z)).reshape((SUB_X, SUB_Y, SUB_Z, IFACE)).astype(jnp.int32),
    }


def slot_table(node_count, freedom):
    entries = []
    offset = 0
    for first in range(3):
        for second in range(3):
            for third in range(3):
                placed = (first, second, third)
                if placed == (1, 1, 1):
                    continue
                inside = sum(1 for facing in placed if facing == 1)
                length = freedom * node_count ** inside
                entries.append((placed, offset, length))
                offset += length
    return entries


def mirror(placed, direction):
    return tuple(2 if coord_pos == direction else coord_val for coord_pos, coord_val in enumerate(placed))


def side_factor(facing, position, extent):
    if facing == 1:
        return jnp.ones_like(position).astype(jnp.float32)
    if facing == 0:
        return jnp.where(position > 0, 2.0, 1.0).astype(jnp.float32)
    return jnp.where(position < extent - 1, 2.0, 1.0).astype(jnp.float32)


def from_lower(array, axis_num):
    extent = array.shape[axis_num]
    zeros_part = jnp.zeros_like(lax.slice_in_dim(array, 0, 1, axis=axis_num))
    return jnp.concatenate([zeros_part, lax.slice_in_dim(array, 0, extent - 1, axis=axis_num)], axis=axis_num)


def from_upper(array, axis_num):
    extent = array.shape[axis_num]
    zeros_part = jnp.zeros_like(lax.slice_in_dim(array, 0, 1, axis=axis_num))
    return jnp.concatenate([lax.slice_in_dim(array, 1, extent, axis=axis_num), zeros_part], axis=axis_num)


def local_pair(operands):
    inverse_one, basis_one, scaled_one = operands
    return (jnp.dot(inverse_one, scaled_one, preferred_element_type=jnp.float32),
            jnp.dot(basis_one, scaled_one, preferred_element_type=jnp.float32))


def lift_coarse(operands):
    basis_one, correction_one = operands
    return jnp.dot(basis_one.astype(jnp.float32).T, correction_one, precision=lax.Precision.HIGHEST,
                   preferred_element_type=jnp.float32)


def apply_schur(operands):
    schur_one, update_one = operands
    return jnp.dot(schur_one, update_one, preferred_element_type=jnp.float32)


def reference(load_cases, schur_matrix, local_inverse, coarse_basis, coarse_inverse, canon_rows):
    entries = slot_table(NODES, DOF)
    back_rows = jnp.argsort(canon_rows, axis=-1).astype(jnp.int32)
    grid_pos = (jnp.arange(SUB_X).reshape(-1, 1, 1), jnp.arange(SUB_Y).reshape(1, -1, 1),
                jnp.arange(SUB_Z).reshape(1, 1, -1))
    extents = (SUB_X, SUB_Y, SUB_Z)
    weight_parts = []
    for placed, offset, length in entries:
        factor = jnp.ones((SUB_X, SUB_Y, SUB_Z), jnp.float32)
        for axis_num in range(3):
            factor = factor * side_factor(placed[axis_num], grid_pos[axis_num], extents[axis_num])
        weight_parts.append(jnp.broadcast_to((1.0 / factor)[..., None], (SUB_X, SUB_Y, SUB_Z, length)))
    weight_canon = jnp.concatenate(weight_parts, axis=3)
    weight_local = jnp.take_along_axis(weight_canon, back_rows, axis=3)

    def assemble(values):
        canonical = jnp.take_along_axis(values, canon_rows[..., None], axis=3)
        pieces = {placed: canonical[:, :, :, offset:offset + length] for placed, offset, length in entries}
        for direction in range(3):
            lower_keys = [placed for placed, offset, length in entries if placed[direction] == 0]
            upper_keys = [mirror(placed, direction) for placed in lower_keys]
            lower = jnp.concatenate([pieces[placed] for placed in lower_keys], axis=3)
            upper = jnp.concatenate([pieces[placed] for placed in upper_keys], axis=3)
            new_lower = lower + from_lower(upper, direction)
            new_upper = upper + from_upper(lower, direction)
            position = 0
            for lower_key, upper_key in zip(lower_keys, upper_keys):
                length = pieces[lower_key].shape[3]
                pieces[lower_key] = new_lower[:, :, :, position:position + length]
                pieces[upper_key] = new_upper[:, :, :, position:position + length]
                position += length
        joined = jnp.concatenate([pieces[placed] for placed, offset, length in entries], axis=3)
        return jnp.take_along_axis(joined, back_rows[..., None], axis=3)

    count_sub = SUB_X * SUB_Y * SUB_Z
    full_shape = (SUB_X, SUB_Y, SUB_Z, IFACE, LOADS)
    flat_inverse = local_inverse.reshape(count_sub, IFACE, IFACE)
    flat_schur = schur_matrix.reshape(count_sub, IFACE, IFACE)
    flat_basis = coarse_basis.reshape(count_sub, MODES, IFACE)
    residual = assemble(load_cases)
    solution = jnp.zeros(full_shape, jnp.float32)
    for iteration in range(ITERS):
        scaled = (weight_local[..., None] * residual).astype(jnp.bfloat16)
        local_term, restricted = lax.map(local_pair, (flat_inverse, flat_basis, scaled.reshape(count_sub, IFACE, LOADS)))
        coarse = jnp.dot(coarse_inverse, restricted.reshape(NC, LOADS), precision=lax.Precision.HIGHEST,
                         preferred_element_type=jnp.float32)
        correction = coarse.reshape(count_sub, MODES, LOADS)
        combined = local_term + lax.map(lift_coarse, (flat_basis, correction))
        update = assemble(weight_local[..., None] * combined.reshape(full_shape))
        solution = solution + update
        product = lax.map(apply_schur, (flat_schur, update.astype(jnp.bfloat16).reshape(count_sub, IFACE, LOADS)))
        residual = residual - assemble(product.reshape(full_shape))
    return solution, residual
```

```python
import functools
import itertools

import jax
import jax.numpy as jnp
from jax import lax
from jax.experimental import pallas as pl
from jax.experimental.pallas import tpu as pltpu
from jax.sharding import PartitionSpec as P

NODES = 7
DOF = 3
ITERS = 3
AXES = ("gx", "gy", "gz")
STAGES = ((2,), (0, 1))
PAD = 8
TILE = 256
F32 = jnp.float32
BF16 = jnp.bfloat16


def piece_length(placed):
    return DOF * NODES ** sum(1 for c in placed if c == 1)


PLACES = [p for p in itertools.product(range(3), repeat=3) if p != (1, 1, 1)]
CANON_OFFSET = {}
_at = 0
for _p in PLACES:
    CANON_OFFSET[_p] = _at
    _at += piece_length(_p)
IFACE = _at
SLOT_OFFSET = {}
SLOT_ROWS = {}
_at = 0
for _p in PLACES:
    SLOT_OFFSET[_p] = _at
    SLOT_ROWS[_p] = -(-piece_length(_p) // PAD) * PAD
    _at += SLOT_ROWS[_p]
COARSE_AT = _at
ROWS = -(-(COARSE_AT + 16) // TILE) * TILE


class Message:
    def __init__(self, moves, sizes):
        self.moves = moves
        self.sizes = sizes
        self.faces = "C" not in moves
        self.slots = []
        if self.faces:
            for place in PLACES:
                if all(m is None or c == (0 if m == "A" else 2) for m, c in zip(moves, place)):
                    self.slots.append(place)
        self.rows = sum(SLOT_ROWS[s] for s in self.slots)

    def xor(self):
        code = 0
        for move, size in zip(self.moves, self.sizes):
            code = code * size + {None: 0, "A": 1, "B": 3, "C": 2}[move]
        return code

    def pairs(self):
        out = []
        for place in itertools.product(*(range(s) for s in self.sizes)):
            to = []
            for at, move, size in zip(place, self.moves, self.sizes):
                if move == "A":
                    at = at ^ 1
                elif move == "B":
                    at = (at - 1) % size if at % 2 == 0 else (at + 1) % size
                elif move == "C":
                    at = at ^ 2
                to.append(at)
            flat = [0, 0]
            for a, b, size in zip(place, to, self.sizes):
                flat = [flat[0] * size + a, flat[1] * size + b]
            out.append(tuple(flat))
        return out


def ports(size):
    return ("A",) if size == 2 else ("A", "B")


def stage_messages(dims, sizes, coarse):
    choices = []
    for d in range(3):
        if d not in dims:
            choices.append((None,))
        else:
            extra = ("C",) if coarse and sizes[d] == 4 else ()
            choices.append((None,) + ports(sizes[d]) + extra)
    return [Message(m, sizes) for m in itertools.product(*choices) if any(c is not None for c in m)]


class Plan:
    def __init__(self, sizes):
        self.sizes = sizes
        self.subs = sizes[0] * sizes[1] * sizes[2]
        self.ride = all(s in (2, 4) for s in sizes)
        self.plain = [stage_messages(d, sizes, False) for d in STAGES]
        self.coarse = [stage_messages(d, sizes, True) for d in STAGES]
        self.wide = self.subs * 8

    def messages(self, coarse):
        return self.coarse if coarse and self.ride else self.plain


def position():
    return [lax.axis_index(a) for a in AXES]


def has_b(index, size):
    if size == 2:
        return None
    return jnp.logical_and(index > 0, index < size - 1)


def pick(slot, index, of):
    def choose(d, place):
        if d == 3:
            return of(tuple(place))
        if slot[d] == 1:
            return choose(d + 1, place + [1])
        even, odd = (2, 0) if slot[d] == 0 else (0, 2)
        return jnp.where(index[d] % 2 == 0, choose(d + 1, place + [even]), choose(d + 1, place + [odd]))

    return choose(0, [])


def add_received(plan, index, messages, received, acc, width):
    for message, ref in zip(messages, received):
        if not message.faces:
            continue
        ok = None
        for d, move in enumerate(message.moves):
            if move == "B":
                here = has_b(index[d], plan.sizes[d])
                ok = here if ok is None else jnp.logical_and(ok, here)
        at = 0
        for slot in message.slots:
            rows, to = SLOT_ROWS[slot], SLOT_OFFSET[slot]
            value = ref[at : at + rows, :width]
            if ok is not None:
                value = jnp.where(ok, value, 0.0)
            acc[to : to + rows, :width] += value
            at += rows


def write_payloads(messages, outs, acc, blocks):
    for message, out in zip(messages, outs):
        at = 0
        for slot in message.slots:
            rows, frm = SLOT_ROWS[slot], SLOT_OFFSET[slot]
            out[at : at + rows, :] = acc[frm : frm + rows, :]
            at += rows
        for block in blocks:
            out[at : at + 8, :128] = block
            if out.shape[1] > 128:
                out[at : at + 8, 128:] = jnp.zeros((8, out.shape[1] - 128), F32)
            at += 8


def payload_shapes(messages, blocks, width):
    return [jax.ShapeDtypeStruct((m.rows + 8 * blocks, width), F32) for m in messages]


def transfer(messages, payloads):
    return [lax.ppermute(p, AXES, m.pairs()) for m, p in zip(messages, payloads)]


def vm():
    return pl.BlockSpec(memory_space=pltpu.VMEM)


def call(kernel, outs, operands, specs=None, scratch=(), limit=20, flops=0):
    nbytes = sum(o.size * o.dtype.itemsize for o in list(outs) + list(operands))
    return pl.pallas_call(
        kernel,
        out_shape=tuple(outs),
        in_specs=specs or [vm()] * len(operands),
        out_specs=tuple(vm() for _ in outs),
        scratch_shapes=list(scratch),
        compiler_params=pltpu.CompilerParams(vmem_limit_bytes=limit << 20),
        cost_estimate=pl.CostEstimate(flops=flops, bytes_accessed=nbytes, transcendentals=0),
    )(*operands)


def gather_rows(index, canon, load, acc):
    for slot in PLACES:
        rows, at = SLOT_ROWS[slot], SLOT_OFFSET[slot]
        acc[at + rows - 8 : at + rows, :] = jnp.zeros((8, acc.shape[1]), F32)
    acc[COARSE_AT:, :] = jnp.zeros((ROWS - COARSE_AT, acc.shape[1]), F32)
    for slot in PLACES:
        length, at = piece_length(slot), SLOT_OFFSET[slot]
        off = pick(slot, index, lambda place: jnp.int32(CANON_OFFSET[place]))
        step = 7 if length % 7 == 0 else 3

        def body(i, _, off=off, at=at, step=step):
            for j in range(step):
                row = i * step + j
                acc[pl.ds(at + row, 1), :] = load[canon[off + row], :, :]
            return 0

        lax.fori_loop(0, length // step, body, 0)


def input_kernel(plan, canon, load, acc, *outs):
    gather_rows(position(), canon, load, acc)
    write_payloads(plan.plain[0], outs, acc, [])


def scatter_rows(index, canon, pairs):
    for slot in PLACES:
        length, at = piece_length(slot), SLOT_OFFSET[slot]
        off = pick(slot, index, lambda place: jnp.int32(CANON_OFFSET[place]))
        step = 7 if length % 7 == 0 else 3

        def body(i, _, off=off, at=at, step=step):
            for j in range(step):
                row = i * step + j
                to = canon[off + row]
                for acc, out in pairs:
                    out[to, :, :] = acc[pl.ds(at + row, 1), :]
            return 0

        lax.fori_loop(0, length // step, body, 0)


def split(value, parts):
    out = []
    for _ in range(parts):
        piece = value.astype(BF16)
        out.append(piece)
        value = value - piece.astype(F32)
    return out


def dot(a, b):
    return jnp.dot(a, b, preferred_element_type=F32)


def dot_last(a, b):
    return lax.dot_general(a, b, (((1,), (1,)), ((), ())), preferred_element_type=F32)


def prepare_kernel(plan, canon, inverse, schur, basis, cinv, inverse_out, schur_out, k_out, src, wgt, one, one_w, mid):
    index = position()
    src[...] = jnp.full(src.shape, -1, jnp.int32)
    wgt[...] = jnp.zeros(wgt.shape, F32)
    for slot in PLACES:
        at, length = SLOT_OFFSET[slot], piece_length(slot)
        src[at : at + length, :] = pick(
            slot, index, lambda place, length=length: canon[CANON_OFFSET[place] : CANON_OFFSET[place] + length, :]
        )
        weight = jnp.float32(1.0)
        for d in range(3):
            if slot[d] == 0:
                weight = weight * 0.5
            elif slot[d] == 2 and plan.sizes[d] > 2:
                weight = weight * jnp.where(has_b(index[d], plan.sizes[d]), 0.5, 1.0)
        wgt[at : at + length, :] = jnp.full((length, 1), 1.0, F32) * weight

    if plan.ride:
        nc = cinv.shape[1]
        row = lax.broadcasted_iota(jnp.int32, (nc, plan.wide), 0)
        col = lax.broadcasted_iota(jnp.int32, (nc, plan.wide), 1)
        spread = jnp.where(jnp.logical_and((col >> 3) * 6 + (col & 7) == row, (col & 7) < 6), 1.0, 0.0).astype(BF16)
        spread_inverse = [dot(part, spread).astype(BF16) for part in split(cinv[...], 3)]

    def tile(t):
        return pl.ds(pl.multiple_of(t * TILE, TILE), TILE)

    def build(t, _):
        hit = src[tile(t), :] == lax.broadcasted_iota(jnp.int32, (TILE, IFACE), 1)
        one[tile(t), :] = jnp.where(hit, 1.0, 0.0).astype(BF16)
        one_w[tile(t), :] = jnp.where(hit, wgt[tile(t), :], 0.0).astype(BF16)
        return 0

    lax.fori_loop(0, ROWS // TILE, build, 0)

    def left(t, _):
        mid[tile(t), :] = dot(one_w[tile(t), :], inverse[...]).astype(BF16)
        return 0

    lax.fori_loop(0, ROWS // TILE, left, 0)
    mid[COARSE_AT : COARSE_AT + 16, :] = basis[...]

    def right(t, _):
        inverse_out[tile(t), :] = dot_last(mid[tile(t), :], one_w[...]).astype(BF16)
        turned = dot_last(one_w[tile(t), :], basis[...])
        if plan.ride:
            turned = turned.astype(BF16)
            k_out[tile(t), :] = sum(dot(turned, part) for part in spread_inverse)
        else:
            k_out[tile(t), :] = turned
        return 0

    lax.fori_loop(0, ROWS // TILE, right, 0)

    def left_s(t, _):
        mid[tile(t), :] = dot(one[tile(t), :], schur[...]).astype(BF16)
        return 0

    lax.fori_loop(0, ROWS // TILE, left_s, 0)

    def right_s(t, _):
        schur_out[tile(t), :] = dot_last(mid[tile(t), :], one[...]).astype(BF16)
        return 0

    lax.fori_loop(0, ROWS // TILE, right_s, 0)


def middle_kernel(plan, coarse, width, *refs):
    first, second = plan.messages(coarse)
    ride = coarse and plan.ride
    base, received = refs[0], refs[1 : 1 + len(first)]
    outs, acc = refs[1 + len(first) : -1], refs[-1]
    acc[...] = base[...]
    add_received(plan, position(), first, received, acc, width)
    blocks = []
    if ride:
        blocks.append(base[COARSE_AT : COARSE_AT + 8, :128])
        for message, ref in zip(first, received):
            blocks.append(ref[message.rows : message.rows + 8, :128])
    write_payloads(second, outs, acc, blocks)


def multiply(matrix, vector, out):
    for t in range(ROWS // TILE):
        out[t * TILE : (t + 1) * TILE, :128] = dot(matrix[t * TILE : (t + 1) * TILE, :], vector)


def inverse_kernel(plan, opening, *refs):
    first, second = plan.plain
    refs = list(refs)
    base = refs.pop(0)
    got = [refs.pop(0) for _ in range(len(first) + len(second))]
    matrix = refs.pop(0)
    third = refs.pop(0) if plan.ride or not opening else None
    residual, out = refs.pop(0), refs.pop(0)
    acc = refs.pop(-1)
    outs = refs
    index = position()
    acc[...] = base[...]
    add_received(plan, index, first, got[: len(first)], acc, 128)
    add_received(plan, index, second, got[len(first) :], acc, 128)
    value = acc[...] if opening else third[...] - acc[...]
    residual[...] = value
    multiply(matrix, value.astype(BF16), out)
    if plan.ride:
        if opening:
            out[:, 128:] = third[...]
        write_payloads(plan.coarse[0], outs, out, [out[COARSE_AT : COARSE_AT + 8, :128]])


def lift_kernel(plan, base, turned, correction, out, *outs):
    lifted = turned[...].astype(BF16)
    out[...] = base[...] + sum(dot(lifted, part) for part in split(correction[...], 3))
    write_payloads(plan.plain[0], outs, out, [])


def schur_kernel(plan, opening, *refs):
    first, second = plan.messages(True)
    refs = list(refs)
    base = refs.pop(0)
    got = [refs.pop(0) for _ in range(len(first) + len(second))]
    matrix = refs.pop(0)
    width = base.shape[1]
    sol_in = None if opening else refs.pop(0)
    if plan.ride and not opening:
        h_high, h_low = refs.pop(0), refs.pop(0)
    sol, out = refs.pop(0), refs.pop(0)
    outs = refs[: len(plan.plain[0])]
    refs = refs[len(plan.plain[0]) :]
    if plan.ride and opening:
        h_high, h_low = refs.pop(0), refs.pop(0)
    acc, stack = refs
    index = position()
    acc[...] = base[...]
    add_received(plan, index, first, got[: len(first)], acc, width)
    add_received(plan, index, second, got[len(first) :], acc, width)
    if plan.ride and opening:
        high = acc[:, 128:].astype(BF16)
        h_high[...] = high
        h_low[...] = (acc[:, 128:] - high.astype(F32)).astype(BF16)
    if plan.ride:
        me = (index[0] * plan.sizes[1] + index[1]) * plan.sizes[2] + index[2]
        near = [0] + [m.xor() for m in first]
        values = [base[COARSE_AT : COARSE_AT + 8, :128]]
        values += [ref[m.rows : m.rows + 8, :128] for m, ref in zip(first, got)]
        for code, value in zip(near, values):
            stack[pl.ds(pl.multiple_of((me ^ code) * 8, 8), 8), :] = value
        for m, ref in zip(second, got[len(first) :]):
            for i, code in enumerate(near):
                at = m.rows + 8 * i
                to = pl.multiple_of((me ^ code ^ m.xor()) * 8, 8)
                stack[pl.ds(to, 8), :] = ref[at : at + 8, :128]
        r_high, r_low = split(stack[...], 2)
        update = acc[:, :128] + dot(h_high[...], r_high) + dot(h_high[...], r_low) + dot(h_low[...], r_high)
    else:
        update = acc[...]
    sol[...] = update if opening else sol_in[...] + update
    multiply(matrix, update.astype(BF16), out)
    write_payloads(plan.plain[0], outs, out, [])


def output_kernel(plan, canon, base, *refs):
    first, second = plan.plain
    count = len(first) + len(second)
    got = refs[:count]
    residual, sol, sol_out, residual_out, acc = refs[count:]
    index = position()
    acc[...] = base[...]
    add_received(plan, index, first, got[: len(first)], acc, 128)
    add_received(plan, index, second, got[len(first) :], acc, 128)
    acc[...] = residual[...] - acc[...]
    scatter_rows(index, canon, [(sol, sol_out), (acc, residual_out)])


def shape(rows, cols, dtype=F32):
    return jax.ShapeDtypeStruct((rows, cols), dtype)


def local(plan, load_cases, schur_matrix, local_inverse, coarse_basis, coarse_inverse, canon_rows):
    smem = pl.BlockSpec(memory_space=pltpu.SMEM)
    loads = load_cases.shape[-1]
    canon = canon_rows.reshape(IFACE)
    load = load_cases.reshape(IFACE, 1, loads)
    basis = jnp.pad(coarse_basis[0, 0, 0], ((0, 10), (0, 0)))
    cinv = jnp.pad(coarse_inverse, ((0, 10), (0, 0)))
    plain, coarse = plan.plain, plan.messages(True)
    acc = pltpu.VMEM((ROWS, 128), F32)

    def middle(is_coarse, base, got):
        width = base.shape[1]
        first, second = plan.messages(is_coarse)
        blocks = len(first) + 1 if is_coarse and plan.ride else 0
        return call(
            functools.partial(middle_kernel, plan, is_coarse, width),
            payload_shapes(second, blocks, width),
            [base] + got,
            scratch=[pltpu.VMEM((ROWS, width), F32)],
            limit=40 if width > 512 else 20,
        )

    def assemble(is_coarse, base, payloads):
        first, second = plan.messages(is_coarse)
        got = transfer(first, payloads)
        return got + transfer(second, middle(is_coarse, base, got))

    base, *payloads = call(
        functools.partial(input_kernel, plan),
        [shape(ROWS, 128)] + payload_shapes(plain[0], 0, 128),
        [canon, load],
        specs=[smem, vm()],
    )
    inverse, schur, third = call(
        functools.partial(prepare_kernel, plan),
        [shape(ROWS, ROWS, BF16), shape(ROWS, ROWS, BF16), shape(ROWS, plan.wide if plan.ride else 16)],
        [canon_rows.reshape(IFACE, 1), local_inverse[0, 0, 0], schur_matrix[0, 0, 0], basis, cinv],
        scratch=[
            pltpu.VMEM((ROWS, 1), jnp.int32),
            pltpu.VMEM((ROWS, 1), F32),
            pltpu.VMEM((ROWS, IFACE), BF16),
            pltpu.VMEM((ROWS, IFACE), BF16),
            pltpu.VMEM((ROWS, IFACE), BF16),
        ],
        limit=56,
        flops=4 * 2 * ROWS * IFACE * IFACE,
    )
    got = assemble(False, base, payloads)
    sol, turned = None, third
    flops = 2 * ROWS * ROWS * 128
    for iteration in range(ITERS):
        opening = iteration == 0
        width = 128 + plan.wide if opening and plan.ride else 128
        residual, base, *payloads = call(
            functools.partial(inverse_kernel, plan, opening),
            [shape(ROWS, 128), shape(ROWS, width)] + (payload_shapes(coarse[0], 1, width) if plan.ride else []),
            [base] + got + [inverse] + ([third] if plan.ride or not opening else []),
            scratch=[acc],
            flops=flops,
        )
        if not plan.ride:
            rows = lax.all_gather(base[COARSE_AT : COARSE_AT + 6], AXES, axis=0, tiled=True)
            correction = jnp.dot(cinv, rows, precision=lax.Precision.HIGHEST, preferred_element_type=F32)
            base, *payloads = call(
                functools.partial(lift_kernel, plan),
                [shape(ROWS, 128)] + payload_shapes(plain[0], 0, 128),
                [base, turned, correction],
            )
        got = assemble(True, base, payloads)
        kept = []
        if plan.ride:
            kept = [shape(ROWS, plan.wide, BF16)] * 2 if opening else [h_high, h_low]
        results = call(
            functools.partial(schur_kernel, plan, opening),
            [shape(ROWS, 128), shape(ROWS, 128)] + payload_shapes(plain[0], 0, 128) + (kept if opening else []),
            [base] + got + [schur] + ([] if opening else [sol] + kept),
            scratch=[pltpu.VMEM((ROWS, width), F32), pltpu.VMEM((plan.wide, 128), F32)],
            flops=flops,
        )
        sol, base, *payloads = results[: 2 + len(plain[0])]
        if plan.ride and opening:
            h_high, h_low = results[-2:]
        got = assemble(False, base, payloads)
        third = residual
    out = jax.ShapeDtypeStruct((IFACE, 1, loads), F32)
    sol_out, residual_out = call(
        functools.partial(output_kernel, plan),
        [out, out],
        [canon, base] + got + [residual, sol],
        specs=[smem] + [vm()] * (3 + len(got)),
        scratch=[acc],
    )
    return tuple(o.reshape(1, 1, 1, IFACE, loads) for o in (sol_out, residual_out))


def solution(mesh):
    plan = Plan(tuple(mesh.shape[a] for a in AXES))
    in_specs = (
        P("gx", "gy", "gz", None, None),
        P("gx", "gy", "gz", None, None),
        P("gx", "gy", "gz", None, None),
        P("gx", "gy", "gz", None, None),
        P(("gx", "gy", "gz"), None),
        P("gx", "gy", "gz", None),
    )
    out_specs = (P("gx", "gy", "gz", None, None), P("gx", "gy", "gz", None, None))
    return jax.shard_map(
        functools.partial(local, plan), mesh=mesh, in_specs=in_specs, out_specs=out_specs, check_vma=False
    )
```

```python
import functools
import itertools

import jax
import jax.numpy as jnp
from jax import lax
from jax.experimental import pallas as pl
from jax.experimental.pallas import tpu as pltpu
from jax.sharding import PartitionSpec as P

NODES = 7
DOF = 3
ITERS = 3
AXES = ("gx", "gy", "gz")
STAGES = ((2,), (0, 1))
PAD = 8
CHUNK = 24
TILE = 256
F32 = jnp.float32
BF16 = jnp.bfloat16


def piece_length(placed):
    return DOF * NODES ** sum(1 for c in placed if c == 1)


PLACES = [p for p in itertools.product(range(3), repeat=3) if p != (1, 1, 1)]
CANON_OFFSET = {}
_at = 0
for _p in PLACES:
    CANON_OFFSET[_p] = _at
    _at += piece_length(_p)
IFACE = _at
SLOT_OFFSET = {}
SLOT_ROWS = {}
_at = 0
for _p in PLACES:
    SLOT_OFFSET[_p] = _at
    SLOT_ROWS[_p] = -(-piece_length(_p) // PAD) * PAD
    _at += SLOT_ROWS[_p]
COARSE_AT = _at
ROWS = -(-(COARSE_AT + 16) // TILE) * TILE


class Message:
    def __init__(self, moves, sizes):
        self.moves = moves
        self.sizes = sizes
        self.faces = "C" not in moves
        self.slots = []
        if self.faces:
            for place in PLACES:
                if all(m is None or c == (0 if m == "A" else 2) for m, c in zip(moves, place)):
                    self.slots.append(place)
        self.rows = sum(SLOT_ROWS[s] for s in self.slots)
        self.basis = []

    def xor(self):
        code = 0
        for move, size in zip(self.moves, self.sizes):
            code = code * size + {None: 0, "A": 1, "B": 3, "C": 2}[move]
        return code

    def pairs(self):
        out = []
        for place in itertools.product(*(range(s) for s in self.sizes)):
            to = []
            for at, move, size in zip(place, self.moves, self.sizes):
                if move == "A":
                    at = at ^ 1
                elif move == "B":
                    at = (at - 1) % size if at % 2 == 0 else (at + 1) % size
                elif move == "C":
                    at = at ^ 2
                to.append(at)
            flat = [0, 0]
            for a, b, size in zip(place, to, self.sizes):
                flat = [flat[0] * size + a, flat[1] * size + b]
            out.append(tuple(flat))
        return out


def ports(size):
    return ("A",) if size == 2 else ("A", "B")


def stage_messages(dims, sizes, coarse):
    choices = []
    for d in range(3):
        if d not in dims:
            choices.append((None,))
        else:
            extra = ("C",) if coarse and sizes[d] == 4 else ()
            choices.append((None,) + ports(sizes[d]) + extra)
    return [Message(m, sizes) for m in itertools.product(*choices) if any(c is not None for c in m)]


class Plan:
    def __init__(self, sizes):
        self.sizes = sizes
        self.subs = sizes[0] * sizes[1] * sizes[2]
        self.ride = all(s in (2, 4) for s in sizes)
        self.plain = [stage_messages(d, sizes, False) for d in STAGES]
        self.coarse = [stage_messages(d, sizes, True) for d in STAGES]
        self.wide = self.subs * 8
        first, second = self.coarse
        for message in first:
            message.basis = [((), slot) for slot in message.slots]
        for message in second:
            message.basis = [((), slot) for slot in message.slots]
            for other in first:
                message.basis += [((other,), slot) for slot in message.slots if slot in other.slots]

    def messages(self, coarse):
        return self.coarse if coarse and self.ride else self.plain


def position():
    return [lax.axis_index(a) for a in AXES]


def has_b(index, size):
    if size == 2:
        return None
    return jnp.logical_and(index > 0, index < size - 1)


def pick(slot, index, of):
    def choose(d, place):
        if d == 3:
            return of(tuple(place))
        if slot[d] == 1:
            return choose(d + 1, place + [1])
        even, odd = (2, 0) if slot[d] == 0 else (0, 2)
        return jnp.where(index[d] % 2 == 0, choose(d + 1, place + [even]), choose(d + 1, place + [odd]))

    return choose(0, [])


def add_received(plan, index, messages, received, acc):
    for message, ref in zip(messages, received):
        if not message.faces:
            continue
        ok = None
        for d, move in enumerate(message.moves):
            if move == "B":
                here = has_b(index[d], plan.sizes[d])
                ok = here if ok is None else jnp.logical_and(ok, here)
        at = 0
        for slot in message.slots:
            rows, to = SLOT_ROWS[slot], SLOT_OFFSET[slot]
            value = ref[at : at + rows, :]
            if ok is not None:
                value = jnp.where(ok, value, 0.0)
            acc[to : to + rows, :] += value
            at += rows


def write_payloads(messages, outs, acc, blocks, pack=None):
    for message, out in zip(messages, outs):
        at = 0
        for slot in message.slots:
            rows, frm = SLOT_ROWS[slot], SLOT_OFFSET[slot]
            out[at : at + rows, :] = acc[frm : frm + rows, :]
            at += rows
        for block in blocks:
            out[at : at + 8, :] = block
            at += 8
        if pack is not None and message.faces:
            out[at : at + CHUNK, :] = pack(message)


def payload_shapes(messages, blocks, packed=False):
    return [
        jax.ShapeDtypeStruct((m.rows + 8 * blocks + (CHUNK if packed and m.faces else 0), 128), F32)
        for m in messages
    ]


def packer(own, stage, unpacked):
    def pack(message):
        at = 0
        for source, slot in message.basis:
            rows = SLOT_ROWS[slot]
            if source:
                ref = unpacked[source[0]]
                frm = sum(SLOT_ROWS[s] for s in source[0].slots[: source[0].slots.index(slot)])
            else:
                ref, frm = own, SLOT_OFFSET[slot]
            stage[at : at + rows, :] = ref[frm : frm + rows, :]
            at += rows
        count = -(-at // CHUNK)
        if at < count * CHUNK:
            stage[at : count * CHUNK, :] = jnp.zeros((count * CHUNK - at, 128), F32)
        total = stage[0:CHUNK, :]
        for k in range(1, count):
            total += pltpu.roll(stage[k * CHUNK : (k + 1) * CHUNK, :], 8 * k, 1)
        return total

    return pack


def unpack(message, block, out):
    count = -(-sum(SLOT_ROWS[slot] for _, slot in message.basis) // CHUNK)
    lane = lax.broadcasted_iota(jnp.int32, (CHUNK, 128), 1)
    for k in range(count):
        turned = pltpu.roll(block, 128 - 8 * k, 1) if k else block
        out[k * CHUNK : (k + 1) * CHUNK, :] = jnp.where(lane < 8, turned, 0.0)


def transfer(messages, payloads):
    return [lax.ppermute(p, AXES, m.pairs()) for m, p in zip(messages, payloads)]


def vm():
    return pl.BlockSpec(memory_space=pltpu.VMEM)


def call(kernel, outs, operands, specs=None, scratch=(), limit=20, flops=0):
    nbytes = sum(o.size * o.dtype.itemsize for o in list(outs) + list(operands))
    return pl.pallas_call(
        kernel,
        out_shape=tuple(outs),
        in_specs=specs or [vm()] * len(operands),
        out_specs=tuple(vm() for _ in outs),
        scratch_shapes=list(scratch),
        compiler_params=pltpu.CompilerParams(vmem_limit_bytes=limit << 20),
        cost_estimate=pl.CostEstimate(flops=flops, bytes_accessed=nbytes, transcendentals=0),
    )(*operands)


def gather_rows(index, canon, load, acc):
    for slot in PLACES:
        rows, at = SLOT_ROWS[slot], SLOT_OFFSET[slot]
        acc[at + rows - 8 : at + rows, :] = jnp.zeros((8, acc.shape[1]), F32)
    acc[COARSE_AT:, :] = jnp.zeros((ROWS - COARSE_AT, acc.shape[1]), F32)
    for slot in PLACES:
        length, at = piece_length(slot), SLOT_OFFSET[slot]
        off = pick(slot, index, lambda place: jnp.int32(CANON_OFFSET[place]))
        step = 7 if length % 7 == 0 else 3

        def body(i, _, off=off, at=at, step=step):
            for j in range(step):
                row = i * step + j
                acc[pl.ds(at + row, 1), :] = load[canon[off + row], :, :]
            return 0

        lax.fori_loop(0, length // step, body, 0)


def input_kernel(plan, canon, load, acc, *outs):
    gather_rows(position(), canon, load, acc)
    write_payloads(plan.plain[0], outs, acc, [])


def scatter_rows(index, canon, pairs):
    for slot in PLACES:
        length, at = piece_length(slot), SLOT_OFFSET[slot]
        off = pick(slot, index, lambda place: jnp.int32(CANON_OFFSET[place]))
        step = 7 if length % 7 == 0 else 3

        def body(i, _, off=off, at=at, step=step):
            for j in range(step):
                row = i * step + j
                to = canon[off + row]
                for acc, out in pairs:
                    out[to, :, :] = acc[pl.ds(at + row, 1), :]
            return 0

        lax.fori_loop(0, length // step, body, 0)


def split(value, parts):
    out = []
    for _ in range(parts):
        piece = value.astype(BF16)
        out.append(piece)
        value = value - piece.astype(F32)
    return out


def dot(a, b):
    return jnp.dot(a, b, preferred_element_type=F32)


def dot_last(a, b):
    return lax.dot_general(a, b, (((1,), (1,)), ((), ())), preferred_element_type=F32)


def tile(t):
    return pl.ds(pl.multiple_of(t * TILE, TILE), TILE)


def each_tile(body):
    def step(t, _):
        body(tile(t))
        return 0

    lax.fori_loop(0, ROWS // TILE, step, 0)


def select_kernel(plan, canon, basis, cinv, one, one_w, turned, *rest):
    src, wgt = rest[-2:]
    index = position()
    src[...] = jnp.full(src.shape, -1, jnp.int32)
    wgt[...] = jnp.zeros(wgt.shape, F32)
    for slot in PLACES:
        at, length = SLOT_OFFSET[slot], piece_length(slot)
        src[at : at + length, :] = pick(
            slot, index, lambda place, length=length: canon[CANON_OFFSET[place] : CANON_OFFSET[place] + length, :]
        )
        weight = jnp.float32(1.0)
        for d in range(3):
            if slot[d] == 0:
                weight = weight * 0.5
            elif slot[d] == 2 and plan.sizes[d] > 2:
                weight = weight * jnp.where(has_b(index[d], plan.sizes[d]), 0.5, 1.0)
        wgt[at : at + length, :] = jnp.full((length, 1), 1.0, F32) * weight
    if plan.ride:
        nc = cinv.shape[1]
        row = lax.broadcasted_iota(jnp.int32, (nc, plan.wide), 0)
        col = lax.broadcasted_iota(jnp.int32, (nc, plan.wide), 1)
        spread = jnp.where(jnp.logical_and((col >> 3) * 6 + (col & 7) == row, (col & 7) < 6), 1.0, 0.0).astype(BF16)
        rest[0][...] = sum(dot(part, spread) for part in split(cinv[...], 3))[:8]

    def build(rows):
        hit = src[rows, :] == lax.broadcasted_iota(jnp.int32, (TILE, IFACE), 1)
        one[rows, :] = jnp.where(hit, 1.0, 0.0).astype(BF16)
        weighted = jnp.where(hit, wgt[rows, :], 0.0).astype(BF16)
        one_w[rows, :] = weighted
        turned[rows, :] = dot_last(weighted, basis[...])

    each_tile(build)


def left_kernel(one, matrix, mid):
    def body(rows):
        mid[rows, :] = dot(one[rows, :], matrix[...]).astype(BF16)

    each_tile(body)


def right_kernel(one, mid, basis, out):
    def body(rows):
        out[rows, :] = dot_last(mid[rows, :], one[...]).astype(BF16)

    each_tile(body)
    if basis is not None:
        out[COARSE_AT : COARSE_AT + 16, :] = dot_last(basis[:16, :], one[...]).astype(BF16)


def middle_kernel(plan, coarse, opening, *refs):
    first, second = plan.messages(coarse)
    ride = coarse and plan.ride
    setup = ride and opening
    refs = list(refs)
    base = refs.pop(0)
    received = [refs.pop(0) for _ in first]
    own_blocks, pack = [], None
    if setup:
        spread, turned = refs.pop(0), refs.pop(0)
        own_blocks = [spread[:, 128 * i : 128 * (i + 1)] for i in range(plan.wide // 128)]
        stage = refs.pop(-1)
        kept = {m: refs.pop(-1) for m in reversed(first) if m.faces}
        for message, ref in zip(first, received):
            if message.faces:
                at = message.rows + 8 * (1 + len(own_blocks))
                unpack(message, ref[at : at + CHUNK, :], kept[message])
        pack = packer(turned, stage, kept)
    acc = refs.pop(-1)
    outs = refs
    acc[...] = base[...]
    add_received(plan, position(), first, received, acc)
    blocks = []
    if ride:
        per = 1 + len(own_blocks)
        blocks = [base[COARSE_AT : COARSE_AT + 8, :]] + own_blocks
        for message, ref in zip(first, received):
            blocks += [ref[message.rows + 8 * i : message.rows + 8 * (i + 1), :] for i in range(per)]
    write_payloads(second, outs, acc, blocks, pack)


def multiply(matrix, vector, out):
    for t in range(ROWS // TILE):
        out[t * TILE : (t + 1) * TILE, :] = dot(matrix[t * TILE : (t + 1) * TILE, :], vector)


def inverse_kernel(plan, opening, *refs):
    first, second = plan.plain
    refs = list(refs)
    base = refs.pop(0)
    got = [refs.pop(0) for _ in range(len(first) + len(second))]
    matrix = refs.pop(0)
    before = None if opening else refs.pop(0)
    own_blocks, pack = [], None
    if opening and plan.ride:
        spread, turned = refs.pop(0), refs.pop(0)
        own_blocks = [spread[:, 128 * i : 128 * (i + 1)] for i in range(plan.wide // 128)]
        pack = packer(turned, refs.pop(-1), {})
    acc = refs.pop(-1)
    residual, out, *outs = refs
    index = position()
    acc[...] = base[...]
    add_received(plan, index, first, got[: len(first)], acc)
    add_received(plan, index, second, got[len(first) :], acc)
    value = acc[...] if opening else before[...] - acc[...]
    residual[...] = value
    multiply(matrix, value.astype(BF16), out)
    if plan.ride:
        write_payloads(plan.coarse[0], outs, out, [out[COARSE_AT : COARSE_AT + 8, :]] + own_blocks, pack)


def lift_kernel(plan, base, turned, correction, out, *outs):
    lifted = turned[...].astype(BF16)
    out[...] = base[...] + sum(dot(lifted, part) for part in split(correction[...], 3))
    write_payloads(plan.plain[0], outs, out, [])


def collect(plan, index, own, got, per, which, stack, at_column):
    first, second = plan.coarse
    me = (index[0] * plan.sizes[1] + index[1]) * plan.sizes[2] + index[2]
    near = [0] + [m.xor() for m in first]

    def put(code, value):
        stack[pl.ds(pl.multiple_of((me ^ code) * 8, 8), 8), at_column : at_column + 128] = value

    put(0, own)
    for m, ref in zip(first, got):
        at = m.rows + 8 * which
        put(m.xor(), ref[at : at + 8, :])
    for m, ref in zip(second, got[len(first) :]):
        for i, code in enumerate(near):
            at = m.rows + 8 * (per * i + which)
            put(code ^ m.xor(), ref[at : at + 8, :])


def lifting(plan, index, got, per, turned, spread, stack, many, unpacked, out):
    first, second = plan.coarse
    halves = plan.wide // 128
    me = (index[0] * plan.sizes[1] + index[1]) * plan.sizes[2] + index[2]

    def place(code, value, to, ok):
        there = me ^ code
        value = pltpu.roll(value, (there & 15) * 8, 1)
        rows = value.shape[0]
        for half in range(halves):
            here = (there >> 4) == half
            if ok is not None:
                here = jnp.logical_and(here, ok)
            many[to : to + rows, 128 * half : 128 * (half + 1)] += jnp.where(here, value, 0.0)

    def exists(message):
        ok = None
        for d, move in enumerate(message.moves):
            if move == "B":
                here = has_b(index[d], plan.sizes[d])
                ok = here if ok is None else jnp.logical_and(ok, here)
        return ok

    many[...] = jnp.zeros(many.shape, F32)
    for t in range(ROWS // TILE):
        place(0, turned[t * TILE : (t + 1) * TILE, :], t * TILE, None)
    for m, ref in zip(first + second, got):
        if not m.faces:
            continue
        blocks = per * (1 if m in first else 1 + len(first))
        at = m.rows + 8 * blocks
        unpack(m, ref[at : at + CHUNK, :], unpacked)
        at, ok = 0, exists(m)
        for source, slot in m.basis:
            code, fine = m.xor(), ok
            if source:
                code ^= source[0].xor()
                also = exists(source[0])
                if also is not None:
                    fine = also if fine is None else jnp.logical_and(fine, also)
            place(code, unpacked[at : at + SLOT_ROWS[slot], :], SLOT_OFFSET[slot], fine)
            at += SLOT_ROWS[slot]
    for half in range(halves):
        own = spread[:, 128 * half : 128 * (half + 1)]
        collect(plan, index, own, got, per, 1 + half, stack, 128 * half)
    parts = jnp.concatenate(split(stack[...], 3), axis=0)

    def body(rows):
        basis = many[rows, :].astype(BF16)
        whole = dot(jnp.concatenate([basis] * 3, axis=1), parts)
        high, low = split(whole, 2)
        out[rows, :] = jnp.concatenate([high, high, low], axis=1)

    each_tile(body)


def schur_kernel(plan, opening, *refs):
    first, second = plan.messages(True)
    refs = list(refs)
    base = refs.pop(0)
    got = [refs.pop(0) for _ in range(len(first) + len(second))]
    matrix = refs.pop(0)
    setup = plan.ride and opening
    sol_in = None if opening else refs.pop(0)
    if setup:
        spread, turned = refs.pop(0), refs.pop(0)
        unpacked, many, wide_stack = refs.pop(-1), refs.pop(-1), refs.pop(-1)
    elif plan.ride:
        lift = refs.pop(0)
    acc, stack = refs.pop(-2), refs.pop(-1)
    sol, out = refs.pop(0), refs.pop(0)
    outs = refs[: len(plan.plain[0])]
    index = position()
    per = 1
    if setup:
        lift = refs[-1]
        per = 1 + plan.wide // 128
        lifting(plan, index, got, per, turned, spread, wide_stack, many, unpacked, lift)
    acc[...] = base[...]
    add_received(plan, index, first, got[: len(first)], acc)
    add_received(plan, index, second, got[len(first) :], acc)
    if plan.ride:
        collect(plan, index, base[COARSE_AT : COARSE_AT + 8, :], got, per, 0, stack, 0)
        high, low = split(stack[...], 2)
        multiply(lift, jnp.concatenate([high, low, high], axis=0), out)
        update = acc[...] + out[...]
    else:
        update = acc[...]
    sol[...] = update if opening else sol_in[...] + update
    multiply(matrix, update.astype(BF16), out)
    write_payloads(plan.plain[0], outs, out, [])


def output_kernel(plan, canon, base, *refs):
    first, second = plan.plain
    count = len(first) + len(second)
    got = refs[:count]
    residual, sol, sol_out, residual_out, acc = refs[count:]
    index = position()
    acc[...] = base[...]
    add_received(plan, index, first, got[: len(first)], acc)
    add_received(plan, index, second, got[len(first) :], acc)
    acc[...] = residual[...] - acc[...]
    scatter_rows(index, canon, [(sol, sol_out), (acc, residual_out)])


def shape(rows, cols, dtype=F32):
    return jax.ShapeDtypeStruct((rows, cols), dtype)


def local(plan, load_cases, schur_matrix, local_inverse, coarse_basis, coarse_inverse, canon_rows):
    smem = pl.BlockSpec(memory_space=pltpu.SMEM)
    loads = load_cases.shape[-1]
    canon = canon_rows.reshape(IFACE)
    load = load_cases.reshape(IFACE, 1, loads)
    basis = jnp.pad(coarse_basis[0, 0, 0], ((0, 122), (0, 0)))
    cinv = jnp.pad(coarse_inverse, ((0, 10), (0, 0)))
    plain, coarse = plan.plain, plan.messages(True)
    acc = pltpu.VMEM((ROWS, 128), F32)
    pieces = pltpu.VMEM((16 * CHUNK, 128), F32)
    setup_blocks = plan.wide // 128 if plan.ride else 0

    def middle(is_coarse, opening, base, got, extra):
        first, second = plan.messages(is_coarse)
        setup = is_coarse and opening and plan.ride
        blocks = 0
        if is_coarse and plan.ride:
            blocks = (len(first) + 1) * (1 + (setup_blocks if opening else 0))
        return call(
            functools.partial(middle_kernel, plan, is_coarse, opening),
            payload_shapes(second, blocks, setup),
            [base] + got + (extra if setup else []),
            scratch=[acc] + ([pieces] * (1 + sum(m.faces for m in first)) if setup else []),
        )

    def assemble(is_coarse, opening, base, payloads, extra):
        first, second = plan.messages(is_coarse)
        got = transfer(first, payloads)
        return got + transfer(second, middle(is_coarse, opening, base, got, extra))

    base, *payloads = call(
        functools.partial(input_kernel, plan),
        [shape(ROWS, 128)] + payload_shapes(plain[0], 0),
        [canon, load],
        specs=[smem, vm()],
    )
    one, one_w, turned, *spread = call(
        functools.partial(select_kernel, plan),
        [shape(ROWS, IFACE, BF16), shape(ROWS, IFACE, BF16), shape(ROWS, 128)]
        + ([shape(8, plan.wide)] if plan.ride else []),
        [canon_rows.reshape(IFACE, 1), basis, cinv],
        scratch=[pltpu.VMEM((ROWS, 1), jnp.int32), pltpu.VMEM((ROWS, 1), F32)],
        flops=2 * ROWS * IFACE * 1158,
    )
    flops = 2 * ROWS * IFACE * IFACE
    middle_shape, square = shape(ROWS, IFACE, BF16), shape(ROWS, ROWS, BF16)

    def right_plain(a, b, out):
        right_kernel(a, b, None, out)

    (half,) = call(left_kernel, [middle_shape], [one_w, local_inverse[0, 0, 0]], flops=flops)
    (inverse,) = call(right_kernel, [square], [one_w, half, basis], flops=flops)
    (half,) = call(left_kernel, [middle_shape], [one, schur_matrix[0, 0, 0]], flops=flops)
    (schur,) = call(right_plain, [square], [one, half], flops=flops)
    got = assemble(False, False, base, payloads, [])
    sol = None
    extra = spread + [turned]
    flops = 2 * ROWS * ROWS * 128
    for iteration in range(ITERS):
        opening = iteration == 0
        setup = opening and plan.ride
        residual, base, *payloads = call(
            functools.partial(inverse_kernel, plan, opening),
            [shape(ROWS, 128), shape(ROWS, 128)]
            + (payload_shapes(coarse[0], 1 + (setup_blocks if opening else 0), setup) if plan.ride else []),
            [base] + got + [inverse] + ([] if opening else [residual]) + (extra if setup else []),
            scratch=[acc] + ([pieces] if setup else []),
            flops=flops,
        )
        if not plan.ride:
            rows = lax.all_gather(base[COARSE_AT : COARSE_AT + 6], AXES, axis=0, tiled=True)
            correction = jnp.dot(cinv, rows, precision=lax.Precision.HIGHEST, preferred_element_type=F32)
            base, *payloads = call(
                functools.partial(lift_kernel, plan),
                [shape(ROWS, 128)] + payload_shapes(plain[0], 0),
                [base, turned, jnp.pad(correction, ((0, 112), (0, 0)))],
            )
        got = assemble(True, opening, base, payloads, extra)
        given = [] if opening else [sol]
        if plan.ride:
            given += extra if opening else [lift]
        stack = [pltpu.VMEM((plan.wide, plan.wide), F32), pltpu.VMEM((ROWS, plan.wide), F32), pieces]
        results = call(
            functools.partial(schur_kernel, plan, opening),
            [shape(ROWS, 128), shape(ROWS, 128)]
            + payload_shapes(plain[0], 0)
            + ([shape(ROWS, 3 * plan.wide, BF16)] if setup else []),
            [base] + got + [schur] + given,
            scratch=[acc, pltpu.VMEM((plan.wide, 128), F32)] + (stack if setup else []),
            flops=flops,
        )
        sol, base, *payloads = results[: 2 + len(plain[0])]
        if setup:
            lift = results[-1]
        got = assemble(False, opening, base, payloads, [])
    out = jax.ShapeDtypeStruct((IFACE, 1, loads), F32)
    sol_out, residual_out = call(
        functools.partial(output_kernel, plan),
        [out, out],
        [canon, base] + got + [residual, sol],
        specs=[smem] + [vm()] * (3 + len(got)),
        scratch=[acc],
    )
    return tuple(o.reshape(1, 1, 1, IFACE, loads) for o in (sol_out, residual_out))


def solution(mesh):
    plan = Plan(tuple(mesh.shape[a] for a in AXES))
    in_specs = (
        P("gx", "gy", "gz", None, None),
        P("gx", "gy", "gz", None, None),
        P("gx", "gy", "gz", None, None),
        P("gx", "gy", "gz", None, None),
        P(("gx", "gy", "gz"), None),
        P("gx", "gy", "gz", None),
    )
    out_specs = (P("gx", "gy", "gz", None, None), P("gx", "gy", "gz", None, None))
    return jax.shard_map(
        functools.partial(local, plan), mesh=mesh, in_specs=in_specs, out_specs=out_specs, check_vma=False
    )
```

```python
import functools
import itertools

import jax
import jax.numpy as jnp
from jax import lax
from jax.experimental import pallas as pl
from jax.experimental.pallas import tpu as pltpu
from jax.sharding import PartitionSpec as P

NODES = 7
DOF = 3
ITERS = 3
AXES = ("gx", "gy", "gz")
STAGES = ((1,), (0, 2))
SPARE = (2, 1)
PAD = 8
CHUNK = 24
TILE = 256
F32 = jnp.float32
BF16 = jnp.bfloat16


def piece_length(placed):
    return DOF * NODES ** sum(1 for c in placed if c == 1)


PLACES = [p for p in itertools.product(range(3), repeat=3) if p != (1, 1, 1)]
CANON_OFFSET = {}
_at = 0
for _p in PLACES:
    CANON_OFFSET[_p] = _at
    _at += piece_length(_p)
IFACE = _at
LENGTH = {p: piece_length(p) for p in PLACES}
EARLY = [p for p in PLACES if p[1] != 1]
LATE = [p for p in PLACES if p[1] == 1]
SLOT_OFFSET = {}


def _lay(slots, at):
    for slot in slots:
        SLOT_OFFSET[slot] = at
        at += -(-LENGTH[slot] // PAD) * PAD
    return at


COARSE_AT = _lay(EARLY, 0)
SPLIT = -(-(COARSE_AT + 16) // 16) * 16
ROWS = -(-_lay(LATE, SPLIT) // TILE) * TILE
PARTS = {"all": (0, ROWS), "early": (0, SPLIT), "late": (SPLIT, ROWS)}


class Message:
    def __init__(self, moves, sizes, wrap, ride, spare):
        self.moves = moves
        self.sizes = sizes
        self.wrap = wrap
        self.ride = ride
        self.spare = spare
        self.faces = not any(m in ("C", "W") for m in moves)
        self.slots = []
        if self.faces:
            for place in EARLY + LATE:
                if all(m is None or c == (0 if m == "A" else 2) for m, c in zip(moves, place)):
                    self.slots.append(place)
        self.rows = -(-sum(LENGTH[s] for s in self.slots) // PAD) * PAD
        self.basis = []

    def xor(self):
        code = 0
        for move, size in zip(self.moves, self.sizes):
            code = code * size + {None: 0, "A": 1, "B": 3, "C": 2, "W": 3}[move]
        return code

    def pairs(self):
        out = []
        for place in itertools.product(*(range(s) for s in self.sizes)):
            to, whole = [], True
            for at, move, size in zip(place, self.moves, self.sizes):
                if move == "A":
                    at = at ^ 1
                elif move == "B":
                    whole = whole and (self.wrap or 0 < at < size - 1)
                    at = (at - 1) % size if at % 2 == 0 else (at + 1) % size
                elif move == "C":
                    at = at ^ 2
                elif move == "W":
                    at = at ^ 3
                to.append(at)
            if not whole:
                to = [at ^ 1 if d == self.spare else at for d, at in enumerate(place)]
            flat = [0, 0]
            for a, b, size in zip(place, to, self.sizes):
                flat = [flat[0] * size + a, flat[1] * size + b]
            out.append(tuple(flat))
        return out


def stage_messages(stage, sizes, coarse):
    choices = []
    for d in range(3):
        if d not in STAGES[stage]:
            choices.append((None,))
        else:
            extra = ("C", "W") if coarse and stage == 0 and sizes[d] == 4 else ()
            choices.append((None, "A") + (("B",) if sizes[d] > 2 else ()) + extra)
    out = []
    for moves in itertools.product(*choices):
        if all(m is None for m in moves):
            continue
        ride = coarse and (moves[1] != "B" if stage == 0 else moves[2] != "A")
        out.append(Message(moves, sizes, ride and stage == 1, ride, SPARE[stage]))
    return out


class Plan:
    def __init__(self, sizes):
        self.sizes = sizes
        self.subs = sizes[0] * sizes[1] * sizes[2]
        self.ride = all(s in (2, 4) for s in sizes)
        self.wide = self.subs * 8
        self.plain = [stage_messages(i, sizes, False) for i in range(2)]
        self.coarse = self.plain
        self.setup = 0
        if self.ride:
            self.local = Message((None, None, "A"), sizes, False, True, 0)
            self.coarse = [stage_messages(i, sizes, True) for i in range(2)]
            self.setup = self.wide // 128
            first, second = self.coarse
            for message in first:
                message.basis = [(None, slot) for slot in message.slots]
            for message in second:
                message.basis = [(None, slot) for slot in message.slots]
                for other in first:
                    message.basis += [(other, slot) for slot in message.slots if slot in other.slots]

    def per(self, kind):
        return {"plain": 0, "update": 1, "initial": self.setup}[kind] if self.ride else 0

    def messages(self, kind):
        return self.plain if self.per(kind) == 0 else self.coarse

    def codes(self, stage):
        known = [0, self.local.xor()]
        if stage == 1:
            known = [k ^ m for m in [0] + [m.xor() for m in self.coarse[0] if m.ride] for k in known]
        return known

    def payload_shapes(self, kind, stage):
        per = self.per(kind)
        out = []
        for m in self.messages(kind)[stage]:
            rows = m.rows
            if m.ride:
                rows += 8 * per * len(self.codes(stage))
            if kind == "initial" and self.ride and m.faces:
                rows += CHUNK
            out.append(shape(rows, 128))
        return out


def position():
    return [lax.axis_index(a) for a in AXES]


def has_b(index, size):
    return jnp.logical_and(index > 0, index < size - 1)


def exists(plan, index, message):
    ok = None
    for d, move in enumerate(message.moves):
        if move == "B":
            here = has_b(index[d], plan.sizes[d])
            ok = here if ok is None else jnp.logical_and(ok, here)
    return ok


def both(a, b):
    return b if a is None else a if b is None else jnp.logical_and(a, b)


def pick(slot, index, of):
    def choose(d, place):
        if d == 3:
            return of(tuple(place))
        if slot[d] == 1:
            return choose(d + 1, place + [1])
        even, odd = (2, 0) if slot[d] == 0 else (0, 2)
        return jnp.where(index[d] % 2 == 0, choose(d + 1, place + [even]), choose(d + 1, place + [odd]))

    return choose(0, [])


def add_received(plan, index, messages, received, acc):
    for message, ref in zip(messages, received):
        if not message.faces:
            continue
        ok = exists(plan, index, message)
        at = 0
        for slot in message.slots:
            rows, to = LENGTH[slot], SLOT_OFFSET[slot]
            value = ref[at : at + rows, :]
            if ok is not None:
                value = jnp.where(ok, value, 0.0)
            acc[to : to + rows, :] += value
            at += rows


def write_payloads(messages, outs, acc, blocks, pack=None):
    for message, out in zip(messages, outs):
        at = 0
        for slot in message.slots:
            rows, frm = LENGTH[slot], SLOT_OFFSET[slot]
            out[at : at + rows, :] = acc[frm : frm + rows, :]
            at += rows
        at = message.rows
        if message.ride:
            for block in blocks:
                out[at : at + 8, :] = block
                at += 8
        if pack is not None and message.faces:
            out[at : at + CHUNK, :] = pack(message)


def packer(own, stage, unpacked):
    def pack(message):
        at = 0
        for source, slot in message.basis:
            rows = LENGTH[slot]
            if source is not None:
                ref = unpacked[source]
                frm = sum(LENGTH[s] for s in source.slots[: source.slots.index(slot)])
            else:
                ref, frm = own, SLOT_OFFSET[slot]
            stage[at : at + rows, :] = ref[frm : frm + rows, :]
            at += rows
        count = -(-at // CHUNK)
        if at < count * CHUNK:
            stage[at : count * CHUNK, :] = jnp.zeros((count * CHUNK - at, 128), F32)
        total = stage[0:CHUNK, :]
        for k in range(1, count):
            total += pltpu.roll(stage[k * CHUNK : (k + 1) * CHUNK, :], 8 * k, 1)
        return total

    return pack


def unpack(message, block, out):
    count = -(-sum(LENGTH[slot] for _, slot in message.basis) // CHUNK)
    lane = lax.broadcasted_iota(jnp.int32, (CHUNK, 128), 1)
    for k in range(count):
        turned = pltpu.roll(block, 128 - 8 * k, 1) if k else block
        out[k * CHUNK : (k + 1) * CHUNK, :] = jnp.where(lane < 8, turned, 0.0)


def transfer(messages, payloads):
    return [lax.ppermute(p, AXES, m.pairs()) for m, p in zip(messages, payloads)]


def vm():
    return pl.BlockSpec(memory_space=pltpu.VMEM)


def shape(rows, cols, dtype=F32):
    return jax.ShapeDtypeStruct((rows, cols), dtype)


def call(kernel, outs, operands, specs=None, scratch=(), limit=20, flops=0):
    nbytes = sum(o.size * o.dtype.itemsize for o in list(outs) + list(operands))
    return pl.pallas_call(
        kernel,
        out_shape=tuple(outs),
        in_specs=specs or [vm()] * len(operands),
        out_specs=tuple(vm() for _ in outs),
        scratch_shapes=list(scratch),
        compiler_params=pltpu.CompilerParams(vmem_limit_bytes=limit << 20),
        cost_estimate=pl.CostEstimate(flops=flops, bytes_accessed=nbytes, transcendentals=0),
    )(*operands)


def gather_kernel(slots, start, canon, load, acc):
    index = position()
    acc[...] = jnp.zeros(acc.shape, F32)
    for slot in slots:
        length, at = LENGTH[slot], SLOT_OFFSET[slot] - start
        off = pick(slot, index, lambda place: jnp.int32(CANON_OFFSET[place]))
        step = 21 if length % 21 == 0 else 3

        def body(i, _, off=off, at=at, step=step):
            for j in range(step):
                row = i * step + j
                acc[pl.ds(at + row, 1), :] = load[canon[0, off + row], :, :]
            return 0

        lax.fori_loop(0, length // step, body, 0)


def scatter_rows(index, canon, acc, out):
    for slot in PLACES:
        length, at = LENGTH[slot], SLOT_OFFSET[slot]
        off = pick(slot, index, lambda place: jnp.int32(CANON_OFFSET[place]))
        step = 21 if length % 21 == 0 else 3

        def body(i, _, off=off, at=at, step=step):
            for j in range(step):
                row = i * step + j
                out[canon[0, off + row], :, :] = acc[pl.ds(at + row, 1), :]
            return 0

        lax.fori_loop(0, length // step, body, 0)


def scatter_kernel(canon, acc, out):
    scatter_rows(position(), canon, acc, out)


def split(value, parts):
    out = []
    for _ in range(parts):
        piece = value.astype(BF16)
        out.append(piece)
        value = value - piece.astype(F32)
    return out


def dot(a, b):
    return jnp.dot(a, b, preferred_element_type=F32)


def dot_last(a, b):
    return lax.dot_general(a, b, (((1,), (1,)), ((), ())), preferred_element_type=F32)


def tile(t):
    return pl.ds(pl.multiple_of(t * TILE, TILE), TILE)


def each_tile(body):
    def step(t, _):
        body(tile(t))
        return 0

    lax.fori_loop(0, ROWS // TILE, step, 0)


def select_kernel(plan, canon, basis, cinv, one, one_w, turned, *rest):
    src, wgt = rest[-2:]
    index = position()
    src[...] = jnp.full(src.shape, -1, jnp.int32)
    wgt[...] = jnp.zeros(wgt.shape, F32)
    for slot in PLACES:
        at, length = SLOT_OFFSET[slot], LENGTH[slot]
        src[at : at + length, :] = pick(
            slot, index, lambda place, length=length: canon[CANON_OFFSET[place] : CANON_OFFSET[place] + length, :]
        )
        weight = jnp.float32(1.0)
        for d in range(3):
            if slot[d] == 0:
                weight = weight * 0.5
            elif slot[d] == 2 and plan.sizes[d] > 2:
                weight = weight * jnp.where(has_b(index[d], plan.sizes[d]), 0.5, 1.0)
        wgt[at : at + length, :] = jnp.full((length, 1), 1.0, F32) * weight
    if plan.ride:
        spread_out = rest[0]
        nc = cinv.shape[1]
        row = lax.broadcasted_iota(jnp.int32, (nc, plan.wide), 0)
        col = lax.broadcasted_iota(jnp.int32, (nc, plan.wide), 1)
        spread = jnp.where(jnp.logical_and((col >> 3) * 6 + (col & 7) == row, (col & 7) < 6), 1.0, 0.0).astype(BF16)
        value = sum(dot(part, spread) for part in split(cinv[...], 3))
        spread_out[...] = jnp.zeros(spread_out.shape, F32)
        for i in range(plan.setup):
            spread_out[8 * i : 8 * i + 6, :] = value[:, 128 * i : 128 * (i + 1)]
    turned[...] = jnp.zeros(turned.shape, F32)

    def build(rows):
        hit = src[rows, :] == lax.broadcasted_iota(jnp.int32, (TILE, IFACE), 1)
        one[rows, :] = jnp.where(hit, 1.0, 0.0).astype(BF16)
        weighted = jnp.where(hit, wgt[rows, :], 0.0).astype(BF16)
        one_w[rows, :] = weighted
        turned[rows, :6] = dot_last(weighted, basis[...])

    each_tile(build)


def left_kernel(one, matrix, mid):
    def body(rows):
        mid[rows, :] = dot(one[rows, :], matrix[...]).astype(BF16)

    each_tile(body)


def right_kernel(one, mid, basis, out, few):
    def body(rows):
        out[rows, :] = dot_last(mid[rows, :], one[...]).astype(BF16)

    each_tile(body)
    if basis is not None:
        few[...] = jnp.zeros(few.shape, F32)
        few[:6, :] = dot_last(basis[...], one[...])
        out[COARSE_AT : COARSE_AT + 16, :] = few[...].astype(BF16)


def fill(acc, parts):
    at = 0
    for part in parts:
        acc[at : at + part.shape[0], :] = part[...]
        at += part.shape[0]


def known_blocks(plan, own, received, messages, per):
    blocks = own + [received[0][8 * i : 8 * (i + 1), :] for i in range(per)]
    for message, ref in zip(messages, received[1:]):
        if message.ride:
            blocks += [ref[message.rows + 8 * i : message.rows + 8 * (i + 1), :] for i in range(2 * per)]
    return blocks


def first_kernel(plan, kind, *refs):
    refs = list(refs)
    base, own, local = refs[:3]
    refs = refs[3:]
    per = plan.per(kind)
    pack = None
    if kind == "initial":
        turned = refs.pop(0)
        pack = packer(turned, refs.pop(-1), {})
        mine = [own[8 * i : 8 * (i + 1), :] for i in range(per)]
    else:
        mine = [own[...]]
    write_payloads(plan.coarse[0], refs, base, known_blocks(plan, mine, [local], [], per), pack)


def middle_kernel(plan, kind, count, *refs):
    first, second = plan.messages(kind)
    per = plan.per(kind)
    refs = list(refs)
    parts = [refs.pop(0) for _ in range(count)]
    received = [refs.pop(0) for _ in first]
    blocks, pack = [], None
    if per:
        own, local = refs.pop(0), refs.pop(0)
        mine = [own[8 * i : 8 * (i + 1), :] for i in range(per)]
        blocks = known_blocks(plan, mine, [local] + received, first, per)
    if per and kind == "initial":
        turned = refs.pop(0)
        stage = refs.pop(-1)
        kept = {m: refs.pop(-1) for m in reversed(first) if m.faces}
        for message, ref in zip(first, received):
            if message.faces:
                unpack(message, ref[ref.shape[0] - CHUNK :, :], kept[message])
        pack = packer(turned, stage, kept)
    acc = refs.pop(-1)
    fill(acc, parts)
    add_received(plan, position(), first, received, acc)
    write_payloads(second, refs, acc, blocks, pack)


def product_kernel(part, matrix, vector, out):
    start, stop = PARTS[part]
    size = (stop - start) // (4 if part == "all" else 2)
    for t in range(start, stop, size):
        out[t - start : t - start + size, :] = dot(matrix[t : t + size, :], vector[...])


def finish(plan, kind, parts, got, acc):
    first, second = plan.messages(kind)
    index = position()
    fill(acc, parts)
    add_received(plan, index, first, got[: len(first)], acc)
    add_received(plan, index, second, got[len(first) :], acc)


def residual_kernel(plan, opening, count, *refs):
    kind = "initial" if opening else "plain"
    refs = list(refs)
    parts = [refs.pop(0) for _ in range(count)]
    got = [refs.pop(0) for _ in range(sum(len(m) for m in plan.messages(kind)))]
    matrix = refs.pop(0)
    before = None if opening else refs.pop(0)
    residual, rounded, restricted, acc = refs
    finish(plan, kind, parts, got, acc)
    value = acc[...] if opening else before[...] - acc[...]
    residual[...] = value
    rounded[...] = value.astype(BF16)
    restricted[...] = dot(matrix[COARSE_AT : COARSE_AT + 16, :], rounded[...])[:8]


def lift_kernel(plan, base, turned, correction, out, *outs):
    lifted = turned[...].astype(BF16)
    out[...] = base[...] + sum(dot(lifted, part) for part in split(correction[...], 3))
    write_payloads(plan.plain[0], outs, out, [])


def collect(plan, own, got, per, which, stack, at_column):
    first, second = plan.coarse
    index = position()
    me = (index[0] * plan.sizes[1] + index[1]) * plan.sizes[2] + index[2]

    def put(code, value):
        stack[pl.ds(pl.multiple_of((me ^ code) * 8, 8), 8), at_column : at_column + 128] = value

    local, got = got[0], got[1:]
    put(0, own[8 * which : 8 * (which + 1), :])
    put(plan.local.xor(), local[8 * which : 8 * (which + 1), :])
    for stage, messages in enumerate((first, second)):
        for m, ref in zip(messages, got):
            if m.ride:
                for i, code in enumerate(plan.codes(stage)):
                    at = m.rows + 8 * (per * i + which)
                    put(code ^ m.xor(), ref[at : at + 8, :])
        got = got[len(messages) :]


def lifting_kernel(plan, *refs):
    first, second = plan.coarse
    turned, spread, local, *got, out, stack, many, unpacked = refs
    per = plan.setup
    index = position()
    me = (index[0] * plan.sizes[1] + index[1]) * plan.sizes[2] + index[2]

    def place(code, value, to, ok):
        there = me ^ code
        value = pltpu.roll(value, (there & 15) * 8, 1)
        rows = value.shape[0]
        for half in range(per):
            here = both((there >> 4) == half, ok)
            many[to : to + rows, 128 * half : 128 * (half + 1)] += jnp.where(here, value, 0.0)

    many[...] = jnp.zeros(many.shape, F32)
    for t in range(ROWS // TILE):
        place(0, turned[t * TILE : (t + 1) * TILE, :], t * TILE, None)
    for m, ref in zip(first + second, got):
        if not m.faces:
            continue
        unpack(m, ref[ref.shape[0] - CHUNK :, :], unpacked)
        at, ok = 0, exists(plan, index, m)
        for source, slot in m.basis:
            code, fine = m.xor(), ok
            if source is not None:
                code ^= source.xor()
                fine = both(exists(plan, index, source), ok)
            place(code, unpacked[at : at + LENGTH[slot], :], SLOT_OFFSET[slot], fine)
            at += LENGTH[slot]
    for half in range(per):
        collect(plan, spread, [local] + got, per, half, stack, 128 * half)
    parts = jnp.concatenate(split(stack[...], 3), axis=0)

    def body(rows):
        basis = many[rows, :].astype(BF16)
        whole = dot(jnp.concatenate([basis] * 3, axis=1), parts)
        high, low = split(whole, 2)
        out[rows, :] = jnp.concatenate([high, high, low], axis=1)

    each_tile(body)


def update_kernel(plan, *refs):
    refs = list(refs)
    base = refs.pop(0)
    got = [refs.pop(0) for _ in range(sum(len(m) for m in plan.messages("update")))]
    matrix = refs.pop(0)
    if plan.ride:
        lift, own, local = refs.pop(0), refs.pop(0), refs.pop(0)
        stack = refs.pop(-1)
    acc = refs.pop(-1)
    update, rounded, early, *outs = refs
    finish(plan, "update", [base], got, acc)
    if plan.ride:
        collect(plan, own, [local] + got, 1, 0, stack, 0)
        high, low = split(stack[...], 2)
        right = jnp.concatenate([high, low, high], axis=0)
        for t in range(0, ROWS, 320):
            value = acc[t : t + 320, :] + dot(lift[t : t + 320, :], right)
            update[t : t + 320, :] = value
            rounded[t : t + 320, :] = value.astype(BF16)
    else:
        update[...] = acc[...]
        rounded[...] = acc[...].astype(BF16)
    product_kernel("early", matrix, rounded, early)
    write_payloads(plan.plain[0], outs, early, [])


def later_kernel(opening, matrix, rounded, update, *refs):
    late, total = refs[-2:]
    product_kernel("late", matrix, rounded, late)
    total[...] = update[...] if opening else refs[0][...] + update[...]


def output_kernel(plan, canon, early, late, *refs):
    *got, residual, out, acc = refs
    finish(plan, "plain", [early, late], got, acc)
    acc[...] = residual[...] - acc[...]
    scatter_rows(position(), canon, acc, out)


def local(plan, load_cases, schur_matrix, local_inverse, coarse_basis, coarse_inverse, canon_rows):
    smem = pl.BlockSpec(memory_space=pltpu.SMEM)
    loads = load_cases.shape[-1]
    canon = canon_rows.reshape(1, IFACE)
    load = load_cases.reshape(IFACE, 1, loads)
    basis = coarse_basis[0, 0, 0]
    acc = pltpu.VMEM((ROWS, 128), F32)
    pieces = pltpu.VMEM((16 * CHUNK, 128), F32)
    early_rows, late_rows = SPLIT, ROWS - SPLIT

    def first(kind, base, own, swapped, more):
        return call(
            functools.partial(first_kernel, plan, kind),
            plan.payload_shapes(kind, 0),
            [base, own, swapped] + more,
            scratch=[pieces] if kind == "initial" else [],
        )

    def assemble(kind, parts, payloads, blocks, more, late=None):
        messages = plan.messages(kind)
        got = transfer(messages[0], payloads)
        setup = kind == "initial" and plan.ride
        payloads = call(
            functools.partial(middle_kernel, plan, kind, len(parts)),
            plan.payload_shapes(kind, 1),
            parts + got + blocks + (more if setup else []),
            scratch=[acc] + ([pieces] * (1 + sum(m.faces for m in messages[0])) if setup else []),
        )
        return got + transfer(messages[1], payloads)

    one, one_w, turned, *spread = call(
        functools.partial(select_kernel, plan),
        [shape(ROWS, IFACE, BF16), shape(ROWS, IFACE, BF16), shape(ROWS, 128)]
        + ([shape(8 * plan.setup, 128)] if plan.ride else []),
        [canon_rows.reshape(IFACE, 1), basis, coarse_inverse],
        scratch=[pltpu.VMEM((ROWS, 1), jnp.int32), pltpu.VMEM((ROWS, 1), F32)],
        flops=ROWS * IFACE * 1158,
    )
    (early,) = call(
        functools.partial(gather_kernel, EARLY, 0), [shape(early_rows, 128)], [canon, load], specs=[smem, vm()]
    )
    (late,) = call(
        functools.partial(gather_kernel, LATE, SPLIT), [shape(late_rows, 128)], [canon, load], specs=[smem, vm()]
    )
    flops = 2 * ROWS * IFACE * IFACE
    middle_shape, square = shape(ROWS, IFACE, BF16), shape(ROWS, ROWS, BF16)

    def right_plain(a, b, out):
        right_kernel(a, b, None, out, None)

    (half,) = call(left_kernel, [middle_shape], [one_w, local_inverse[0, 0, 0]], flops=flops)
    (inverse,) = call(
        right_kernel, [square], [one_w, half, basis], scratch=[pltpu.VMEM((16, ROWS), F32)], flops=flops
    )
    blocks = []
    if plan.ride:
        blocks = spread + transfer([plan.local], spread)
        payloads = first("initial", early, *blocks, [turned])
    else:
        payloads = call(
            lambda base, *outs: write_payloads(plan.plain[0], outs, base, []),
            plan.payload_shapes("plain", 0),
            [early],
        )
    parts = [early, late]
    got = assemble("initial", parts, payloads, blocks, [turned])
    if plan.ride:
        (lift,) = call(
            functools.partial(lifting_kernel, plan),
            [shape(ROWS, 3 * plan.wide, BF16)],
            [turned] + blocks + got,
            scratch=[pltpu.VMEM((plan.wide, plan.wide), F32), pltpu.VMEM((ROWS, plan.wide), F32), pieces],
            flops=2 * ROWS * 3 * plan.wide * plan.wide,
        )
    (half,) = call(left_kernel, [middle_shape], [one, schur_matrix[0, 0, 0]], flops=flops)
    (schur,) = call(right_plain, [square], [one, half], flops=flops)
    sol = residual = None
    flops = 2 * ROWS * ROWS * 128
    for iteration in range(ITERS):
        opening = iteration == 0
        residual, rounded, restricted = call(
            functools.partial(residual_kernel, plan, opening, len(parts)),
            [shape(ROWS, 128), shape(ROWS, 128, BF16), shape(8, 128)],
            parts + got + [inverse] + ([] if opening else [residual]),
            scratch=[acc],
        )
        (base,) = call(
            functools.partial(product_kernel, "all"), [shape(ROWS, 128)], [inverse, rounded], flops=flops
        )
        if plan.ride:
            blocks = [restricted] + transfer([plan.local], [restricted])
            payloads = first("update", base, *blocks, [])
        else:
            blocks = []
            rows = lax.all_gather(restricted[:6], AXES, axis=0, tiled=True)
            correction = jnp.dot(coarse_inverse, rows, precision=lax.Precision.HIGHEST, preferred_element_type=F32)
            base, *payloads = call(
                functools.partial(lift_kernel, plan),
                [shape(ROWS, 128)] + plan.payload_shapes("plain", 0),
                [base, turned, jnp.pad(correction, ((0, 122), (0, 0)))],
            )
        got = assemble("update", [base], payloads, blocks, [])
        update, rounded, early, *payloads = call(
            functools.partial(update_kernel, plan),
            [shape(ROWS, 128), shape(ROWS, 128, BF16), shape(early_rows, 128)] + plan.payload_shapes("plain", 0),
            [base] + got + [schur] + ([lift] + blocks if plan.ride else []),
            scratch=[acc] + ([pltpu.VMEM((plan.wide, 128), F32)] if plan.ride else []),
            flops=flops,
        )
        late, sol = call(
            functools.partial(later_kernel, opening),
            [shape(late_rows, 128), shape(ROWS, 128)],
            [schur, rounded, update] + ([] if opening else [sol]),
            flops=flops // 2,
        )
        parts = [early, late]
        got = assemble("plain", parts, payloads, [], [])
    out = jax.ShapeDtypeStruct((IFACE, 1, loads), F32)
    (sol_out,) = call(scatter_kernel, [out], [canon, sol], specs=[smem, vm()])
    (residual_out,) = call(
        functools.partial(output_kernel, plan),
        [out],
        [canon] + parts + got + [residual],
        specs=[smem] + [vm()] * (3 + len(got)),
        scratch=[acc],
    )
    return tuple(o.reshape(1, 1, 1, IFACE, loads) for o in (sol_out, residual_out))


def solution(mesh):
    plan = Plan(tuple(mesh.shape[a] for a in AXES))
    in_specs = (
        P("gx", "gy", "gz", None, None),
        P("gx", "gy", "gz", None, None),
        P("gx", "gy", "gz", None, None),
        P("gx", "gy", "gz", None, None),
        P(("gx", "gy", "gz"), None),
        P("gx", "gy", "gz", None),
    )
    out_specs = (P("gx", "gy", "gz", None, None), P("gx", "gy", "gz", None, None))
    return jax.shard_map(
        functools.partial(local, plan), mesh=mesh, in_specs=in_specs, out_specs=out_specs, check_vma=False
    )
```

```python
import functools
import itertools

import jax
import jax.numpy as jnp
from jax import lax
from jax.experimental import pallas as pl
from jax.experimental.pallas import tpu as pltpu
from jax.sharding import PartitionSpec as P

NODES = 7
DOF = 3
ITERS = 3
AXES = ("gx", "gy", "gz")
STAGES = ((1,), (0, 2))
SPARE = (2, 1)
PAD = 8
CHUNK = 24
TILE = 256
F32 = jnp.float32
BF16 = jnp.bfloat16


def piece_length(placed):
    return DOF * NODES ** sum(1 for c in placed if c == 1)


PLACES = [p for p in itertools.product(range(3), repeat=3) if p != (1, 1, 1)]
CANON_OFFSET = {}
_at = 0
for _p in PLACES:
    CANON_OFFSET[_p] = _at
    _at += piece_length(_p)
IFACE = _at
LENGTH = {p: piece_length(p) for p in PLACES}
EARLY = [p for p in PLACES if p[1] != 1]
LATE = [p for p in PLACES if p[1] == 1]
SLOT_OFFSET = {}


def _lay(slots, at):
    for slot in slots:
        SLOT_OFFSET[slot] = at
        at += -(-LENGTH[slot] // PAD) * PAD
    return at


COARSE_AT = _lay(EARLY, 0)
SPLIT = -(-(COARSE_AT + 16) // 16) * 16
ROWS = -(-_lay(LATE, SPLIT) // TILE) * TILE
PARTS = {"all": (0, ROWS), "early": (0, SPLIT), "late": (SPLIT, ROWS)}


class Message:
    def __init__(self, moves, sizes, wrap, ride, spare):
        self.moves = moves
        self.sizes = sizes
        self.wrap = wrap
        self.ride = ride
        self.spare = spare
        self.faces = not any(m in ("C", "W") for m in moves)
        self.slots = []
        if self.faces:
            for place in EARLY + LATE:
                if all(m is None or c == (0 if m == "A" else 2) for m, c in zip(moves, place)):
                    self.slots.append(place)
        self.rows = -(-sum(LENGTH[s] for s in self.slots) // PAD) * PAD
        self.basis = []

    def xor(self):
        code = 0
        for move, size in zip(self.moves, self.sizes):
            code = code * size + {None: 0, "A": 1, "B": 3, "C": 2, "W": 3}[move]
        return code

    def pairs(self):
        out = []
        for place in itertools.product(*(range(s) for s in self.sizes)):
            to, whole = [], True
            for at, move, size in zip(place, self.moves, self.sizes):
                if move == "A":
                    at = at ^ 1
                elif move == "B":
                    whole = whole and (self.wrap or 0 < at < size - 1)
                    at = (at - 1) % size if at % 2 == 0 else (at + 1) % size
                elif move == "C":
                    at = at ^ 2
                elif move == "W":
                    at = at ^ 3
                to.append(at)
            if not whole:
                to = [at ^ 1 if d == self.spare else at for d, at in enumerate(place)]
            flat = [0, 0]
            for a, b, size in zip(place, to, self.sizes):
                flat = [flat[0] * size + a, flat[1] * size + b]
            out.append(tuple(flat))
        return out


def stage_messages(stage, sizes, coarse=None):
    choices = []
    for d in range(3):
        if d not in STAGES[stage]:
            choices.append((None,))
        else:
            extra = ("C", "W") if coarse == "update" and stage == 0 and sizes[d] == 4 else ()
            choices.append((None, "A") + (("B",) if sizes[d] > 2 else ()) + extra)
    out = []
    for moves in itertools.product(*choices):
        if all(m is None for m in moves):
            continue
        ride = coarse and (moves[1] != "B" if stage == 0 else moves[2] != "A")
        out.append(Message(moves, sizes, ride and stage == 1, ride, SPARE[stage]))
    return out


class Plan:
    def __init__(self, sizes):
        self.sizes = sizes
        self.subs = sizes[0] * sizes[1] * sizes[2]
        self.ride = all(s in (2, 4) for s in sizes)
        self.wide = self.subs * 8
        self.plain = [stage_messages(i, sizes) for i in range(2)]
        self.setup = 0
        if self.ride:
            self.setup = self.wide // 128
            self.coarse = {k: [stage_messages(i, sizes, k) for i in range(2)] for k in ("initial", "update")}
            self.before = {"update": [Message((None, None, "A"), sizes, False, True, 0)]}
            self.before["initial"] = list(self.before["update"])
            if sizes[1] == 4:
                more = [(None, "C", None), (None, "C", "A")]
                self.before["initial"] += [Message(m, sizes, False, True, 0) for m in more]
            first, second = self.coarse["initial"]
            for message in first:
                message.basis = [(None, slot) for slot in message.slots]
            for message in second:
                message.basis = [(None, slot) for slot in message.slots]
                for other in first:
                    message.basis += [(other, slot) for slot in message.slots if slot in other.slots]

    def per(self, kind):
        return {"plain": 0, "update": 1, "initial": self.setup}[kind] if self.ride else 0

    def messages(self, kind):
        return self.plain if self.per(kind) == 0 else self.coarse[kind]

    def codes(self, kind, stage):
        known = [0] + [m.xor() for m in self.before[kind]]
        if stage == 1:
            known = [k ^ m for m in [0] + [m.xor() for m in self.coarse[kind][0] if m.ride] for k in known]
        return known

    def payload_shapes(self, kind, stage):
        per = self.per(kind)
        out = []
        for m in self.messages(kind)[stage]:
            rows = m.rows
            if m.ride:
                rows += 8 * per * len(self.codes(kind, stage))
            if kind == "initial" and self.ride and m.faces:
                rows += CHUNK
            out.append(shape(rows, 128))
        return out


def position():
    return [lax.axis_index(a) for a in AXES]


def has_b(index, size):
    return jnp.logical_and(index > 0, index < size - 1)


def exists(plan, index, message):
    ok = None
    for d, move in enumerate(message.moves):
        if move == "B":
            here = has_b(index[d], plan.sizes[d])
            ok = here if ok is None else jnp.logical_and(ok, here)
    return ok


def both(a, b):
    return b if a is None else a if b is None else jnp.logical_and(a, b)


def pick(slot, index, of):
    def choose(d, place):
        if d == 3:
            return of(tuple(place))
        if slot[d] == 1:
            return choose(d + 1, place + [1])
        even, odd = (2, 0) if slot[d] == 0 else (0, 2)
        return jnp.where(index[d] % 2 == 0, choose(d + 1, place + [even]), choose(d + 1, place + [odd]))

    return choose(0, [])


def add_received(plan, index, messages, received, acc):
    for message, ref in zip(messages, received):
        if not message.faces:
            continue
        ok = exists(plan, index, message)
        at = 0
        for slot in message.slots:
            rows, to = LENGTH[slot], SLOT_OFFSET[slot]
            value = ref[at : at + rows, :]
            if ok is not None:
                value = jnp.where(ok, value, 0.0)
            acc[to : to + rows, :] += value
            at += rows


def write_payloads(messages, outs, acc, blocks, pack=None):
    for message, out in zip(messages, outs):
        at = 0
        for slot in message.slots:
            rows, frm = LENGTH[slot], SLOT_OFFSET[slot]
            out[at : at + rows, :] = acc[frm : frm + rows, :]
            at += rows
        at = message.rows
        if message.ride:
            for block in blocks:
                out[at : at + 8, :] = block
                at += 8
        if pack is not None and message.faces:
            out[at : at + CHUNK, :] = pack(message)


def packer(own, stage, unpacked):
    def pack(message):
        at = 0
        for source, slot in message.basis:
            rows = LENGTH[slot]
            if source is not None:
                ref = unpacked[source]
                frm = sum(LENGTH[s] for s in source.slots[: source.slots.index(slot)])
            else:
                ref, frm = own, SLOT_OFFSET[slot]
            stage[at : at + rows, :] = ref[frm : frm + rows, :]
            at += rows
        count = -(-at // CHUNK)
        if at < count * CHUNK:
            stage[at : count * CHUNK, :] = jnp.zeros((count * CHUNK - at, 128), F32)
        total = stage[0:CHUNK, :]
        for k in range(1, count):
            total += pltpu.roll(stage[k * CHUNK : (k + 1) * CHUNK, :], 8 * k, 1)
        return total

    return pack


def unpack(message, block, out):
    count = -(-sum(LENGTH[slot] for _, slot in message.basis) // CHUNK)
    lane = lax.broadcasted_iota(jnp.int32, (CHUNK, 128), 1)
    for k in range(count):
        turned = pltpu.roll(block, 128 - 8 * k, 1) if k else block
        out[k * CHUNK : (k + 1) * CHUNK, :] = jnp.where(lane < 8, turned, 0.0)


def transfer(messages, payloads):
    return [lax.ppermute(p, AXES, m.pairs()) for m, p in zip(messages, payloads)]


def vm():
    return pl.BlockSpec(memory_space=pltpu.VMEM)


def shape(rows, cols, dtype=F32):
    return jax.ShapeDtypeStruct((rows, cols), dtype)


def call(kernel, outs, operands, specs=None, scratch=(), limit=20, flops=0):
    nbytes = sum(o.size * o.dtype.itemsize for o in list(outs) + list(operands))
    return pl.pallas_call(
        kernel,
        out_shape=tuple(outs),
        in_specs=specs or [vm()] * len(operands),
        out_specs=tuple(vm() for _ in outs),
        scratch_shapes=list(scratch),
        compiler_params=pltpu.CompilerParams(vmem_limit_bytes=limit << 20),
        cost_estimate=pl.CostEstimate(flops=flops, bytes_accessed=nbytes, transcendentals=0),
    )(*operands)


def gather_kernel(slots, start, canon, load, acc):
    index = position()
    acc[...] = jnp.zeros(acc.shape, F32)
    for slot in slots:
        length, at = LENGTH[slot], SLOT_OFFSET[slot] - start
        off = pick(slot, index, lambda place: jnp.int32(CANON_OFFSET[place]))
        step = 21 if length % 21 == 0 else 3

        def body(i, _, off=off, at=at, step=step):
            for j in range(step):
                row = i * step + j
                acc[pl.ds(at + row, 1), :] = load[canon[0, off + row], :, :]
            return 0

        lax.fori_loop(0, length // step, body, 0)


def scatter_rows(index, canon, acc, out):
    for slot in PLACES:
        length, at = LENGTH[slot], SLOT_OFFSET[slot]
        off = pick(slot, index, lambda place: jnp.int32(CANON_OFFSET[place]))
        step = 21 if length % 21 == 0 else 3

        def body(i, _, off=off, at=at, step=step):
            for j in range(step):
                row = i * step + j
                out[canon[0, off + row], :, :] = acc[pl.ds(at + row, 1), :]
            return 0

        lax.fori_loop(0, length // step, body, 0)


def scatter_kernel(canon, acc, out):
    scatter_rows(position(), canon, acc, out)


def split(value, parts):
    out = []
    for _ in range(parts):
        piece = value.astype(BF16)
        out.append(piece)
        value = value - piece.astype(F32)
    return out


def dot(a, b):
    return jnp.dot(a, b, preferred_element_type=F32)


def dot_last(a, b):
    return lax.dot_general(a, b, (((1,), (1,)), ((), ())), preferred_element_type=F32)


def tile(t):
    return pl.ds(pl.multiple_of(t * TILE, TILE), TILE)


def each_tile(body):
    def step(t, _):
        body(tile(t))
        return 0

    lax.fori_loop(0, ROWS // TILE, step, 0)


def select_kernel(plan, canon, one, weight_out, src):
    index = position()
    src[...] = jnp.full(src.shape, -1, jnp.int32)
    weight_out[...] = jnp.zeros(weight_out.shape, F32)
    for slot in PLACES:
        at, length = SLOT_OFFSET[slot], LENGTH[slot]
        src[at : at + length, :] = pick(
            slot, index, lambda place, length=length: canon[CANON_OFFSET[place] : CANON_OFFSET[place] + length, :]
        )
        weight = jnp.float32(1.0)
        for d in range(3):
            if slot[d] == 0:
                weight = weight * 0.5
            elif slot[d] == 2 and plan.sizes[d] > 2:
                weight = weight * jnp.where(has_b(index[d], plan.sizes[d]), 0.5, 1.0)
        weight_out[at : at + length, :] = jnp.full((length, 128), 1.0, F32) * weight

    def build(rows):
        hit = src[rows, :] == lax.broadcasted_iota(jnp.int32, (TILE, IFACE), 1)
        one[rows, :] = jnp.where(hit, 1.0, 0.0).astype(BF16)

    each_tile(build)


def spread_kernel(plan, cinv, out):
    nc = cinv.shape[1]
    row = lax.broadcasted_iota(jnp.int32, (nc, plan.wide), 0)
    col = lax.broadcasted_iota(jnp.int32, (nc, plan.wide), 1)
    spread = jnp.where(jnp.logical_and((col >> 3) * 6 + (col & 7) == row, (col & 7) < 6), 1.0, 0.0).astype(BF16)
    value = sum(dot(part, spread) for part in split(cinv[...], 3))
    out[...] = jnp.zeros(out.shape, F32)
    for i in range(plan.setup):
        out[8 * i : 8 * i + 6, :] = value[:, 128 * i : 128 * (i + 1)]


def turn_kernel(one, weight, basis, turned):
    turned[...] = jnp.zeros(turned.shape, F32)
    turned[:, :6] = dot_last(one[...], basis[...]) * weight[:, :6]


def left_kernel(one, matrix, weight, basis, mid, few):
    for t in range(0, ROWS, TILE):
        value = dot(one[t : t + TILE, :], matrix[...])
        if weight is not None:
            value = value * weight[t : t + TILE, :1]
        mid[t : t + TILE, :] = value.astype(BF16)
    if basis is not None:
        few[...] = jnp.zeros(few.shape, F32)
        few[:6, :] = basis[...].astype(F32)
        mid[COARSE_AT : COARSE_AT + 16, :] = few[...].astype(BF16)


def right_kernel(one, mid, out):
    for t in range(0, ROWS, TILE):
        out[t : t + TILE, :] = dot_last(mid[t : t + TILE, :], one[...]).astype(BF16)


def fill(acc, parts):
    at = 0
    for part in parts:
        acc[at : at + part.shape[0], :] = part[...]
        at += part.shape[0]


def known_blocks(plan, kind, own, swapped, arrived, per):
    blocks = own + [ref[8 * i : 8 * (i + 1), :] for ref in swapped for i in range(per)]
    count = len(blocks)
    for message, ref in zip(plan.coarse[kind][0], arrived):
        if message.ride:
            blocks += [ref[message.rows + 8 * i : message.rows + 8 * (i + 1), :] for i in range(count)]
    return blocks


def first_kernel(plan, kind, *refs):
    refs = list(refs)
    base, own = refs.pop(0), refs.pop(0)
    swapped = [refs.pop(0) for _ in plan.before[kind]]
    per = plan.per(kind)
    pack = None
    if kind == "initial":
        turned = refs.pop(0)
        pack = packer(turned, refs.pop(-1), {})
    mine = [own[8 * i : 8 * (i + 1), :] for i in range(per)]
    write_payloads(plan.coarse[kind][0], refs, base, known_blocks(plan, kind, mine, swapped, [], per), pack)


def middle_kernel(plan, kind, count, *refs):
    first, second = plan.messages(kind)
    per = plan.per(kind)
    refs = list(refs)
    parts = [refs.pop(0) for _ in range(count)]
    received = [refs.pop(0) for _ in first]
    blocks, pack = [], None
    if per:
        own = refs.pop(0)
        swapped = [refs.pop(0) for _ in plan.before[kind]]
        mine = [own[8 * i : 8 * (i + 1), :] for i in range(per)]
        blocks = known_blocks(plan, kind, mine, swapped, received, per)
    if per and kind == "initial":
        turned = refs.pop(0)
        stage = refs.pop(-1)
        kept = {m: refs.pop(-1) for m in reversed(first) if m.faces}
        for message, ref in zip(first, received):
            if message.faces:
                unpack(message, ref[ref.shape[0] - CHUNK :, :], kept[message])
        pack = packer(turned, stage, kept)
    acc = refs.pop(-1)
    fill(acc, parts)
    add_received(plan, position(), first, received, acc)
    write_payloads(second, refs, acc, blocks, pack)


def product_kernel(part, matrix, vector, out):
    start, stop = PARTS[part]
    size = (stop - start) // (4 if part == "all" else 2)
    for t in range(start, stop, size):
        out[t - start : t - start + size, :] = dot(matrix[t : t + size, :], vector[...])


def finish(plan, kind, parts, got, acc):
    first, second = plan.messages(kind)
    index = position()
    fill(acc, parts)
    add_received(plan, index, first, got[: len(first)], acc)
    add_received(plan, index, second, got[len(first) :], acc)


def residual_kernel(plan, opening, count, *refs):
    kind = "initial" if opening else "plain"
    refs = list(refs)
    parts = [refs.pop(0) for _ in range(count)]
    got = [refs.pop(0) for _ in range(sum(len(m) for m in plan.messages(kind)))]
    matrix, weight = refs.pop(0), refs.pop(0)
    before = None if opening else refs.pop(0)
    residual, rounded, restricted, acc = refs
    finish(plan, kind, parts, got, acc)
    value = acc[...] if opening else before[...] - acc[...]
    residual[...] = value
    rounded[...] = (weight[...] * value).astype(BF16)
    restricted[...] = dot(matrix[COARSE_AT : COARSE_AT + 16, :], rounded[...])[:8]


def lift_kernel(plan, base, turned, correction, out, *outs):
    lifted = turned[...].astype(BF16)
    out[...] = base[...] + sum(dot(lifted, part) for part in split(correction[...], 3))
    write_payloads(plan.plain[0], outs, out, [])


def collect(plan, kind, own, got, per, which, stack, at_column):
    first, second = plan.coarse[kind]
    index = position()
    me = (index[0] * plan.sizes[1] + index[1]) * plan.sizes[2] + index[2]

    def put(code, value):
        stack[pl.ds(pl.multiple_of((me ^ code) * 8, 8), 8), at_column : at_column + 128] = value

    put(0, own[8 * which : 8 * (which + 1), :])
    for m in plan.before[kind]:
        put(m.xor(), got[0][8 * which : 8 * (which + 1), :])
        got = got[1:]
    for stage, messages in enumerate((first, second)):
        for m, ref in zip(messages, got):
            if m.ride:
                for i, code in enumerate(plan.codes(kind, stage)):
                    at = m.rows + 8 * (per * i + which)
                    put(code ^ m.xor(), ref[at : at + 8, :])
        got = got[len(messages) :]


def lifting_kernel(plan, *refs):
    first, second = plan.coarse["initial"]
    turned, spread, *got, out, stack, many, unpacked = refs
    swapped, got = got[: len(plan.before["initial"])], got[len(plan.before["initial"]) :]
    per = plan.setup
    index = position()
    me = (index[0] * plan.sizes[1] + index[1]) * plan.sizes[2] + index[2]

    def place(code, value, to, ok):
        there = me ^ code
        value = pltpu.roll(value, (there & 15) * 8, 1)
        rows = value.shape[0]
        for half in range(per):
            here = both((there >> 4) == half, ok)
            many[to : to + rows, 128 * half : 128 * (half + 1)] += jnp.where(here, value, 0.0)

    many[...] = jnp.zeros(many.shape, F32)
    for t in range(ROWS // TILE):
        place(0, turned[t * TILE : (t + 1) * TILE, :], t * TILE, None)
    for m, ref in zip(first + second, got):
        if not m.faces:
            continue
        unpack(m, ref[ref.shape[0] - CHUNK :, :], unpacked)
        at, ok = 0, exists(plan, index, m)
        for source, slot in m.basis:
            code, fine = m.xor(), ok
            if source is not None:
                code ^= source.xor()
                fine = both(exists(plan, index, source), ok)
            place(code, unpacked[at : at + LENGTH[slot], :], SLOT_OFFSET[slot], fine)
            at += LENGTH[slot]
    for half in range(per):
        collect(plan, "initial", spread, swapped + got, per, half, stack, 128 * half)
    parts = jnp.concatenate(split(stack[...], 3), axis=0)

    def body(rows):
        basis = many[rows, :].astype(BF16)
        whole = dot(jnp.concatenate([basis] * 3, axis=1), parts)
        high, low = split(whole, 2)
        out[rows, :] = jnp.concatenate([high, high, low], axis=1)

    each_tile(body)


def update_kernel(plan, *refs):
    refs = list(refs)
    base = refs.pop(0)
    got = [refs.pop(0) for _ in range(sum(len(m) for m in plan.messages("update")))]
    matrix = refs.pop(0)
    if plan.ride:
        lift, own = refs.pop(0), refs.pop(0)
        swapped = [refs.pop(0) for _ in plan.before["update"]]
        stack = refs.pop(-1)
    acc = refs.pop(-1)
    update, rounded, early, *outs = refs
    finish(plan, "update", [base], got, acc)
    if plan.ride:
        collect(plan, "update", own, swapped + got, 1, 0, stack, 0)
        high, low = split(stack[...], 2)
        right = jnp.concatenate([high, low, high], axis=0)
        for t in range(0, ROWS, 320):
            value = acc[t : t + 320, :] + dot(lift[t : t + 320, :], right)
            update[t : t + 320, :] = value
            rounded[t : t + 320, :] = value.astype(BF16)
    else:
        update[...] = acc[...]
        rounded[...] = acc[...].astype(BF16)
    product_kernel("early", matrix, rounded, early)
    write_payloads(plan.plain[0], outs, early, [])


def later_kernel(opening, matrix, rounded, update, *refs):
    late, total = refs[-2:]
    product_kernel("late", matrix, rounded, late)
    total[...] = update[...] if opening else refs[0][...] + update[...]


def output_kernel(plan, canon, early, late, *refs):
    *got, residual, out, acc = refs
    finish(plan, "plain", [early, late], got, acc)
    acc[...] = residual[...] - acc[...]
    scatter_rows(position(), canon, acc, out)


def local(plan, load_cases, schur_matrix, local_inverse, coarse_basis, coarse_inverse, canon_rows):
    smem = pl.BlockSpec(memory_space=pltpu.SMEM)
    loads = load_cases.shape[-1]
    canon = canon_rows.reshape(1, IFACE)
    load = load_cases.reshape(IFACE, 1, loads)
    basis = coarse_basis[0, 0, 0]
    acc = pltpu.VMEM((ROWS, 128), F32)
    pieces = pltpu.VMEM((16 * CHUNK, 128), F32)
    early_rows, late_rows = SPLIT, ROWS - SPLIT

    def spread_out(kind, own):
        return [own] + transfer(plan.before[kind], [own] * len(plan.before[kind]))

    def first(kind, base, blocks, more):
        return call(
            functools.partial(first_kernel, plan, kind),
            plan.payload_shapes(kind, 0),
            [base] + blocks + more,
            scratch=[pieces] if kind == "initial" else [],
        )

    def assemble(kind, parts, payloads, blocks, more):
        messages = plan.messages(kind)
        got = transfer(messages[0], payloads)
        setup = kind == "initial" and plan.ride
        payloads = call(
            functools.partial(middle_kernel, plan, kind, len(parts)),
            plan.payload_shapes(kind, 1),
            parts + got + blocks + (more if setup else []),
            scratch=[acc] + ([pieces] * (1 + sum(m.faces for m in messages[0])) if setup else []),
        )
        return got + transfer(messages[1], payloads)

    one, weight = call(
        functools.partial(select_kernel, plan),
        [shape(ROWS, IFACE, BF16), shape(ROWS, 128)],
        [canon_rows.reshape(IFACE, 1)],
        scratch=[pltpu.VMEM((ROWS, 1), jnp.int32)],
        flops=ROWS * IFACE * 1158,
    )
    if plan.ride:
        (spread,) = call(
            functools.partial(spread_kernel, plan), [shape(8 * plan.setup, 128)], [coarse_inverse]
        )
    (turned,) = call(turn_kernel, [shape(ROWS, 128)], [one, weight, basis])
    (early,) = call(
        functools.partial(gather_kernel, EARLY, 0), [shape(early_rows, 128)], [canon, load], specs=[smem, vm()]
    )
    (late,) = call(
        functools.partial(gather_kernel, LATE, SPLIT), [shape(late_rows, 128)], [canon, load], specs=[smem, vm()]
    )
    flops = 2 * ROWS * IFACE * IFACE
    middle_shape, square = shape(ROWS, IFACE, BF16), shape(ROWS, ROWS, BF16)

    def left_plain(one, matrix, mid):
        left_kernel(one, matrix, None, None, mid, None)

    (half,) = call(
        left_kernel,
        [middle_shape],
        [one, local_inverse[0, 0, 0], weight, basis],
        scratch=[pltpu.VMEM((16, IFACE), F32)],
        flops=flops,
    )
    (inverse,) = call(right_kernel, [square], [one, half], flops=flops)
    blocks = []
    if plan.ride:
        blocks = spread_out("initial", spread)
        payloads = first("initial", early, blocks, [turned])
    else:
        payloads = call(
            lambda base, *outs: write_payloads(plan.plain[0], outs, base, []),
            plan.payload_shapes("plain", 0),
            [early],
        )
    parts = [early, late]
    got = assemble("initial", parts, payloads, blocks, [turned])
    if plan.ride:
        (lift,) = call(
            functools.partial(lifting_kernel, plan),
            [shape(ROWS, 3 * plan.wide, BF16)],
            [turned] + blocks + got,
            scratch=[pltpu.VMEM((plan.wide, plan.wide), F32), pltpu.VMEM((ROWS, plan.wide), F32), pieces],
            flops=2 * ROWS * 3 * plan.wide * plan.wide,
        )
    (half,) = call(left_plain, [middle_shape], [one, schur_matrix[0, 0, 0]], flops=flops)
    (schur,) = call(right_kernel, [square], [one, half], flops=flops)
    sol = residual = None
    flops = 2 * ROWS * ROWS * 128
    for iteration in range(ITERS):
        opening = iteration == 0
        residual, rounded, restricted = call(
            functools.partial(residual_kernel, plan, opening, len(parts)),
            [shape(ROWS, 128), shape(ROWS, 128, BF16), shape(8, 128)],
            parts + got + [inverse, weight] + ([] if opening else [residual]),
            scratch=[acc],
        )
        if plan.ride:
            blocks = spread_out("update", restricted)
        (base,) = call(
            functools.partial(product_kernel, "all"), [shape(ROWS, 128)], [inverse, rounded], flops=flops
        )
        if plan.ride:
            payloads = first("update", base, blocks, [])
        else:
            blocks = []
            rows = lax.all_gather(restricted[:6], AXES, axis=0, tiled=True)
            correction = jnp.dot(coarse_inverse, rows, precision=lax.Precision.HIGHEST, preferred_element_type=F32)
            base, *payloads = call(
                functools.partial(lift_kernel, plan),
                [shape(ROWS, 128)] + plan.payload_shapes("plain", 0),
                [base, turned, jnp.pad(correction, ((0, 122), (0, 0)))],
            )
        got = assemble("update", [base], payloads, blocks, [])
        update, rounded, early, *payloads = call(
            functools.partial(update_kernel, plan),
            [shape(ROWS, 128), shape(ROWS, 128, BF16), shape(early_rows, 128)] + plan.payload_shapes("plain", 0),
            [base] + got + [schur] + ([lift] + blocks if plan.ride else []),
            scratch=[acc] + ([pltpu.VMEM((plan.wide, 128), F32)] if plan.ride else []),
            flops=flops,
        )
        late, sol = call(
            functools.partial(later_kernel, opening),
            [shape(late_rows, 128), shape(ROWS, 128)],
            [schur, rounded, update] + ([] if opening else [sol]),
            flops=flops // 2,
        )
        parts = [early, late]
        got = assemble("plain", parts, payloads, [], [])
    out = jax.ShapeDtypeStruct((IFACE, 1, loads), F32)
    (sol_out,) = call(scatter_kernel, [out], [canon, sol], specs=[smem, vm()])
    (residual_out,) = call(
        functools.partial(output_kernel, plan),
        [out],
        [canon] + parts + got + [residual],
        specs=[smem] + [vm()] * (3 + len(got)),
        scratch=[acc],
    )
    return tuple(o.reshape(1, 1, 1, IFACE, loads) for o in (sol_out, residual_out))


def solution(mesh):
    plan = Plan(tuple(mesh.shape[a] for a in AXES))
    in_specs = (
        P("gx", "gy", "gz", None, None),
        P("gx", "gy", "gz", None, None),
        P("gx", "gy", "gz", None, None),
        P("gx", "gy", "gz", None, None),
        P(("gx", "gy", "gz"), None),
        P("gx", "gy", "gz", None),
    )
    out_specs = (P("gx", "gy", "gz", None, None), P("gx", "gy", "gz", None, None))
    return jax.shard_map(
        functools.partial(local, plan), mesh=mesh, in_specs=in_specs, out_specs=out_specs, check_vma=False
    )
```

```python
import functools
import itertools

import jax
import jax.numpy as jnp
from jax import lax
from jax.experimental import pallas as pl
from jax.experimental.pallas import tpu as pltpu
from jax.sharding import PartitionSpec as P

NODES = 7
DOF = 3
ITERS = 3
AXES = ("gx", "gy", "gz")
STAGES = ((1,), (0, 2))
SPARE = (2, 1)
PAD = 8
CHUNK = 24
TILE = 256
BATCH = 16
F32 = jnp.float32
BF16 = jnp.bfloat16


def piece_length(placed):
    return DOF * NODES ** sum(1 for c in placed if c == 1)


PLACES = [p for p in itertools.product(range(3), repeat=3) if p != (1, 1, 1)]
CANON_OFFSET = {}
_at = 0
for _p in PLACES:
    CANON_OFFSET[_p] = _at
    _at += piece_length(_p)
IFACE = _at
LENGTH = {p: piece_length(p) for p in PLACES}
EARLY = [p for p in PLACES if p[1] != 1]
LATE = [p for p in PLACES if p[1] == 1]
SLOT_OFFSET = {}


def _lay(slots, at):
    for slot in slots:
        SLOT_OFFSET[slot] = at
        at += -(-LENGTH[slot] // PAD) * PAD
    return at


COARSE_AT = _lay(EARLY, 0)
SPLIT = -(-(COARSE_AT + 16) // 16) * 16
ROWS = -(-_lay(LATE, SPLIT) // TILE) * TILE
PARTS = {"all": (0, ROWS), "early": (0, SPLIT), "late": (SPLIT, ROWS)}


class Message:
    def __init__(self, moves, sizes, wrap, ride, spare):
        self.moves = moves
        self.sizes = sizes
        self.wrap = wrap
        self.ride = ride
        self.spare = spare
        self.faces = not any(m in ("C", "W") for m in moves)
        self.slots = []
        if self.faces:
            for place in EARLY + LATE:
                if all(m is None or c == (0 if m == "A" else 2) for m, c in zip(moves, place)):
                    self.slots.append(place)
        self.rows = -(-sum(LENGTH[s] for s in self.slots) // PAD) * PAD
        self.basis = []

    def xor(self):
        code = 0
        for move, size in zip(self.moves, self.sizes):
            code = code * size + {None: 0, "A": 1, "B": 3, "C": 2, "W": 3}[move]
        return code

    def pairs(self):
        out = []
        for place in itertools.product(*(range(s) for s in self.sizes)):
            to, whole = [], True
            for at, move, size in zip(place, self.moves, self.sizes):
                if move == "A":
                    at = at ^ 1
                elif move == "B":
                    whole = whole and (self.wrap or 0 < at < size - 1)
                    at = (at - 1) % size if at % 2 == 0 else (at + 1) % size
                elif move == "C":
                    at = at ^ 2
                elif move == "W":
                    at = at ^ 3
                to.append(at)
            if not whole:
                to = [at ^ 1 if d == self.spare else at for d, at in enumerate(place)]
            flat = [0, 0]
            for a, b, size in zip(place, to, self.sizes):
                flat = [flat[0] * size + a, flat[1] * size + b]
            out.append(tuple(flat))
        return out


def stage_messages(stage, sizes, coarse=None):
    choices = []
    for d in range(3):
        if d not in STAGES[stage]:
            choices.append((None,))
        else:
            extra = ("C", "W") if coarse == "update" and stage == 0 and sizes[d] == 4 else ()
            choices.append((None, "A") + (("B",) if sizes[d] > 2 else ()) + extra)
    out = []
    for moves in itertools.product(*choices):
        if all(m is None for m in moves):
            continue
        ride = coarse and (moves[1] != "B" if stage == 0 else moves[2] != "A")
        out.append(Message(moves, sizes, ride and stage == 1, ride, SPARE[stage]))
    return out


class Plan:
    def __init__(self, sizes):
        self.sizes = sizes
        self.subs = sizes[0] * sizes[1] * sizes[2]
        self.ride = all(s in (2, 4) for s in sizes)
        self.wide = self.subs * 8
        self.plain = [stage_messages(i, sizes) for i in range(2)]
        self.setup = 0
        if self.ride:
            self.setup = self.wide // 128
            self.coarse = {k: [stage_messages(i, sizes, k) for i in range(2)] for k in ("initial", "update")}
            self.before = {"update": [Message((None, None, "A"), sizes, False, True, 0)]}
            self.before["initial"] = list(self.before["update"])
            if sizes[1] == 4:
                more = [(None, "C", None), (None, "C", "A")]
                self.before["initial"] += [Message(m, sizes, False, True, 0) for m in more]
            first, second = self.coarse["initial"]
            for message in first:
                message.basis = [(None, slot) for slot in message.slots]
            for message in second:
                message.basis = [(None, slot) for slot in message.slots]
                for other in first:
                    message.basis += [(other, slot) for slot in message.slots if slot in other.slots]

    def per(self, kind):
        return {"plain": 0, "update": 1, "initial": self.setup}[kind] if self.ride else 0

    def messages(self, kind):
        return self.plain if self.per(kind) == 0 else self.coarse[kind]

    def codes(self, kind, stage):
        known = [0] + [m.xor() for m in self.before[kind]]
        if stage == 1:
            known = [k ^ m for m in [0] + [m.xor() for m in self.coarse[kind][0] if m.ride] for k in known]
        return known

    def payload_shapes(self, kind, stage):
        per = self.per(kind)
        out = []
        for m in self.messages(kind)[stage]:
            rows = m.rows
            if m.ride:
                rows += 8 * per * len(self.codes(kind, stage))
            if kind == "initial" and self.ride and m.faces:
                rows += CHUNK
            out.append(shape(rows, 128))
        return out


def position():
    return [lax.axis_index(a) for a in AXES]


def has_b(index, size):
    return jnp.logical_and(index > 0, index < size - 1)


def exists(plan, index, message):
    ok = None
    for d, move in enumerate(message.moves):
        if move == "B":
            here = has_b(index[d], plan.sizes[d])
            ok = here if ok is None else jnp.logical_and(ok, here)
    return ok


def both(a, b):
    return b if a is None else a if b is None else jnp.logical_and(a, b)


def pick(slot, index, of):
    def choose(d, place):
        if d == 3:
            return of(tuple(place))
        if slot[d] == 1:
            return choose(d + 1, place + [1])
        even, odd = (2, 0) if slot[d] == 0 else (0, 2)
        return jnp.where(index[d] % 2 == 0, choose(d + 1, place + [even]), choose(d + 1, place + [odd]))

    return choose(0, [])


def add_received(plan, index, messages, received, acc):
    for message, ref in zip(messages, received):
        if not message.faces:
            continue
        ok = exists(plan, index, message)
        at = 0
        for slot in message.slots:
            rows, to = LENGTH[slot], SLOT_OFFSET[slot]
            value = ref[at : at + rows, :]
            if ok is not None:
                value = jnp.where(ok, value, 0.0)
            acc[to : to + rows, :] += value
            at += rows


def write_payloads(messages, outs, acc, blocks, pack=None):
    for message, out in zip(messages, outs):
        at = 0
        for slot in message.slots:
            rows, frm = LENGTH[slot], SLOT_OFFSET[slot]
            out[at : at + rows, :] = acc[frm : frm + rows, :]
            at += rows
        at = message.rows
        if message.ride:
            for block in blocks:
                out[at : at + 8, :] = block
                at += 8
        if pack is not None and message.faces:
            out[at : at + CHUNK, :] = pack(message)


def packer(own, stage, unpacked):
    def pack(message):
        at = 0
        for source, slot in message.basis:
            rows = LENGTH[slot]
            if source is not None:
                ref = unpacked[source]
                frm = sum(LENGTH[s] for s in source.slots[: source.slots.index(slot)])
            else:
                ref, frm = own, SLOT_OFFSET[slot]
            stage[at : at + rows, :] = ref[frm : frm + rows, :]
            at += rows
        count = -(-at // CHUNK)
        if at < count * CHUNK:
            stage[at : count * CHUNK, :] = jnp.zeros((count * CHUNK - at, 128), F32)
        total = stage[0:CHUNK, :]
        for k in range(1, count):
            total += pltpu.roll(stage[k * CHUNK : (k + 1) * CHUNK, :], 8 * k, 1)
        return total

    return pack


def unpack(message, block, out):
    count = -(-sum(LENGTH[slot] for _, slot in message.basis) // CHUNK)
    lane = lax.broadcasted_iota(jnp.int32, (CHUNK, 128), 1)
    for k in range(count):
        turned = pltpu.roll(block, 128 - 8 * k, 1) if k else block
        out[k * CHUNK : (k + 1) * CHUNK, :] = jnp.where(lane < 8, turned, 0.0)


def transfer(messages, payloads):
    return [lax.ppermute(p, AXES, m.pairs()) for m, p in zip(messages, payloads)]


def vm():
    return pl.BlockSpec(memory_space=pltpu.VMEM)


def shape(rows, cols, dtype=F32):
    return jax.ShapeDtypeStruct((rows, cols), dtype)


def call(kernel, outs, operands, specs=None, scratch=(), limit=20, flops=0):
    nbytes = sum(o.size * o.dtype.itemsize for o in list(outs) + list(operands))
    return pl.pallas_call(
        kernel,
        out_shape=tuple(outs),
        in_specs=specs or [vm()] * len(operands),
        out_specs=tuple(vm() for _ in outs),
        scratch_shapes=list(scratch),
        compiler_params=pltpu.CompilerParams(vmem_limit_bytes=limit << 20),
        cost_estimate=pl.CostEstimate(flops=flops, bytes_accessed=nbytes, transcendentals=0),
    )(*operands)


def gather_kernel(slots, start, canon, load, acc):
    index = position()
    acc[...] = jnp.zeros(acc.shape, F32)
    for slot in slots:
        length, at = LENGTH[slot], SLOT_OFFSET[slot] - start
        off = pick(slot, index, lambda place: jnp.int32(CANON_OFFSET[place]))
        for first in range(0, length, BATCH):
            batch = range(first, min(first + BATCH, length))
            values = [load[canon[0, off + row], :, :] for row in batch]
            for row, value in zip(batch, values):
                acc[at + row : at + row + 1, :] = value


def scatter_rows(index, canon, acc, out):
    for slot in PLACES:
        length, at = LENGTH[slot], SLOT_OFFSET[slot]
        off = pick(slot, index, lambda place: jnp.int32(CANON_OFFSET[place]))
        for first in range(0, length, BATCH):
            batch = range(first, min(first + BATCH, length))
            values = [acc[at + row : at + row + 1, :] for row in batch]
            places = [canon[0, off + row] for row in batch]
            for to, value in zip(places, values):
                out[to, :, :] = value


def scatter_kernel(canon, acc, out):
    scatter_rows(position(), canon, acc, out)


def split(value, parts):
    out = []
    for _ in range(parts):
        piece = value.astype(BF16)
        out.append(piece)
        value = value - piece.astype(F32)
    return out


def dot(a, b):
    return jnp.dot(a, b, preferred_element_type=F32)


def dot_last(a, b):
    return lax.dot_general(a, b, (((1,), (1,)), ((), ())), preferred_element_type=F32)


def tile(t):
    return pl.ds(pl.multiple_of(t * TILE, TILE), TILE)


def each_tile(body):
    def step(t, _):
        body(tile(t))
        return 0

    lax.fori_loop(0, ROWS // TILE, step, 0)


def select_kernel(plan, canon, basis, one, weight_out, turned, src):
    index = position()
    src[...] = jnp.full(src.shape, -1, jnp.int32)
    weight_out[...] = jnp.zeros(weight_out.shape, F32)
    for slot in PLACES:
        at, length = SLOT_OFFSET[slot], LENGTH[slot]
        src[at : at + length, :] = pick(
            slot, index, lambda place, length=length: canon[CANON_OFFSET[place] : CANON_OFFSET[place] + length, :]
        )
        weight = jnp.float32(1.0)
        for d in range(3):
            if slot[d] == 0:
                weight = weight * 0.5
            elif slot[d] == 2 and plan.sizes[d] > 2:
                weight = weight * jnp.where(has_b(index[d], plan.sizes[d]), 0.5, 1.0)
        weight_out[at : at + length, :] = jnp.full((length, 128), 1.0, F32) * weight

    turned[...] = jnp.zeros(turned.shape, F32)
    for t in range(0, ROWS, TILE):
        rows = slice(t, t + TILE)
        hit = src[rows, :] == lax.broadcasted_iota(jnp.int32, (TILE, IFACE), 1)
        picked = jnp.where(hit, 1.0, 0.0).astype(BF16)
        one[rows, :] = picked
        turned[rows, :6] = dot_last(picked, basis[...]) * weight_out[rows, :6]


def spread_kernel(plan, cinv, out):
    nc = cinv.shape[1]
    row = lax.broadcasted_iota(jnp.int32, (nc, plan.wide), 0)
    col = lax.broadcasted_iota(jnp.int32, (nc, plan.wide), 1)
    spread = jnp.where(jnp.logical_and((col >> 3) * 6 + (col & 7) == row, (col & 7) < 6), 1.0, 0.0).astype(BF16)
    value = sum(dot(part, spread) for part in split(cinv[...], 3))
    out[...] = jnp.zeros(out.shape, F32)
    for i in range(plan.setup):
        out[8 * i : 8 * i + 6, :] = value[:, 128 * i : 128 * (i + 1)]


def left_kernel(one, matrix, weight, basis, mid, few):
    for t in range(0, ROWS, TILE):
        value = dot(one[t : t + TILE, :], matrix[...])
        if weight is not None:
            value = value * weight[t : t + TILE, :1]
        mid[t : t + TILE, :] = value.astype(BF16)
    if basis is not None:
        few[...] = jnp.zeros(few.shape, F32)
        few[:6, :] = basis[...].astype(F32)
        mid[COARSE_AT : COARSE_AT + 16, :] = few[...].astype(BF16)


def right_left_kernel(one, mid, other, out, mid_other):
    right_kernel(one, mid, out)
    left_kernel(one, other, None, None, mid_other, None)


def right_kernel(one, mid, out):
    for t in range(0, ROWS, TILE):
        out[t : t + TILE, :] = dot_last(mid[t : t + TILE, :], one[...]).astype(BF16)


def fill(acc, parts):
    at = 0
    for part in parts:
        acc[at : at + part.shape[0], :] = part[...]
        at += part.shape[0]


def known_blocks(plan, kind, own, swapped, arrived, per):
    blocks = own + [ref[8 * i : 8 * (i + 1), :] for ref in swapped for i in range(per)]
    count = len(blocks)
    for message, ref in zip(plan.coarse[kind][0], arrived):
        if message.ride:
            blocks += [ref[message.rows + 8 * i : message.rows + 8 * (i + 1), :] for i in range(count)]
    return blocks


def first_kernel(plan, kind, *refs):
    refs = list(refs)
    base, own = refs.pop(0), refs.pop(0)
    swapped = [refs.pop(0) for _ in plan.before[kind]]
    per = plan.per(kind)
    pack = None
    if kind == "initial":
        turned = refs.pop(0)
        pack = packer(turned, refs.pop(-1), {})
    mine = [own[8 * i : 8 * (i + 1), :] for i in range(per)]
    write_payloads(plan.coarse[kind][0], refs, base, known_blocks(plan, kind, mine, swapped, [], per), pack)


def middle_kernel(plan, kind, count, after, *refs):
    first, second = plan.messages(kind)
    per = plan.per(kind)
    refs = list(refs)
    parts = [refs.pop(0) for _ in range(count)]
    if after:
        refs.pop(0)
    received = [refs.pop(0) for _ in first]
    blocks, pack = [], None
    if per:
        own = refs.pop(0)
        swapped = [refs.pop(0) for _ in plan.before[kind]]
        mine = [own[8 * i : 8 * (i + 1), :] for i in range(per)]
        blocks = known_blocks(plan, kind, mine, swapped, received, per)
    if per and kind == "initial":
        turned = refs.pop(0)
        stage = refs.pop(-1)
        kept = {m: refs.pop(-1) for m in reversed(first) if m.faces}
        for message, ref in zip(first, received):
            if message.faces:
                unpack(message, ref[ref.shape[0] - CHUNK :, :], kept[message])
        pack = packer(turned, stage, kept)
    acc = refs.pop(-1)
    fill(acc, parts)
    add_received(plan, position(), first, received, acc)
    write_payloads(second, refs, acc, blocks, pack)


def product_kernel(part, matrix, vector, out):
    start, stop = PARTS[part]
    size = (stop - start) // (4 if part == "all" else 2)
    for t in range(start, stop, size):
        out[t - start : t - start + size, :] = dot(matrix[t : t + size, :], vector[...])


def finish(plan, kind, parts, got, acc):
    first, second = plan.messages(kind)
    index = position()
    fill(acc, parts)
    add_received(plan, index, first, got[: len(first)], acc)
    add_received(plan, index, second, got[len(first) :], acc)


def residual_kernel(plan, opening, count, *refs):
    kind = "initial" if opening else "plain"
    refs = list(refs)
    parts = [refs.pop(0) for _ in range(count)]
    got = [refs.pop(0) for _ in range(sum(len(m) for m in plan.messages(kind)))]
    matrix, weight = refs.pop(0), refs.pop(0)
    before = None if opening else refs.pop(0)
    residual, rounded, restricted, acc = refs
    finish(plan, kind, parts, got, acc)
    value = acc[...] if opening else before[...] - acc[...]
    residual[...] = value
    rounded[...] = (weight[...] * value).astype(BF16)
    restricted[...] = dot(matrix[COARSE_AT : COARSE_AT + 16, :], rounded[...])[:8]


def lift_kernel(plan, base, turned, correction, out, *outs):
    lifted = turned[...].astype(BF16)
    out[...] = base[...] + sum(dot(lifted, part) for part in split(correction[...], 3))
    write_payloads(plan.plain[0], outs, out, [])


def collect(plan, kind, own, got, per, which, stack, at_column):
    first, second = plan.coarse[kind]
    index = position()
    me = (index[0] * plan.sizes[1] + index[1]) * plan.sizes[2] + index[2]

    def put(code, value):
        stack[pl.ds(pl.multiple_of((me ^ code) * 8, 8), 8), at_column : at_column + 128] = value

    put(0, own[8 * which : 8 * (which + 1), :])
    for m in plan.before[kind]:
        put(m.xor(), got[0][8 * which : 8 * (which + 1), :])
        got = got[1:]
    for stage, messages in enumerate((first, second)):
        for m, ref in zip(messages, got):
            if m.ride:
                for i, code in enumerate(plan.codes(kind, stage)):
                    at = m.rows + 8 * (per * i + which)
                    put(code ^ m.xor(), ref[at : at + 8, :])
        got = got[len(messages) :]


def lifting_kernel(plan, *refs):
    first, second = plan.coarse["initial"]
    turned, spread, *got, out, stack, many, unpacked = refs
    swapped, got = got[: len(plan.before["initial"])], got[len(plan.before["initial"]) :]
    per = plan.setup
    index = position()
    me = (index[0] * plan.sizes[1] + index[1]) * plan.sizes[2] + index[2]

    def place(code, value, to, ok):
        there = me ^ code
        value = pltpu.roll(value, (there & 15) * 8, 1)
        rows = value.shape[0]
        for half in range(per):
            here = both((there >> 4) == half, ok)
            many[to : to + rows, 128 * half : 128 * (half + 1)] += jnp.where(here, value, 0.0)

    many[...] = jnp.zeros(many.shape, F32)
    for t in range(ROWS // TILE):
        place(0, turned[t * TILE : (t + 1) * TILE, :], t * TILE, None)
    for m, ref in zip(first + second, got):
        if not m.faces:
            continue
        unpack(m, ref[ref.shape[0] - CHUNK :, :], unpacked)
        at, ok = 0, exists(plan, index, m)
        for source, slot in m.basis:
            code, fine = m.xor(), ok
            if source is not None:
                code ^= source.xor()
                fine = both(exists(plan, index, source), ok)
            place(code, unpacked[at : at + LENGTH[slot], :], SLOT_OFFSET[slot], fine)
            at += LENGTH[slot]
    for half in range(per):
        collect(plan, "initial", spread, swapped + got, per, half, stack, 128 * half)
    parts = jnp.concatenate(split(stack[...], 3), axis=0)

    def body(rows):
        basis = many[rows, :].astype(BF16)
        whole = dot(jnp.concatenate([basis] * 3, axis=1), parts)
        high, low = split(whole, 2)
        out[rows, :] = jnp.concatenate([high, high, low], axis=1)

    each_tile(body)


def update_kernel(plan, *refs):
    refs = list(refs)
    base = refs.pop(0)
    got = [refs.pop(0) for _ in range(sum(len(m) for m in plan.messages("update")))]
    matrix = refs.pop(0)
    if plan.ride:
        lift, own = refs.pop(0), refs.pop(0)
        swapped = [refs.pop(0) for _ in plan.before["update"]]
        stack = refs.pop(-1)
    acc = refs.pop(-1)
    update, rounded, early, *outs = refs
    finish(plan, "update", [base], got, acc)
    if plan.ride:
        collect(plan, "update", own, swapped + got, 1, 0, stack, 0)
        high, low = split(stack[...], 2)
        right = jnp.concatenate([high, low, high], axis=0)
        for t in range(0, ROWS, 320):
            value = acc[t : t + 320, :] + dot(lift[t : t + 320, :], right)
            update[t : t + 320, :] = value
            rounded[t : t + 320, :] = value.astype(BF16)
    else:
        update[...] = acc[...]
        rounded[...] = acc[...].astype(BF16)
    product_kernel("early", matrix, rounded, early)
    write_payloads(plan.plain[0], outs, early, [])


def later_kernel(opening, matrix, rounded, update, *refs):
    late, total = refs[-2:]
    product_kernel("late", matrix, rounded, late)
    total[...] = update[...] if opening else refs[0][...] + update[...]


def output_kernel(plan, canon, early, late, *refs):
    *got, residual, out, acc = refs
    finish(plan, "plain", [early, late], got, acc)
    acc[...] = residual[...] - acc[...]
    scatter_rows(position(), canon, acc, out)


def local(plan, load_cases, schur_matrix, local_inverse, coarse_basis, coarse_inverse, canon_rows):
    smem = pl.BlockSpec(memory_space=pltpu.SMEM)
    loads = load_cases.shape[-1]
    canon = canon_rows.reshape(1, IFACE)
    load = load_cases.reshape(IFACE, 1, loads)
    basis = coarse_basis[0, 0, 0]
    acc = pltpu.VMEM((ROWS, 128), F32)
    pieces = pltpu.VMEM((16 * CHUNK, 128), F32)
    early_rows, late_rows = SPLIT, ROWS - SPLIT

    def spread_out(kind, own):
        return [own] + transfer(plan.before[kind], [own] * len(plan.before[kind]))

    def first(kind, base, blocks, more):
        return call(
            functools.partial(first_kernel, plan, kind),
            plan.payload_shapes(kind, 0),
            [base] + blocks + more,
            scratch=[pieces] if kind == "initial" else [],
        )

    def assemble(kind, parts, payloads, blocks, more, after=()):
        messages = plan.messages(kind)
        got = transfer(messages[0], payloads)
        setup = kind == "initial" and plan.ride
        payloads = call(
            functools.partial(middle_kernel, plan, kind, len(parts), bool(after)),
            plan.payload_shapes(kind, 1),
            parts + list(after) + got + blocks + (more if setup else []),
            scratch=[acc] + ([pieces] * (1 + sum(m.faces for m in messages[0])) if setup else []),
        )
        return got + transfer(messages[1], payloads)

    one, weight, turned = call(
        functools.partial(select_kernel, plan),
        [shape(ROWS, IFACE, BF16), shape(ROWS, 128), shape(ROWS, 128)],
        [canon_rows.reshape(IFACE, 1), basis],
        scratch=[pltpu.VMEM((ROWS, 1), jnp.int32)],
        flops=ROWS * IFACE * 1158,
    )
    if plan.ride:
        (spread,) = call(
            functools.partial(spread_kernel, plan), [shape(8 * plan.setup, 128)], [coarse_inverse]
        )
    (early,) = call(
        functools.partial(gather_kernel, EARLY, 0), [shape(early_rows, 128)], [canon, load], specs=[smem, vm()]
    )
    (late,) = call(
        functools.partial(gather_kernel, LATE, SPLIT), [shape(late_rows, 128)], [canon, load], specs=[smem, vm()]
    )
    flops = 2 * ROWS * IFACE * IFACE
    middle_shape, square = shape(ROWS, IFACE, BF16), shape(ROWS, ROWS, BF16)

    (half,) = call(
        left_kernel,
        [middle_shape],
        [one, local_inverse[0, 0, 0], weight, basis],
        scratch=[pltpu.VMEM((16, IFACE), F32)],
        flops=flops,
    )
    inverse, half = call(
        right_left_kernel, [square, middle_shape], [one, half, schur_matrix[0, 0, 0]], flops=2 * flops
    )
    blocks = []
    if plan.ride:
        blocks = spread_out("initial", spread)
        payloads = first("initial", early, blocks, [turned])
    else:
        payloads = call(
            lambda base, *outs: write_payloads(plan.plain[0], outs, base, []),
            plan.payload_shapes("plain", 0),
            [early],
        )
    parts = [early, late]
    got = assemble("initial", parts, payloads, blocks, [turned])
    if plan.ride:
        (lift,) = call(
            functools.partial(lifting_kernel, plan),
            [shape(ROWS, 3 * plan.wide, BF16)],
            [turned] + blocks + got,
            scratch=[pltpu.VMEM((plan.wide, plan.wide), F32), pltpu.VMEM((ROWS, plan.wide), F32), pieces],
            flops=2 * ROWS * 3 * plan.wide * plan.wide,
        )
    (schur,) = call(right_kernel, [square], [one, half], flops=flops)
    sol = residual = None
    flops = 2 * ROWS * ROWS * 128
    for iteration in range(ITERS):
        opening = iteration == 0
        residual, rounded, restricted = call(
            functools.partial(residual_kernel, plan, opening, len(parts)),
            [shape(ROWS, 128), shape(ROWS, 128, BF16), shape(8, 128)],
            parts + got + [inverse, weight] + ([] if opening else [residual]),
            scratch=[acc],
        )
        if plan.ride:
            blocks = spread_out("update", restricted)
        (base,) = call(
            functools.partial(product_kernel, "all"), [shape(ROWS, 128)], [inverse, rounded], flops=flops
        )
        if plan.ride:
            payloads = first("update", base, blocks, [])
        else:
            blocks = []
            rows = lax.all_gather(restricted[:6], AXES, axis=0, tiled=True)
            correction = jnp.dot(coarse_inverse, rows, precision=lax.Precision.HIGHEST, preferred_element_type=F32)
            base, *payloads = call(
                functools.partial(lift_kernel, plan),
                [shape(ROWS, 128)] + plan.payload_shapes("plain", 0),
                [base, turned, jnp.pad(correction, ((0, 122), (0, 0)))],
            )
        got = assemble("update", [base], payloads, blocks, [], [lift] if opening and plan.ride else [])
        update, rounded, early, *payloads = call(
            functools.partial(update_kernel, plan),
            [shape(ROWS, 128), shape(ROWS, 128, BF16), shape(early_rows, 128)] + plan.payload_shapes("plain", 0),
            [base] + got + [schur] + ([lift] + blocks if plan.ride else []),
            scratch=[acc] + ([pltpu.VMEM((plan.wide, 128), F32)] if plan.ride else []),
            flops=flops,
        )
        late, sol = call(
            functools.partial(later_kernel, opening),
            [shape(late_rows, 128), shape(ROWS, 128)],
            [schur, rounded, update] + ([] if opening else [sol]),
            flops=flops // 2,
        )
        parts = [early, late]
        got = assemble("plain", parts, payloads, [], [])
    out = jax.ShapeDtypeStruct((IFACE, 1, loads), F32)
    (sol_out,) = call(scatter_kernel, [out], [canon, sol], specs=[smem, vm()])
    (residual_out,) = call(
        functools.partial(output_kernel, plan),
        [out],
        [canon] + parts + got + [residual],
        specs=[smem] + [vm()] * (3 + len(got)),
        scratch=[acc],
    )
    return tuple(o.reshape(1, 1, 1, IFACE, loads) for o in (sol_out, residual_out))


def solution(mesh):
    plan = Plan(tuple(mesh.shape[a] for a in AXES))
    in_specs = (
        P("gx", "gy", "gz", None, None),
        P("gx", "gy", "gz", None, None),
        P("gx", "gy", "gz", None, None),
        P("gx", "gy", "gz", None, None),
        P(("gx", "gy", "gz"), None),
        P("gx", "gy", "gz", None),
    )
    out_specs = (P("gx", "gy", "gz", None, None), P("gx", "gy", "gz", None, None))
    return jax.shard_map(
        functools.partial(local, plan), mesh=mesh, in_specs=in_specs, out_specs=out_specs, check_vma=False
    )
```

```python
import functools
import itertools

import jax
import jax.numpy as jnp
from jax import lax
from jax.experimental import pallas as pl
from jax.experimental.pallas import tpu as pltpu
from jax.sharding import PartitionSpec as P

NODES = 7
DOF = 3
ITERS = 3
AXES = ("gx", "gy", "gz")
STAGES = ((1,), (0, 2))
SPARE = (2, 1)
PAD = 8
CHUNK = 24
TILE = 256
BATCH = 16
F32 = jnp.float32
BF16 = jnp.bfloat16


def piece_length(placed):
    return DOF * NODES ** sum(1 for c in placed if c == 1)


PLACES = [p for p in itertools.product(range(3), repeat=3) if p != (1, 1, 1)]
CANON_OFFSET = {}
_at = 0
for _p in PLACES:
    CANON_OFFSET[_p] = _at
    _at += piece_length(_p)
IFACE = _at
LENGTH = {p: piece_length(p) for p in PLACES}
EARLY = [p for p in PLACES if p[1] != 1]
LATE = [p for p in PLACES if p[1] == 1]
SLOT_OFFSET = {}


def _lay(slots, at):
    for slot in slots:
        SLOT_OFFSET[slot] = at
        at += -(-LENGTH[slot] // PAD) * PAD
    return at


COARSE_AT = _lay(EARLY, 0)
SPLIT = -(-(COARSE_AT + 16) // 16) * 16
ROWS = -(-_lay(LATE, SPLIT) // TILE) * TILE
PARTS = {"all": (0, ROWS), "early": (0, SPLIT), "late": (SPLIT, ROWS)}


class Message:
    def __init__(self, moves, sizes, wrap, ride, spare):
        self.moves = moves
        self.sizes = sizes
        self.wrap = wrap
        self.ride = ride
        self.spare = spare
        self.faces = not any(m in ("C", "W") for m in moves)
        self.slots = []
        if self.faces:
            for place in EARLY + LATE:
                if all(m is None or c == (0 if m == "A" else 2) for m, c in zip(moves, place)):
                    self.slots.append(place)
        self.rows = -(-sum(LENGTH[s] for s in self.slots) // PAD) * PAD
        self.basis = []

    def xor(self):
        code = 0
        for move, size in zip(self.moves, self.sizes):
            code = code * size + {None: 0, "A": 1, "B": 3, "C": 2, "W": 3}[move]
        return code

    def pairs(self):
        out = []
        for place in itertools.product(*(range(s) for s in self.sizes)):
            to, whole = [], True
            for at, move, size in zip(place, self.moves, self.sizes):
                if move == "A":
                    at = at ^ 1
                elif move == "B":
                    whole = whole and (self.wrap or 0 < at < size - 1)
                    at = (at - 1) % size if at % 2 == 0 else (at + 1) % size
                elif move == "C":
                    at = at ^ 2
                elif move == "W":
                    at = at ^ 3
                to.append(at)
            if not whole:
                to = [at ^ 1 if d == self.spare else at for d, at in enumerate(place)]
            flat = [0, 0]
            for a, b, size in zip(place, to, self.sizes):
                flat = [flat[0] * size + a, flat[1] * size + b]
            out.append(tuple(flat))
        return out


def stage_messages(stage, sizes, coarse=None):
    choices = []
    for d in range(3):
        if d not in STAGES[stage]:
            choices.append((None,))
        else:
            extra = ("C", "W") if coarse == "update" and stage == 0 and sizes[d] == 4 else ()
            choices.append((None, "A") + (("B",) if sizes[d] > 2 else ()) + extra)
    out = []
    for moves in itertools.product(*choices):
        if all(m is None for m in moves):
            continue
        ride = coarse and (moves[1] != "B" if stage == 0 else moves[2] != "A")
        out.append(Message(moves, sizes, ride and stage == 1, ride, SPARE[stage]))
    return out


class Plan:
    def __init__(self, sizes):
        self.sizes = sizes
        self.subs = sizes[0] * sizes[1] * sizes[2]
        self.ride = all(s in (2, 4) for s in sizes)
        self.wide = self.subs * 8
        self.plain = [stage_messages(i, sizes) for i in range(2)]
        self.setup = 0
        if self.ride:
            self.setup = self.wide // 128
            self.coarse = {k: [stage_messages(i, sizes, k) for i in range(2)] for k in ("initial", "update")}
            self.before = {"update": [Message((None, None, "A"), sizes, False, True, 0)]}
            self.before["initial"] = list(self.before["update"])
            if sizes[1] == 4:
                more = [(None, "C", None), (None, "C", "A")]
                self.before["initial"] += [Message(m, sizes, False, True, 0) for m in more]
            first, second = self.coarse["initial"]
            for message in first:
                message.basis = [(None, slot) for slot in message.slots]
            for message in second:
                message.basis = [(None, slot) for slot in message.slots]
                for other in first:
                    message.basis += [(other, slot) for slot in message.slots if slot in other.slots]

    def per(self, kind):
        return {"plain": 0, "update": 1, "initial": self.setup}[kind] if self.ride else 0

    def messages(self, kind):
        return self.plain if self.per(kind) == 0 else self.coarse[kind]

    def codes(self, kind, stage):
        known = [0] + [m.xor() for m in self.before[kind]]
        if stage == 1:
            known = [k ^ m for m in [0] + [m.xor() for m in self.coarse[kind][0] if m.ride] for k in known]
        return known

    def payload_shapes(self, kind, stage):
        per = self.per(kind)
        out = []
        for m in self.messages(kind)[stage]:
            rows = m.rows
            if m.ride:
                rows += 8 * per * len(self.codes(kind, stage))
            if kind == "initial" and self.ride and m.faces:
                rows += CHUNK
            out.append(shape(rows, 128))
        return out


def position():
    return [lax.axis_index(a) for a in AXES]


def has_b(index, size):
    return jnp.logical_and(index > 0, index < size - 1)


def exists(plan, index, message):
    ok = None
    for d, move in enumerate(message.moves):
        if move == "B":
            here = has_b(index[d], plan.sizes[d])
            ok = here if ok is None else jnp.logical_and(ok, here)
    return ok


def both(a, b):
    return b if a is None else a if b is None else jnp.logical_and(a, b)


def pick(slot, index, of):
    def choose(d, place):
        if d == 3:
            return of(tuple(place))
        if slot[d] == 1:
            return choose(d + 1, place + [1])
        even, odd = (2, 0) if slot[d] == 0 else (0, 2)
        return jnp.where(index[d] % 2 == 0, choose(d + 1, place + [even]), choose(d + 1, place + [odd]))

    return choose(0, [])


def add_received(plan, index, messages, received, acc):
    for message, ref in zip(messages, received):
        if not message.faces:
            continue
        ok = exists(plan, index, message)
        at = 0
        for slot in message.slots:
            rows, to = LENGTH[slot], SLOT_OFFSET[slot]
            value = ref[at : at + rows, :]
            if ok is not None:
                value = jnp.where(ok, value, 0.0)
            acc[to : to + rows, :] += value
            at += rows


def write_payloads(messages, outs, acc, blocks, pack=None):
    for message, out in zip(messages, outs):
        at = 0
        for slot in message.slots:
            rows, frm = LENGTH[slot], SLOT_OFFSET[slot]
            out[at : at + rows, :] = acc[frm : frm + rows, :]
            at += rows
        at = message.rows
        if message.ride:
            for block in blocks:
                out[at : at + 8, :] = block
                at += 8
        if pack is not None and message.faces:
            out[at : at + CHUNK, :] = pack(message)


def packer(own, stage, unpacked):
    def pack(message):
        at = 0
        for source, slot in message.basis:
            rows = LENGTH[slot]
            if source is not None:
                ref = unpacked[source]
                frm = sum(LENGTH[s] for s in source.slots[: source.slots.index(slot)])
            else:
                ref, frm = own, SLOT_OFFSET[slot]
            stage[at : at + rows, :] = ref[frm : frm + rows, :]
            at += rows
        count = -(-at // CHUNK)
        if at < count * CHUNK:
            stage[at : count * CHUNK, :] = jnp.zeros((count * CHUNK - at, 128), F32)
        total = stage[0:CHUNK, :]
        for k in range(1, count):
            total += pltpu.roll(stage[k * CHUNK : (k + 1) * CHUNK, :], 8 * k, 1)
        return total

    return pack


def unpack(message, block, out):
    count = -(-sum(LENGTH[slot] for _, slot in message.basis) // CHUNK)
    lane = lax.broadcasted_iota(jnp.int32, (CHUNK, 128), 1)
    for k in range(count):
        turned = pltpu.roll(block, 128 - 8 * k, 1) if k else block
        out[k * CHUNK : (k + 1) * CHUNK, :] = jnp.where(lane < 8, turned, 0.0)


def transfer(messages, payloads):
    return [lax.ppermute(p, AXES, m.pairs()) for m, p in zip(messages, payloads)]


def vm():
    return pl.BlockSpec(memory_space=pltpu.VMEM)


def shape(rows, cols, dtype=F32):
    return jax.ShapeDtypeStruct((rows, cols), dtype)


def call(kernel, outs, operands, specs=None, scratch=(), limit=20, flops=0):
    nbytes = sum(o.size * o.dtype.itemsize for o in list(outs) + list(operands))
    return pl.pallas_call(
        kernel,
        out_shape=tuple(outs),
        in_specs=specs or [vm()] * len(operands),
        out_specs=tuple(vm() for _ in outs),
        scratch_shapes=list(scratch),
        compiler_params=pltpu.CompilerParams(vmem_limit_bytes=limit << 20),
        cost_estimate=pl.CostEstimate(flops=flops, bytes_accessed=nbytes, transcendentals=0),
    )(*operands)


def gather_kernel(slots, start, canon, load, acc):
    index = position()
    acc[...] = jnp.zeros(acc.shape, F32)
    for slot in slots:
        length, at = LENGTH[slot], SLOT_OFFSET[slot] - start
        off = pick(slot, index, lambda place: jnp.int32(CANON_OFFSET[place]))
        for first in range(0, length, BATCH):
            batch = range(first, min(first + BATCH, length))
            values = [load[canon[0, off + row], :, :] for row in batch]
            for row, value in zip(batch, values):
                acc[at + row : at + row + 1, :] = value


def scatter_rows(index, canon, acc, out):
    for slot in PLACES:
        length, at = LENGTH[slot], SLOT_OFFSET[slot]
        off = pick(slot, index, lambda place: jnp.int32(CANON_OFFSET[place]))
        for first in range(0, length, BATCH):
            batch = range(first, min(first + BATCH, length))
            values = [acc[at + row : at + row + 1, :] for row in batch]
            places = [canon[0, off + row] for row in batch]
            for to, value in zip(places, values):
                out[to, :, :] = value


def scatter_kernel(canon, acc, out):
    scatter_rows(position(), canon, acc, out)


def split(value, parts):
    out = []
    for _ in range(parts):
        piece = value.astype(BF16)
        out.append(piece)
        value = value - piece.astype(F32)
    return out


def dot(a, b):
    return jnp.dot(a, b, preferred_element_type=F32)


def dot_last(a, b):
    return lax.dot_general(a, b, (((1,), (1,)), ((), ())), preferred_element_type=F32)


def tile(t):
    return pl.ds(pl.multiple_of(t * TILE, TILE), TILE)


def each_tile(body):
    def step(t, _):
        body(tile(t))
        return 0

    lax.fori_loop(0, ROWS // TILE, step, 0)


def select_kernel(plan, canon, one, weight_out, src):
    index = position()
    src[...] = jnp.full(src.shape, -1, jnp.int32)
    weight_out[...] = jnp.zeros(weight_out.shape, F32)
    for slot in PLACES:
        at, length = SLOT_OFFSET[slot], LENGTH[slot]
        src[at : at + length, :] = pick(
            slot, index, lambda place, length=length: canon[CANON_OFFSET[place] : CANON_OFFSET[place] + length, :]
        )
        weight = jnp.float32(1.0)
        for d in range(3):
            if slot[d] == 0:
                weight = weight * 0.5
            elif slot[d] == 2 and plan.sizes[d] > 2:
                weight = weight * jnp.where(has_b(index[d], plan.sizes[d]), 0.5, 1.0)
        weight_out[at : at + length, :] = jnp.full((length, 128), 1.0, F32) * weight

    for t in range(0, ROWS, TILE):
        rows = slice(t, t + TILE)
        hit = src[rows, :] == lax.broadcasted_iota(jnp.int32, (TILE, IFACE), 1)
        one[rows, :] = jnp.where(hit, 1.0, 0.0).astype(BF16)


def spread_kernel(plan, cinv, out):
    nc = cinv.shape[1]
    row = lax.broadcasted_iota(jnp.int32, (nc, plan.wide), 0)
    col = lax.broadcasted_iota(jnp.int32, (nc, plan.wide), 1)
    spread = jnp.where(jnp.logical_and((col >> 3) * 6 + (col & 7) == row, (col & 7) < 6), 1.0, 0.0).astype(BF16)
    value = sum(dot(part, spread) for part in split(cinv[...], 3))
    out[...] = jnp.zeros(out.shape, F32)
    for i in range(plan.setup):
        out[8 * i : 8 * i + 6, :] = value[:, 128 * i : 128 * (i + 1)]


def turn_kernel(one, weight, basis, turned):
    turned[...] = jnp.zeros(turned.shape, F32)
    turned[:, :6] = dot_last(one[...], basis[...]) * weight[:, :6]


def left_kernel(one, matrix, basis, mid, few):
    for t in range(0, ROWS, TILE):
        mid[t : t + TILE, :] = dot(one[t : t + TILE, :], matrix[...]).astype(BF16)
    if basis is not None:
        few[...] = jnp.zeros(few.shape, F32)
        few[:6, :] = basis[...].astype(F32)
        mid[COARSE_AT : COARSE_AT + 16, :] = few[...].astype(BF16)


def right_left_kernel(one, mid, weight, other, out, mid_other):
    right(one, mid, weight, out)
    left_kernel(one, other, None, mid_other, None)


def right_kernel(one, mid, out):
    right(one, mid, None, out)


def right(one, mid, weight, out):
    order = sorted(range(ROWS // TILE), key=lambda t: (t != COARSE_AT // TILE, t))

    def put(value, i, j):
        if weight is not None:
            scale = weight[i * TILE : (i + 1) * TILE, :1]
            if i == order[0]:
                row = lax.broadcasted_iota(jnp.int32, (TILE, 1), 0) + i * TILE
                inside = jnp.logical_and(row >= COARSE_AT, row < COARSE_AT + 16)
                scale = jnp.where(inside, 1.0, scale)
            value = value * scale
        out[i * TILE : (i + 1) * TILE, j * TILE : (j + 1) * TILE] = value.astype(BF16)

    for a, i in enumerate(order):
        for j in order[a:]:
            value = dot_last(mid[i * TILE : (i + 1) * TILE, :], one[j * TILE : (j + 1) * TILE, :])
            put(value, i, j)
            if i != j:
                put(value.T, j, i)


def fill(acc, parts):
    at = 0
    for part in parts:
        acc[at : at + part.shape[0], :] = part[...]
        at += part.shape[0]


def known_blocks(plan, kind, own, swapped, arrived, per):
    blocks = own + [ref[8 * i : 8 * (i + 1), :] for ref in swapped for i in range(per)]
    count = len(blocks)
    for message, ref in zip(plan.coarse[kind][0], arrived):
        if message.ride:
            blocks += [ref[message.rows + 8 * i : message.rows + 8 * (i + 1), :] for i in range(count)]
    return blocks


def first_kernel(plan, kind, *refs):
    refs = list(refs)
    base, own = refs.pop(0), refs.pop(0)
    swapped = [refs.pop(0) for _ in plan.before[kind]]
    per = plan.per(kind)
    pack = None
    if kind == "initial":
        turned = refs.pop(0)
        pack = packer(turned, refs.pop(-1), {})
    mine = [own[8 * i : 8 * (i + 1), :] for i in range(per)]
    write_payloads(plan.coarse[kind][0], refs, base, known_blocks(plan, kind, mine, swapped, [], per), pack)


def middle_kernel(plan, kind, count, after, *refs):
    first, second = plan.messages(kind)
    per = plan.per(kind)
    refs = list(refs)
    parts = [refs.pop(0) for _ in range(count)]
    if after:
        refs.pop(0)
    received = [refs.pop(0) for _ in first]
    blocks, pack = [], None
    if per:
        own = refs.pop(0)
        swapped = [refs.pop(0) for _ in plan.before[kind]]
        mine = [own[8 * i : 8 * (i + 1), :] for i in range(per)]
        blocks = known_blocks(plan, kind, mine, swapped, received, per)
    if per and kind == "initial":
        turned = refs.pop(0)
        stage = refs.pop(-1)
        kept = {m: refs.pop(-1) for m in reversed(first) if m.faces}
        for message, ref in zip(first, received):
            if message.faces:
                unpack(message, ref[ref.shape[0] - CHUNK :, :], kept[message])
        pack = packer(turned, stage, kept)
    acc = refs.pop(-1)
    fill(acc, parts)
    add_received(plan, position(), first, received, acc)
    write_payloads(second, refs, acc, blocks, pack)


def product_kernel(part, matrix, vector, out):
    start, stop = PARTS[part]
    size = (stop - start) // (4 if part == "all" else 2)
    for t in range(start, stop, size):
        out[t - start : t - start + size, :] = dot(matrix[t : t + size, :], vector[...])


def finish(plan, kind, parts, got, acc):
    first, second = plan.messages(kind)
    index = position()
    fill(acc, parts)
    add_received(plan, index, first, got[: len(first)], acc)
    add_received(plan, index, second, got[len(first) :], acc)


def residual_kernel(plan, opening, count, *refs):
    kind = "initial" if opening else "plain"
    refs = list(refs)
    parts = [refs.pop(0) for _ in range(count)]
    got = [refs.pop(0) for _ in range(sum(len(m) for m in plan.messages(kind)))]
    matrix, weight = refs.pop(0), refs.pop(0)
    before = None if opening else refs.pop(0)
    residual, rounded, restricted, acc = refs
    finish(plan, kind, parts, got, acc)
    value = acc[...] if opening else before[...] - acc[...]
    residual[...] = value
    rounded[...] = (weight[...] * value).astype(BF16)
    restricted[...] = dot(matrix[COARSE_AT : COARSE_AT + 16, :], rounded[...])[:8]


def lift_kernel(plan, base, turned, correction, out, *outs):
    lifted = turned[...].astype(BF16)
    out[...] = base[...] + sum(dot(lifted, part) for part in split(correction[...], 3))
    write_payloads(plan.plain[0], outs, out, [])


def collect(plan, kind, own, got, per, which, stack, at_column):
    first, second = plan.coarse[kind]
    index = position()
    me = (index[0] * plan.sizes[1] + index[1]) * plan.sizes[2] + index[2]

    def put(code, value):
        stack[pl.ds(pl.multiple_of((me ^ code) * 8, 8), 8), at_column : at_column + 128] = value

    put(0, own[8 * which : 8 * (which + 1), :])
    for m in plan.before[kind]:
        put(m.xor(), got[0][8 * which : 8 * (which + 1), :])
        got = got[1:]
    for stage, messages in enumerate((first, second)):
        for m, ref in zip(messages, got):
            if m.ride:
                for i, code in enumerate(plan.codes(kind, stage)):
                    at = m.rows + 8 * (per * i + which)
                    put(code ^ m.xor(), ref[at : at + 8, :])
        got = got[len(messages) :]


def lifting_kernel(plan, *refs):
    first, second = plan.coarse["initial"]
    turned, spread, *got, out, stack, many, unpacked = refs
    swapped, got = got[: len(plan.before["initial"])], got[len(plan.before["initial"]) :]
    per = plan.setup
    index = position()
    me = (index[0] * plan.sizes[1] + index[1]) * plan.sizes[2] + index[2]

    def place(code, value, to, ok):
        there = me ^ code
        value = pltpu.roll(value, (there & 15) * 8, 1)
        rows = value.shape[0]
        for half in range(per):
            here = both((there >> 4) == half, ok)
            many[to : to + rows, 128 * half : 128 * (half + 1)] += jnp.where(here, value, 0.0)

    many[...] = jnp.zeros(many.shape, F32)
    for t in range(ROWS // TILE):
        place(0, turned[t * TILE : (t + 1) * TILE, :], t * TILE, None)
    for m, ref in zip(first + second, got):
        if not m.faces:
            continue
        unpack(m, ref[ref.shape[0] - CHUNK :, :], unpacked)
        at, ok = 0, exists(plan, index, m)
        for source, slot in m.basis:
            code, fine = m.xor(), ok
            if source is not None:
                code ^= source.xor()
                fine = both(exists(plan, index, source), ok)
            place(code, unpacked[at : at + LENGTH[slot], :], SLOT_OFFSET[slot], fine)
            at += LENGTH[slot]
    for half in range(per):
        collect(plan, "initial", spread, swapped + got, per, half, stack, 128 * half)
    parts = jnp.concatenate(split(stack[...], 3), axis=0)

    def body(rows):
        basis = many[rows, :].astype(BF16)
        whole = dot(jnp.concatenate([basis] * 3, axis=1), parts)
        high, low = split(whole, 2)
        out[rows, :] = jnp.concatenate([high, high, low], axis=1)

    each_tile(body)


def update_kernel(plan, *refs):
    refs = list(refs)
    base = refs.pop(0)
    got = [refs.pop(0) for _ in range(sum(len(m) for m in plan.messages("update")))]
    matrix = refs.pop(0)
    if plan.ride:
        lift, own = refs.pop(0), refs.pop(0)
        swapped = [refs.pop(0) for _ in plan.before["update"]]
        stack = refs.pop(-1)
    acc = refs.pop(-1)
    update, rounded, early, *outs = refs
    finish(plan, "update", [base], got, acc)
    if plan.ride:
        collect(plan, "update", own, swapped + got, 1, 0, stack, 0)
        high, low = split(stack[...], 2)
        right = jnp.concatenate([high, low, high], axis=0)
        for t in range(0, ROWS, 320):
            value = acc[t : t + 320, :] + dot(lift[t : t + 320, :], right)
            update[t : t + 320, :] = value
            rounded[t : t + 320, :] = value.astype(BF16)
    else:
        update[...] = acc[...]
        rounded[...] = acc[...].astype(BF16)
    product_kernel("early", matrix, rounded, early)
    write_payloads(plan.plain[0], outs, early, [])


def later_kernel(opening, matrix, rounded, update, *refs):
    late, total = refs[-2:]
    product_kernel("late", matrix, rounded, late)
    total[...] = update[...] if opening else refs[0][...] + update[...]


def output_kernel(plan, canon, early, late, *refs):
    *got, residual, out, acc = refs
    finish(plan, "plain", [early, late], got, acc)
    acc[...] = residual[...] - acc[...]
    scatter_rows(position(), canon, acc, out)


def local(plan, load_cases, schur_matrix, local_inverse, coarse_basis, coarse_inverse, canon_rows):
    smem = pl.BlockSpec(memory_space=pltpu.SMEM)
    loads = load_cases.shape[-1]
    canon = canon_rows.reshape(1, IFACE)
    load = load_cases.reshape(IFACE, 1, loads)
    basis = coarse_basis[0, 0, 0]
    acc = pltpu.VMEM((ROWS, 128), F32)
    pieces = pltpu.VMEM((16 * CHUNK, 128), F32)
    early_rows, late_rows = SPLIT, ROWS - SPLIT

    def spread_out(kind, own):
        return [own] + transfer(plan.before[kind], [own] * len(plan.before[kind]))

    def first(kind, base, blocks, more):
        return call(
            functools.partial(first_kernel, plan, kind),
            plan.payload_shapes(kind, 0),
            [base] + blocks + more,
            scratch=[pieces] if kind == "initial" else [],
        )

    def assemble(kind, parts, payloads, blocks, more, after=()):
        messages = plan.messages(kind)
        got = transfer(messages[0], payloads)
        setup = kind == "initial" and plan.ride
        payloads = call(
            functools.partial(middle_kernel, plan, kind, len(parts), bool(after)),
            plan.payload_shapes(kind, 1),
            parts + list(after) + got + blocks + (more if setup else []),
            scratch=[acc] + ([pieces] * (1 + sum(m.faces for m in messages[0])) if setup else []),
        )
        return got + transfer(messages[1], payloads)

    one, weight = call(
        functools.partial(select_kernel, plan),
        [shape(ROWS, IFACE, BF16), shape(ROWS, 128)],
        [canon_rows.reshape(IFACE, 1)],
        scratch=[pltpu.VMEM((ROWS, 1), jnp.int32)],
        flops=ROWS * IFACE * 1158,
    )
    if plan.ride:
        (spread,) = call(
            functools.partial(spread_kernel, plan), [shape(8 * plan.setup, 128)], [coarse_inverse]
        )
    (turned,) = call(turn_kernel, [shape(ROWS, 128)], [one, weight, basis])
    (early,) = call(
        functools.partial(gather_kernel, EARLY, 0), [shape(early_rows, 128)], [canon, load], specs=[smem, vm()]
    )
    (late,) = call(
        functools.partial(gather_kernel, LATE, SPLIT), [shape(late_rows, 128)], [canon, load], specs=[smem, vm()]
    )
    flops = 2 * ROWS * IFACE * IFACE
    middle_shape, square = shape(ROWS, IFACE, BF16), shape(ROWS, ROWS, BF16)

    (half,) = call(
        left_kernel,
        [middle_shape],
        [one, local_inverse[0, 0, 0], basis],
        scratch=[pltpu.VMEM((16, IFACE), F32)],
        flops=flops,
    )
    inverse, half = call(
        right_left_kernel, [square, middle_shape], [one, half, weight, schur_matrix[0, 0, 0]], flops=2 * flops
    )
    blocks = []
    if plan.ride:
        blocks = spread_out("initial", spread)
        payloads = first("initial", early, blocks, [turned])
    else:
        payloads = call(
            lambda base, *outs: write_payloads(plan.plain[0], outs, base, []),
            plan.payload_shapes("plain", 0),
            [early],
        )
    parts = [early, late]
    got = assemble("initial", parts, payloads, blocks, [turned])
    if plan.ride:
        (lift,) = call(
            functools.partial(lifting_kernel, plan),
            [shape(ROWS, 3 * plan.wide, BF16)],
            [turned] + blocks + got,
            scratch=[pltpu.VMEM((plan.wide, plan.wide), F32), pltpu.VMEM((ROWS, plan.wide), F32), pieces],
            flops=2 * ROWS * 3 * plan.wide * plan.wide,
        )
    (schur,) = call(right_kernel, [square], [one, half], flops=flops)
    sol = residual = None
    flops = 2 * ROWS * ROWS * 128
    for iteration in range(ITERS):
        opening = iteration == 0
        residual, rounded, restricted = call(
            functools.partial(residual_kernel, plan, opening, len(parts)),
            [shape(ROWS, 128), shape(ROWS, 128, BF16), shape(8, 128)],
            parts + got + [inverse, weight] + ([] if opening else [residual]),
            scratch=[acc],
        )
        if plan.ride:
            blocks = spread_out("update", restricted)
        (base,) = call(
            functools.partial(product_kernel, "all"), [shape(ROWS, 128)], [inverse, rounded], flops=flops
        )
        if plan.ride:
            payloads = first("update", base, blocks, [])
        else:
            blocks = []
            rows = lax.all_gather(restricted[:6], AXES, axis=0, tiled=True)
            correction = jnp.dot(coarse_inverse, rows, precision=lax.Precision.HIGHEST, preferred_element_type=F32)
            base, *payloads = call(
                functools.partial(lift_kernel, plan),
                [shape(ROWS, 128)] + plan.payload_shapes("plain", 0),
                [base, turned, jnp.pad(correction, ((0, 122), (0, 0)))],
            )
        got = assemble("update", [base], payloads, blocks, [], [lift] if opening and plan.ride else [])
        update, rounded, early, *payloads = call(
            functools.partial(update_kernel, plan),
            [shape(ROWS, 128), shape(ROWS, 128, BF16), shape(early_rows, 128)] + plan.payload_shapes("plain", 0),
            [base] + got + [schur] + ([lift] + blocks if plan.ride else []),
            scratch=[acc] + ([pltpu.VMEM((plan.wide, 128), F32)] if plan.ride else []),
            flops=flops,
        )
        late, sol = call(
            functools.partial(later_kernel, opening),
            [shape(late_rows, 128), shape(ROWS, 128)],
            [schur, rounded, update] + ([] if opening else [sol]),
            flops=flops // 2,
        )
        parts = [early, late]
        got = assemble("plain", parts, payloads, [], [])
    out = jax.ShapeDtypeStruct((IFACE, 1, loads), F32)
    (sol_out,) = call(scatter_kernel, [out], [canon, sol], specs=[smem, vm()])
    (residual_out,) = call(
        functools.partial(output_kernel, plan),
        [out],
        [canon] + parts + got + [residual],
        specs=[smem] + [vm()] * (3 + len(got)),
        scratch=[acc],
    )
    return tuple(o.reshape(1, 1, 1, IFACE, loads) for o in (sol_out, residual_out))


def solution(mesh):
    plan = Plan(tuple(mesh.shape[a] for a in AXES))
    in_specs = (
        P("gx", "gy", "gz", None, None),
        P("gx", "gy", "gz", None, None),
        P("gx", "gy", "gz", None, None),
        P("gx", "gy", "gz", None, None),
        P(("gx", "gy", "gz"), None),
        P("gx", "gy", "gz", None),
    )
    out_specs = (P("gx", "gy", "gz", None, None), P("gx", "gy", "gz", None, None))
    return jax.shard_map(
        functools.partial(local, plan), mesh=mesh, in_specs=in_specs, out_specs=out_specs, check_vma=False
    )
```

```python
import functools
import itertools

import jax
import jax.numpy as jnp
from jax import lax
from jax.experimental import pallas as pl
from jax.experimental.pallas import tpu as pltpu
from jax.sharding import PartitionSpec as P

NODES = 7
DOF = 3
ITERS = 3
AXES = ("gx", "gy", "gz")
STAGES = ((1,), (0, 2))
SPARE = (2, 1)
PAD = 8
CHUNK = 24
TILE = 256
BATCH = 16
F32 = jnp.float32
BF16 = jnp.bfloat16


def piece_length(placed):
    return DOF * NODES ** sum(1 for c in placed if c == 1)


PLACES = [p for p in itertools.product(range(3), repeat=3) if p != (1, 1, 1)]
CANON_OFFSET = {}
_at = 0
for _p in PLACES:
    CANON_OFFSET[_p] = _at
    _at += piece_length(_p)
IFACE = _at
LENGTH = {p: piece_length(p) for p in PLACES}
EARLY = [p for p in PLACES if p[1] != 1]
LATE = [p for p in PLACES if p[1] == 1]
SLOT_OFFSET = {}


def _lay(slots, at):
    for slot in slots:
        SLOT_OFFSET[slot] = at
        at += -(-LENGTH[slot] // PAD) * PAD
    return at


COARSE_AT = _lay(EARLY, 0)
SPLIT = -(-(COARSE_AT + 16) // 16) * 16
ROWS = -(-_lay(LATE, SPLIT) // TILE) * TILE
TILES = ROWS // TILE
CUT_INVERSE = 3
CUT_SCHUR = 2
PARTS = {"all": (0, ROWS), "early": (0, SPLIT), "late": (SPLIT, ROWS)}


class Message:
    def __init__(self, moves, sizes, wrap, ride, spare):
        self.moves = moves
        self.sizes = sizes
        self.wrap = wrap
        self.ride = ride
        self.spare = spare
        self.faces = not any(m in ("C", "W") for m in moves)
        self.slots = []
        if self.faces:
            for place in EARLY + LATE:
                if all(m is None or c == (0 if m == "A" else 2) for m, c in zip(moves, place)):
                    self.slots.append(place)
        self.rows = -(-sum(LENGTH[s] for s in self.slots) // PAD) * PAD
        self.basis = []

    def xor(self):
        code = 0
        for move, size in zip(self.moves, self.sizes):
            code = code * size + {None: 0, "A": 1, "B": 3, "C": 2, "W": 3}[move]
        return code

    def pairs(self):
        out = []
        for place in itertools.product(*(range(s) for s in self.sizes)):
            to, whole = [], True
            for at, move, size in zip(place, self.moves, self.sizes):
                if move == "A":
                    at = at ^ 1
                elif move == "B":
                    whole = whole and (self.wrap or 0 < at < size - 1)
                    at = (at - 1) % size if at % 2 == 0 else (at + 1) % size
                elif move == "C":
                    at = at ^ 2
                elif move == "W":
                    at = at ^ 3
                to.append(at)
            if not whole:
                to = [at ^ 1 if d == self.spare else at for d, at in enumerate(place)]
            flat = [0, 0]
            for a, b, size in zip(place, to, self.sizes):
                flat = [flat[0] * size + a, flat[1] * size + b]
            out.append(tuple(flat))
        return out


def stage_messages(stage, sizes, coarse=None):
    choices = []
    for d in range(3):
        if d not in STAGES[stage]:
            choices.append((None,))
        else:
            extra = ("C", "W") if coarse == "update" and stage == 0 and sizes[d] == 4 else ()
            choices.append((None, "A") + (("B",) if sizes[d] > 2 else ()) + extra)
    out = []
    for moves in itertools.product(*choices):
        if all(m is None for m in moves):
            continue
        ride = coarse and (moves[1] != "B" if stage == 0 else moves[2] != "A")
        out.append(Message(moves, sizes, ride and stage == 1, ride, SPARE[stage]))
    return out


class Plan:
    def __init__(self, sizes):
        self.sizes = sizes
        self.subs = sizes[0] * sizes[1] * sizes[2]
        self.ride = all(s in (2, 4) for s in sizes)
        self.wide = self.subs * 8
        self.plain = [stage_messages(i, sizes) for i in range(2)]
        self.setup = 0
        if self.ride:
            self.setup = self.wide // 128
            self.coarse = {k: [stage_messages(i, sizes, k) for i in range(2)] for k in ("initial", "update")}
            self.before = {"update": [Message((None, None, "A"), sizes, False, True, 0)]}
            self.before["initial"] = list(self.before["update"])
            if sizes[1] == 4:
                more = [(None, "C", None), (None, "C", "A")]
                self.before["initial"] += [Message(m, sizes, False, True, 0) for m in more]
            first, second = self.coarse["initial"]
            for message in first:
                message.basis = [(None, slot) for slot in message.slots]
            for message in second:
                message.basis = [(None, slot) for slot in message.slots]
                for other in first:
                    message.basis += [(other, slot) for slot in message.slots if slot in other.slots]

    def per(self, kind):
        return {"plain": 0, "update": 1, "initial": self.setup}[kind] if self.ride else 0

    def messages(self, kind):
        return self.plain if self.per(kind) == 0 else self.coarse[kind]

    def codes(self, kind, stage):
        known = [0] + [m.xor() for m in self.before[kind]]
        if stage == 1:
            known = [k ^ m for m in [0] + [m.xor() for m in self.coarse[kind][0] if m.ride] for k in known]
        return known

    def payload_shapes(self, kind, stage):
        per = self.per(kind)
        out = []
        for m in self.messages(kind)[stage]:
            rows = m.rows
            if m.ride:
                rows += 8 * per * len(self.codes(kind, stage))
            if kind == "initial" and self.ride and m.faces:
                rows += CHUNK
            out.append(shape(rows, 128))
        return out


def position():
    return [lax.axis_index(a) for a in AXES]


def has_b(index, size):
    return jnp.logical_and(index > 0, index < size - 1)


def exists(plan, index, message):
    ok = None
    for d, move in enumerate(message.moves):
        if move == "B":
            here = has_b(index[d], plan.sizes[d])
            ok = here if ok is None else jnp.logical_and(ok, here)
    return ok


def both(a, b):
    return b if a is None else a if b is None else jnp.logical_and(a, b)


def pick(slot, index, of):
    def choose(d, place):
        if d == 3:
            return of(tuple(place))
        if slot[d] == 1:
            return choose(d + 1, place + [1])
        even, odd = (2, 0) if slot[d] == 0 else (0, 2)
        return jnp.where(index[d] % 2 == 0, choose(d + 1, place + [even]), choose(d + 1, place + [odd]))

    return choose(0, [])


def add_received(plan, index, messages, received, acc):
    for message, ref in zip(messages, received):
        if not message.faces:
            continue
        ok = exists(plan, index, message)
        at = 0
        for slot in message.slots:
            rows, to = LENGTH[slot], SLOT_OFFSET[slot]
            value = ref[at : at + rows, :]
            if ok is not None:
                value = jnp.where(ok, value, 0.0)
            acc[to : to + rows, :] += value
            at += rows


def write_payloads(messages, outs, acc, blocks, pack=None):
    for message, out in zip(messages, outs):
        at = 0
        for slot in message.slots:
            rows, frm = LENGTH[slot], SLOT_OFFSET[slot]
            out[at : at + rows, :] = acc[frm : frm + rows, :]
            at += rows
        at = message.rows
        if message.ride:
            for block in blocks:
                out[at : at + 8, :] = block
                at += 8
        if pack is not None and message.faces:
            out[at : at + CHUNK, :] = pack(message)


def packer(own, stage, unpacked):
    def pack(message):
        at = 0
        for source, slot in message.basis:
            rows = LENGTH[slot]
            if source is not None:
                ref = unpacked[source]
                frm = sum(LENGTH[s] for s in source.slots[: source.slots.index(slot)])
            else:
                ref, frm = own, SLOT_OFFSET[slot]
            stage[at : at + rows, :] = ref[frm : frm + rows, :]
            at += rows
        count = -(-at // CHUNK)
        if at < count * CHUNK:
            stage[at : count * CHUNK, :] = jnp.zeros((count * CHUNK - at, 128), F32)
        total = stage[0:CHUNK, :]
        for k in range(1, count):
            total += pltpu.roll(stage[k * CHUNK : (k + 1) * CHUNK, :], 8 * k, 1)
        return total

    return pack


def unpack(message, block, out):
    count = -(-sum(LENGTH[slot] for _, slot in message.basis) // CHUNK)
    lane = lax.broadcasted_iota(jnp.int32, (CHUNK, 128), 1)
    for k in range(count):
        turned = pltpu.roll(block, 128 - 8 * k, 1) if k else block
        out[k * CHUNK : (k + 1) * CHUNK, :] = jnp.where(lane < 8, turned, 0.0)


def transfer(messages, payloads):
    return [lax.ppermute(p, AXES, m.pairs()) for m, p in zip(messages, payloads)]


def vm():
    return pl.BlockSpec(memory_space=pltpu.VMEM)


def shape(rows, cols, dtype=F32):
    return jax.ShapeDtypeStruct((rows, cols), dtype)


def call(kernel, outs, operands, specs=None, scratch=(), limit=20, flops=0):
    nbytes = sum(o.size * o.dtype.itemsize for o in list(outs) + list(operands))
    return pl.pallas_call(
        kernel,
        out_shape=tuple(outs),
        in_specs=specs or [vm()] * len(operands),
        out_specs=tuple(vm() for _ in outs),
        scratch_shapes=list(scratch),
        compiler_params=pltpu.CompilerParams(vmem_limit_bytes=limit << 20),
        cost_estimate=pl.CostEstimate(flops=flops, bytes_accessed=nbytes, transcendentals=0),
    )(*operands)


def gather_kernel(slots, start, canon, load, acc):
    index = position()
    acc[...] = jnp.zeros(acc.shape, F32)
    for slot in slots:
        length, at = LENGTH[slot], SLOT_OFFSET[slot] - start
        off = pick(slot, index, lambda place: jnp.int32(CANON_OFFSET[place]))
        for first in range(0, length, BATCH):
            batch = range(first, min(first + BATCH, length))
            values = [load[canon[0, off + row], :, :] for row in batch]
            for row, value in zip(batch, values):
                acc[at + row : at + row + 1, :] = value


def scatter_rows(index, canon, acc, out):
    for slot in PLACES:
        length, at = LENGTH[slot], SLOT_OFFSET[slot]
        off = pick(slot, index, lambda place: jnp.int32(CANON_OFFSET[place]))
        for first in range(0, length, BATCH):
            batch = range(first, min(first + BATCH, length))
            values = [acc[at + row : at + row + 1, :] for row in batch]
            places = [canon[0, off + row] for row in batch]
            for to, value in zip(places, values):
                out[to, :, :] = value


def scatter_kernel(canon, acc, out):
    scatter_rows(position(), canon, acc, out)


def split(value, parts):
    out = []
    for _ in range(parts):
        piece = value.astype(BF16)
        out.append(piece)
        value = value - piece.astype(F32)
    return out


def dot(a, b):
    return jnp.dot(a, b, preferred_element_type=F32)


def dot_last(a, b):
    return lax.dot_general(a, b, (((1,), (1,)), ((), ())), preferred_element_type=F32)


def tile(t):
    return pl.ds(pl.multiple_of(t * TILE, TILE), TILE)


def each_tile(body):
    def step(t, _):
        body(tile(t))
        return 0

    lax.fori_loop(0, ROWS // TILE, step, 0)


def select_kernel(plan, canon, one, weight_out, src):
    index = position()
    src[...] = jnp.full(src.shape, -1, jnp.int32)
    weight_out[...] = jnp.zeros(weight_out.shape, F32)
    for slot in PLACES:
        at, length = SLOT_OFFSET[slot], LENGTH[slot]
        src[at : at + length, :] = pick(
            slot, index, lambda place, length=length: canon[CANON_OFFSET[place] : CANON_OFFSET[place] + length, :]
        )
        weight = jnp.float32(1.0)
        for d in range(3):
            if slot[d] == 0:
                weight = weight * 0.5
            elif slot[d] == 2 and plan.sizes[d] > 2:
                weight = weight * jnp.where(has_b(index[d], plan.sizes[d]), 0.5, 1.0)
        weight_out[at : at + length, :] = jnp.full((length, 128), 1.0, F32) * weight

    for t in range(0, ROWS, TILE):
        rows = slice(t, t + TILE)
        hit = src[rows, :] == lax.broadcasted_iota(jnp.int32, (TILE, IFACE), 1)
        one[rows, :] = jnp.where(hit, 1.0, 0.0).astype(BF16)


def spread_kernel(plan, cinv, out):
    nc = cinv.shape[1]
    row = lax.broadcasted_iota(jnp.int32, (nc, plan.wide), 0)
    col = lax.broadcasted_iota(jnp.int32, (nc, plan.wide), 1)
    spread = jnp.where(jnp.logical_and((col >> 3) * 6 + (col & 7) == row, (col & 7) < 6), 1.0, 0.0).astype(BF16)
    value = sum(dot(part, spread) for part in split(cinv[...], 3))
    out[...] = jnp.zeros(out.shape, F32)
    for i in range(plan.setup):
        out[8 * i : 8 * i + 6, :] = value[:, 128 * i : 128 * (i + 1)]


def turn_kernel(one, weight, basis, turned):
    turned[...] = jnp.zeros(turned.shape, F32)
    turned[:, :6] = dot_last(one[...], basis[...]) * weight[:, :6]


def left_tiles(one, matrix, start, stop, out):
    for t in range(start, stop):
        at = (t - start) * TILE
        out[at : at + TILE, :] = dot(one[t * TILE : (t + 1) * TILE, :], matrix[...]).astype(BF16)


def inverse_left_kernel(one, matrix, basis, mid, few):
    left_tiles(one, matrix, 0, CUT_INVERSE, mid)
    few[...] = jnp.zeros(few.shape, F32)
    few[:6, :] = basis[...].astype(F32)
    mid[COARSE_AT : COARSE_AT + 16, :] = few[...].astype(BF16)


def inverse_right_kernel(one, mid, matrix, weight, schur, out, schur_mid, more):
    left_tiles(one, matrix, CUT_INVERSE, TILES, more)
    right(one, (mid, more), weight, out)
    left_tiles(one, schur, 0, CUT_SCHUR, schur_mid)


def schur_right_kernel(one, mid, matrix, out, more):
    left_tiles(one, matrix, CUT_SCHUR, TILES, more)
    right(one, (mid, more), None, out)


def right(one, mids, weight, out):
    order = sorted(range(ROWS // TILE), key=lambda t: (t != COARSE_AT // TILE, t))

    def put(value, i, j):
        if weight is not None:
            scale = weight[i * TILE : (i + 1) * TILE, :1]
            if i == order[0]:
                row = lax.broadcasted_iota(jnp.int32, (TILE, 1), 0) + i * TILE
                inside = jnp.logical_and(row >= COARSE_AT, row < COARSE_AT + 16)
                scale = jnp.where(inside, 1.0, scale)
            value = value * scale
        out[i * TILE : (i + 1) * TILE, j * TILE : (j + 1) * TILE] = value.astype(BF16)

    for a, i in enumerate(order):
        cut = mids[0].shape[0] // TILE
        mid, at = (mids[0], i * TILE) if i < cut else (mids[1], (i - cut) * TILE)
        for j in order[a:]:
            value = dot_last(mid[at : at + TILE, :], one[j * TILE : (j + 1) * TILE, :])
            put(value, i, j)
            if i != j:
                put(value.T, j, i)


def fill(acc, parts):
    at = 0
    for part in parts:
        acc[at : at + part.shape[0], :] = part[...]
        at += part.shape[0]


def known_blocks(plan, kind, own, swapped, arrived, per):
    blocks = own + [ref[8 * i : 8 * (i + 1), :] for ref in swapped for i in range(per)]
    count = len(blocks)
    for message, ref in zip(plan.coarse[kind][0], arrived):
        if message.ride:
            blocks += [ref[message.rows + 8 * i : message.rows + 8 * (i + 1), :] for i in range(count)]
    return blocks


def first_kernel(plan, kind, *refs):
    refs = list(refs)
    base, own = refs.pop(0), refs.pop(0)
    swapped = [refs.pop(0) for _ in plan.before[kind]]
    per = plan.per(kind)
    pack = None
    if kind == "initial":
        turned = refs.pop(0)
        pack = packer(turned, refs.pop(-1), {})
    mine = [own[8 * i : 8 * (i + 1), :] for i in range(per)]
    write_payloads(plan.coarse[kind][0], refs, base, known_blocks(plan, kind, mine, swapped, [], per), pack)


def middle_kernel(plan, kind, count, after, *refs):
    first, second = plan.messages(kind)
    per = plan.per(kind)
    refs = list(refs)
    parts = [refs.pop(0) for _ in range(count)]
    if after:
        refs.pop(0)
    received = [refs.pop(0) for _ in first]
    blocks, pack = [], None
    if per:
        own = refs.pop(0)
        swapped = [refs.pop(0) for _ in plan.before[kind]]
        mine = [own[8 * i : 8 * (i + 1), :] for i in range(per)]
        blocks = known_blocks(plan, kind, mine, swapped, received, per)
    if per and kind == "initial":
        turned = refs.pop(0)
        stage = refs.pop(-1)
        kept = {m: refs.pop(-1) for m in reversed(first) if m.faces}
        for message, ref in zip(first, received):
            if message.faces:
                unpack(message, ref[ref.shape[0] - CHUNK :, :], kept[message])
        pack = packer(turned, stage, kept)
    acc = refs.pop(-1)
    fill(acc, parts)
    add_received(plan, position(), first, received, acc)
    write_payloads(second, refs, acc, blocks, pack)


def product_kernel(part, matrix, vector, out):
    start, stop = PARTS[part]
    size = (stop - start) // (4 if part == "all" else 2)
    for t in range(start, stop, size):
        out[t - start : t - start + size, :] = dot(matrix[t : t + size, :], vector[...])


def finish(plan, kind, parts, got, acc):
    first, second = plan.messages(kind)
    index = position()
    fill(acc, parts)
    add_received(plan, index, first, got[: len(first)], acc)
    add_received(plan, index, second, got[len(first) :], acc)


def residual_kernel(plan, opening, count, *refs):
    kind = "initial" if opening else "plain"
    refs = list(refs)
    parts = [refs.pop(0) for _ in range(count)]
    got = [refs.pop(0) for _ in range(sum(len(m) for m in plan.messages(kind)))]
    matrix, weight = refs.pop(0), refs.pop(0)
    before = None if opening else refs.pop(0)
    residual, rounded, restricted, acc = refs
    finish(plan, kind, parts, got, acc)
    value = acc[...] if opening else before[...] - acc[...]
    residual[...] = value
    rounded[...] = (weight[...] * value).astype(BF16)
    restricted[...] = dot(matrix[COARSE_AT : COARSE_AT + 16, :], rounded[...])[:8]


def lift_kernel(plan, base, turned, correction, out, *outs):
    lifted = turned[...].astype(BF16)
    out[...] = base[...] + sum(dot(lifted, part) for part in split(correction[...], 3))
    write_payloads(plan.plain[0], outs, out, [])


def collect(plan, kind, own, got, per, which, stack, at_column):
    first, second = plan.coarse[kind]
    index = position()
    me = (index[0] * plan.sizes[1] + index[1]) * plan.sizes[2] + index[2]

    def put(code, value):
        stack[pl.ds(pl.multiple_of((me ^ code) * 8, 8), 8), at_column : at_column + 128] = value

    put(0, own[8 * which : 8 * (which + 1), :])
    for m in plan.before[kind]:
        put(m.xor(), got[0][8 * which : 8 * (which + 1), :])
        got = got[1:]
    for stage, messages in enumerate((first, second)):
        for m, ref in zip(messages, got):
            if m.ride:
                for i, code in enumerate(plan.codes(kind, stage)):
                    at = m.rows + 8 * (per * i + which)
                    put(code ^ m.xor(), ref[at : at + 8, :])
        got = got[len(messages) :]


def lifting_kernel(plan, *refs):
    first, second = plan.coarse["initial"]
    turned, spread, *got, out, stack, many, unpacked = refs
    swapped, got = got[: len(plan.before["initial"])], got[len(plan.before["initial"]) :]
    per = plan.setup
    index = position()
    me = (index[0] * plan.sizes[1] + index[1]) * plan.sizes[2] + index[2]

    def place(code, value, to, ok):
        there = me ^ code
        value = pltpu.roll(value, (there & 15) * 8, 1)
        rows = value.shape[0]
        for half in range(per):
            here = both((there >> 4) == half, ok)
            many[to : to + rows, 128 * half : 128 * (half + 1)] += jnp.where(here, value, 0.0)

    many[...] = jnp.zeros(many.shape, F32)
    for t in range(ROWS // TILE):
        place(0, turned[t * TILE : (t + 1) * TILE, :], t * TILE, None)
    for m, ref in zip(first + second, got):
        if not m.faces:
            continue
        unpack(m, ref[ref.shape[0] - CHUNK :, :], unpacked)
        at, ok = 0, exists(plan, index, m)
        for source, slot in m.basis:
            code, fine = m.xor(), ok
            if source is not None:
                code ^= source.xor()
                fine = both(exists(plan, index, source), ok)
            place(code, unpacked[at : at + LENGTH[slot], :], SLOT_OFFSET[slot], fine)
            at += LENGTH[slot]
    for half in range(per):
        collect(plan, "initial", spread, swapped + got, per, half, stack, 128 * half)
    parts = jnp.concatenate(split(stack[...], 3), axis=0)

    def body(rows):
        basis = many[rows, :].astype(BF16)
        whole = dot(jnp.concatenate([basis] * 3, axis=1), parts)
        high, low = split(whole, 2)
        out[rows, :] = jnp.concatenate([high, high, low], axis=1)

    each_tile(body)


def update_kernel(plan, *refs):
    refs = list(refs)
    base = refs.pop(0)
    got = [refs.pop(0) for _ in range(sum(len(m) for m in plan.messages("update")))]
    matrix = refs.pop(0)
    if plan.ride:
        lift, own = refs.pop(0), refs.pop(0)
        swapped = [refs.pop(0) for _ in plan.before["update"]]
        stack = refs.pop(-1)
    acc = refs.pop(-1)
    update, rounded, early, *outs = refs
    finish(plan, "update", [base], got, acc)
    if plan.ride:
        collect(plan, "update", own, swapped + got, 1, 0, stack, 0)
        high, low = split(stack[...], 2)
        right = jnp.concatenate([high, low, high], axis=0)
        for t in range(0, ROWS, 320):
            value = acc[t : t + 320, :] + dot(lift[t : t + 320, :], right)
            update[t : t + 320, :] = value
            rounded[t : t + 320, :] = value.astype(BF16)
    else:
        update[...] = acc[...]
        rounded[...] = acc[...].astype(BF16)
    product_kernel("early", matrix, rounded, early)
    write_payloads(plan.plain[0], outs, early, [])


def later_kernel(opening, matrix, rounded, update, *refs):
    late, total = refs[-2:]
    product_kernel("late", matrix, rounded, late)
    total[...] = update[...] if opening else refs[0][...] + update[...]


def output_kernel(plan, canon, early, late, *refs):
    *got, residual, out, acc = refs
    finish(plan, "plain", [early, late], got, acc)
    acc[...] = residual[...] - acc[...]
    scatter_rows(position(), canon, acc, out)


def local(plan, load_cases, schur_matrix, local_inverse, coarse_basis, coarse_inverse, canon_rows):
    smem = pl.BlockSpec(memory_space=pltpu.SMEM)
    loads = load_cases.shape[-1]
    canon = canon_rows.reshape(1, IFACE)
    load = load_cases.reshape(IFACE, 1, loads)
    basis = coarse_basis[0, 0, 0]
    acc = pltpu.VMEM((ROWS, 128), F32)
    pieces = pltpu.VMEM((16 * CHUNK, 128), F32)
    early_rows, late_rows = SPLIT, ROWS - SPLIT

    def spread_out(kind, own):
        return [own] + transfer(plan.before[kind], [own] * len(plan.before[kind]))

    def first(kind, base, blocks, more):
        return call(
            functools.partial(first_kernel, plan, kind),
            plan.payload_shapes(kind, 0),
            [base] + blocks + more,
            scratch=[pieces] if kind == "initial" else [],
        )

    def assemble(kind, parts, payloads, blocks, more, after=()):
        messages = plan.messages(kind)
        got = transfer(messages[0], payloads)
        setup = kind == "initial" and plan.ride
        payloads = call(
            functools.partial(middle_kernel, plan, kind, len(parts), bool(after)),
            plan.payload_shapes(kind, 1),
            parts + list(after) + got + blocks + (more if setup else []),
            scratch=[acc] + ([pieces] * (1 + sum(m.faces for m in messages[0])) if setup else []),
        )
        return got + transfer(messages[1], payloads)

    one, weight = call(
        functools.partial(select_kernel, plan),
        [shape(ROWS, IFACE, BF16), shape(ROWS, 128)],
        [canon_rows.reshape(IFACE, 1)],
        scratch=[pltpu.VMEM((ROWS, 1), jnp.int32)],
        flops=ROWS * IFACE * 1158,
    )
    if plan.ride:
        (spread,) = call(
            functools.partial(spread_kernel, plan), [shape(8 * plan.setup, 128)], [coarse_inverse]
        )
    (turned,) = call(turn_kernel, [shape(ROWS, 128)], [one, weight, basis])
    (early,) = call(
        functools.partial(gather_kernel, EARLY, 0), [shape(early_rows, 128)], [canon, load], specs=[smem, vm()]
    )
    (late,) = call(
        functools.partial(gather_kernel, LATE, SPLIT), [shape(late_rows, 128)], [canon, load], specs=[smem, vm()]
    )
    flops = 2 * ROWS * IFACE * IFACE
    square = shape(ROWS, ROWS, BF16)

    matrix, other = local_inverse[0, 0, 0], schur_matrix[0, 0, 0]
    (half,) = call(
        inverse_left_kernel,
        [shape(CUT_INVERSE * TILE, IFACE, BF16)],
        [one, matrix, basis],
        scratch=[pltpu.VMEM((16, IFACE), F32)],
        flops=flops,
    )
    inverse, half = call(
        inverse_right_kernel,
        [square, shape(CUT_SCHUR * TILE, IFACE, BF16)],
        [one, half, matrix, weight, other],
        scratch=[pltpu.VMEM(((TILES - CUT_INVERSE) * TILE, IFACE), BF16)],
        limit=24,
        flops=2 * flops,
    )
    blocks = []
    if plan.ride:
        blocks = spread_out("initial", spread)
        payloads = first("initial", early, blocks, [turned])
    else:
        payloads = call(
            lambda base, *outs: write_payloads(plan.plain[0], outs, base, []),
            plan.payload_shapes("plain", 0),
            [early],
        )
    parts = [early, late]
    got = assemble("initial", parts, payloads, blocks, [turned])
    if plan.ride:
        (lift,) = call(
            functools.partial(lifting_kernel, plan),
            [shape(ROWS, 3 * plan.wide, BF16)],
            [turned] + blocks + got,
            scratch=[pltpu.VMEM((plan.wide, plan.wide), F32), pltpu.VMEM((ROWS, plan.wide), F32), pieces],
            flops=2 * ROWS * 3 * plan.wide * plan.wide,
        )
    (schur,) = call(
        schur_right_kernel,
        [square],
        [one, half, other],
        scratch=[pltpu.VMEM(((TILES - CUT_SCHUR) * TILE, IFACE), BF16)],
        flops=flops,
    )
    sol = residual = None
    flops = 2 * ROWS * ROWS * 128
    for iteration in range(ITERS):
        opening = iteration == 0
        residual, rounded, restricted = call(
            functools.partial(residual_kernel, plan, opening, len(parts)),
            [shape(ROWS, 128), shape(ROWS, 128, BF16), shape(8, 128)],
            parts + got + [inverse, weight] + ([] if opening else [residual]),
            scratch=[acc],
        )
        if plan.ride:
            blocks = spread_out("update", restricted)
        (base,) = call(
            functools.partial(product_kernel, "all"), [shape(ROWS, 128)], [inverse, rounded], flops=flops
        )
        if plan.ride:
            payloads = first("update", base, blocks, [])
        else:
            blocks = []
            rows = lax.all_gather(restricted[:6], AXES, axis=0, tiled=True)
            correction = jnp.dot(coarse_inverse, rows, precision=lax.Precision.HIGHEST, preferred_element_type=F32)
            base, *payloads = call(
                functools.partial(lift_kernel, plan),
                [shape(ROWS, 128)] + plan.payload_shapes("plain", 0),
                [base, turned, jnp.pad(correction, ((0, 122), (0, 0)))],
            )
        got = assemble("update", [base], payloads, blocks, [], [lift] if opening and plan.ride else [])
        update, rounded, early, *payloads = call(
            functools.partial(update_kernel, plan),
            [shape(ROWS, 128), shape(ROWS, 128, BF16), shape(early_rows, 128)] + plan.payload_shapes("plain", 0),
            [base] + got + [schur] + ([lift] + blocks if plan.ride else []),
            scratch=[acc] + ([pltpu.VMEM((plan.wide, 128), F32)] if plan.ride else []),
            flops=flops,
        )
        late, sol = call(
            functools.partial(later_kernel, opening),
            [shape(late_rows, 128), shape(ROWS, 128)],
            [schur, rounded, update] + ([] if opening else [sol]),
            flops=flops // 2,
        )
        parts = [early, late]
        got = assemble("plain", parts, payloads, [], [])
    out = jax.ShapeDtypeStruct((IFACE, 1, loads), F32)
    (sol_out,) = call(scatter_kernel, [out], [canon, sol], specs=[smem, vm()])
    (residual_out,) = call(
        functools.partial(output_kernel, plan),
        [out],
        [canon] + parts + got + [residual],
        specs=[smem] + [vm()] * (3 + len(got)),
        scratch=[acc],
    )
    return tuple(o.reshape(1, 1, 1, IFACE, loads) for o in (sol_out, residual_out))


def solution(mesh):
    plan = Plan(tuple(mesh.shape[a] for a in AXES))
    in_specs = (
        P("gx", "gy", "gz", None, None),
        P("gx", "gy", "gz", None, None),
        P("gx", "gy", "gz", None, None),
        P("gx", "gy", "gz", None, None),
        P(("gx", "gy", "gz"), None),
        P("gx", "gy", "gz", None),
    )
    out_specs = (P("gx", "gy", "gz", None, None), P("gx", "gy", "gz", None, None))
    return jax.shard_map(
        functools.partial(local, plan), mesh=mesh, in_specs=in_specs, out_specs=out_specs, check_vma=False
    )
```

```python
import functools
import itertools

import jax
import jax.numpy as jnp
from jax import lax
from jax.experimental import pallas as pl
from jax.experimental.pallas import tpu as pltpu
from jax.sharding import PartitionSpec as P

NODES = 7
DOF = 3
ITERS = 3
AXES = ("gx", "gy", "gz")
STAGES = ((1,), (0, 2))
SPARE = (2, 1)
PAD = 8
CHUNK = 24
TILE = 256
BATCH = 16
F32 = jnp.float32
BF16 = jnp.bfloat16


def piece_length(placed):
    return DOF * NODES ** sum(1 for c in placed if c == 1)


PLACES = [p for p in itertools.product(range(3), repeat=3) if p != (1, 1, 1)]
CANON_OFFSET = {}
_at = 0
for _p in PLACES:
    CANON_OFFSET[_p] = _at
    _at += piece_length(_p)
IFACE = _at
LENGTH = {p: piece_length(p) for p in PLACES}
EARLY = [p for p in PLACES if p[1] != 1]
LATE = [p for p in PLACES if p[1] == 1]
SLOT_OFFSET = {}


def _lay(slots, at):
    for slot in slots:
        SLOT_OFFSET[slot] = at
        at += -(-LENGTH[slot] // PAD) * PAD
    return at


COARSE_AT = _lay(EARLY, 0)
SPLIT = -(-(COARSE_AT + 16) // 16) * 16
ROWS = -(-_lay(LATE, SPLIT) // TILE) * TILE
TILES = ROWS // TILE
CUT_INVERSE = 3
CUT_SCHUR = 2
PARTS = {"all": (0, ROWS), "early": (0, SPLIT), "late": (SPLIT, ROWS)}


class Message:
    def __init__(self, moves, sizes, wrap, ride, spare):
        self.moves = moves
        self.sizes = sizes
        self.wrap = wrap
        self.ride = ride
        self.spare = spare
        self.faces = not any(m in ("C", "W") for m in moves)
        self.slots = []
        if self.faces:
            for place in EARLY + LATE:
                if all(m is None or c == (0 if m == "A" else 2) for m, c in zip(moves, place)):
                    self.slots.append(place)
        self.rows = -(-sum(LENGTH[s] for s in self.slots) // PAD) * PAD
        self.basis = []

    def xor(self):
        code = 0
        for move, size in zip(self.moves, self.sizes):
            code = code * size + {None: 0, "A": 1, "B": 3, "C": 2, "W": 3}[move]
        return code

    def pairs(self):
        out = []
        for place in itertools.product(*(range(s) for s in self.sizes)):
            to, whole = [], True
            for at, move, size in zip(place, self.moves, self.sizes):
                if move == "A":
                    at = at ^ 1
                elif move == "B":
                    whole = whole and (self.wrap or 0 < at < size - 1)
                    at = (at - 1) % size if at % 2 == 0 else (at + 1) % size
                elif move == "C":
                    at = at ^ 2
                elif move == "W":
                    at = at ^ 3
                to.append(at)
            if not whole:
                to = [at ^ 1 if d == self.spare else at for d, at in enumerate(place)]
            flat = [0, 0]
            for a, b, size in zip(place, to, self.sizes):
                flat = [flat[0] * size + a, flat[1] * size + b]
            out.append(tuple(flat))
        return out


def stage_messages(stage, sizes, coarse=None):
    choices = []
    for d in range(3):
        if d not in STAGES[stage]:
            choices.append((None,))
        else:
            extra = ("C", "W") if coarse == "update" and stage == 0 and sizes[d] == 4 else ()
            choices.append((None, "A") + (("B",) if sizes[d] > 2 else ()) + extra)
    out = []
    for moves in itertools.product(*choices):
        if all(m is None for m in moves):
            continue
        ride = coarse and (moves[1] != "B" if stage == 0 else moves[2] != "A")
        out.append(Message(moves, sizes, ride and stage == 1, ride, SPARE[stage]))
    return out


class Plan:
    def __init__(self, sizes):
        self.sizes = sizes
        self.subs = sizes[0] * sizes[1] * sizes[2]
        self.ride = all(s in (2, 4) for s in sizes)
        self.wide = self.subs * 8
        self.plain = [stage_messages(i, sizes) for i in range(2)]
        self.setup = 0
        if self.ride:
            self.setup = self.wide // 128
            self.coarse = {k: [stage_messages(i, sizes, k) for i in range(2)] for k in ("initial", "update")}
            self.before = {"update": [Message((None, None, "A"), sizes, False, True, 0)]}
            self.before["initial"] = list(self.before["update"])
            if sizes[1] == 4:
                more = [(None, "C", None), (None, "C", "A")]
                self.before["initial"] += [Message(m, sizes, False, True, 0) for m in more]
            first, second = self.coarse["initial"]
            for message in first:
                message.basis = [(None, slot) for slot in message.slots]
            for message in second:
                message.basis = [(None, slot) for slot in message.slots]
                for other in first:
                    message.basis += [(other, slot) for slot in message.slots if slot in other.slots]

    def per(self, kind):
        return {"plain": 0, "update": 1, "initial": self.setup}[kind] if self.ride else 0

    def messages(self, kind):
        return self.plain if self.per(kind) == 0 else self.coarse[kind]

    def codes(self, kind, stage):
        known = [0] + [m.xor() for m in self.before[kind]]
        if stage == 1:
            known = [k ^ m for m in [0] + [m.xor() for m in self.coarse[kind][0] if m.ride] for k in known]
        return known

    def payload_shapes(self, kind, stage):
        per = self.per(kind)
        out = []
        for m in self.messages(kind)[stage]:
            rows = m.rows
            if m.ride:
                rows += 8 * per * len(self.codes(kind, stage))
            if kind == "initial" and self.ride and m.faces:
                rows += CHUNK
            out.append(shape(rows, 128))
        return out


def position():
    return [lax.axis_index(a) for a in AXES]


def has_b(index, size):
    return jnp.logical_and(index > 0, index < size - 1)


def exists(plan, index, message):
    ok = None
    for d, move in enumerate(message.moves):
        if move == "B":
            here = has_b(index[d], plan.sizes[d])
            ok = here if ok is None else jnp.logical_and(ok, here)
    return ok


def both(a, b):
    return b if a is None else a if b is None else jnp.logical_and(a, b)


def pick(slot, index, of):
    def choose(d, place):
        if d == 3:
            return of(tuple(place))
        if slot[d] == 1:
            return choose(d + 1, place + [1])
        even, odd = (2, 0) if slot[d] == 0 else (0, 2)
        return jnp.where(index[d] % 2 == 0, choose(d + 1, place + [even]), choose(d + 1, place + [odd]))

    return choose(0, [])


def add_received(plan, index, messages, received, acc):
    for message, ref in zip(messages, received):
        if not message.faces:
            continue
        ok = exists(plan, index, message)
        at = 0
        for slot in message.slots:
            rows, to = LENGTH[slot], SLOT_OFFSET[slot]
            value = ref[at : at + rows, :]
            if ok is not None:
                value = jnp.where(ok, value, 0.0)
            acc[to : to + rows, :] += value
            at += rows


def write_payloads(messages, outs, acc, blocks, pack=None):
    for message, out in zip(messages, outs):
        at = 0
        for slot in message.slots:
            rows, frm = LENGTH[slot], SLOT_OFFSET[slot]
            out[at : at + rows, :] = acc[frm : frm + rows, :]
            at += rows
        at = message.rows
        if message.ride:
            for block in blocks:
                out[at : at + 8, :] = block
                at += 8
        if pack is not None and message.faces:
            out[at : at + CHUNK, :] = pack(message)


def packer(own, stage, unpacked):
    def pack(message):
        at = 0
        for source, slot in message.basis:
            rows = LENGTH[slot]
            if source is not None:
                ref = unpacked[source]
                frm = sum(LENGTH[s] for s in source.slots[: source.slots.index(slot)])
            else:
                ref, frm = own, SLOT_OFFSET[slot]
            stage[at : at + rows, :] = ref[frm : frm + rows, :]
            at += rows
        count = -(-at // CHUNK)
        if at < count * CHUNK:
            stage[at : count * CHUNK, :] = jnp.zeros((count * CHUNK - at, 128), F32)
        total = stage[0:CHUNK, :]
        for k in range(1, count):
            total += pltpu.roll(stage[k * CHUNK : (k + 1) * CHUNK, :], 8 * k, 1)
        return total

    return pack


def unpack(message, block, out):
    count = -(-sum(LENGTH[slot] for _, slot in message.basis) // CHUNK)
    lane = lax.broadcasted_iota(jnp.int32, (CHUNK, 128), 1)
    for k in range(count):
        turned = pltpu.roll(block, 128 - 8 * k, 1) if k else block
        out[k * CHUNK : (k + 1) * CHUNK, :] = jnp.where(lane < 8, turned, 0.0)


def transfer(messages, payloads):
    return [lax.ppermute(p, AXES, m.pairs()) for m, p in zip(messages, payloads)]


def vm():
    return pl.BlockSpec(memory_space=pltpu.VMEM)


def shape(rows, cols, dtype=F32):
    return jax.ShapeDtypeStruct((rows, cols), dtype)


def call(kernel, outs, operands, specs=None, scratch=(), limit=20, flops=0):
    nbytes = sum(o.size * o.dtype.itemsize for o in list(outs) + list(operands))
    return pl.pallas_call(
        kernel,
        out_shape=tuple(outs),
        in_specs=specs or [vm()] * len(operands),
        out_specs=tuple(vm() for _ in outs),
        scratch_shapes=list(scratch),
        compiler_params=pltpu.CompilerParams(vmem_limit_bytes=limit << 20),
        cost_estimate=pl.CostEstimate(flops=flops, bytes_accessed=nbytes, transcendentals=0),
    )(*operands)


def gather_kernel(slots, start, canon, load, acc):
    index = position()
    acc[...] = jnp.zeros(acc.shape, F32)
    for slot in slots:
        length, at = LENGTH[slot], SLOT_OFFSET[slot] - start
        off = pick(slot, index, lambda place: jnp.int32(CANON_OFFSET[place]))
        for first in range(0, length, BATCH):
            batch = range(first, min(first + BATCH, length))
            values = [load[canon[0, off + row], :, :] for row in batch]
            for row, value in zip(batch, values):
                acc[at + row : at + row + 1, :] = value


def scatter_rows(index, canon, acc, out):
    for slot in PLACES:
        length, at = LENGTH[slot], SLOT_OFFSET[slot]
        off = pick(slot, index, lambda place: jnp.int32(CANON_OFFSET[place]))
        for first in range(0, length, BATCH):
            batch = range(first, min(first + BATCH, length))
            values = [acc[at + row : at + row + 1, :] for row in batch]
            places = [canon[0, off + row] for row in batch]
            for to, value in zip(places, values):
                out[to, :, :] = value


def scatter_kernel(canon, acc, out):
    scatter_rows(position(), canon, acc, out)


def split(value, parts):
    out = []
    for _ in range(parts):
        piece = value.astype(BF16)
        out.append(piece)
        value = value - piece.astype(F32)
    return out


def dot(a, b):
    return jnp.dot(a, b, preferred_element_type=F32)


def dot_last(a, b):
    return lax.dot_general(a, b, (((1,), (1,)), ((), ())), preferred_element_type=F32)


def tile(t):
    return pl.ds(pl.multiple_of(t * TILE, TILE), TILE)


def each_tile(body):
    def step(t, _):
        body(tile(t))
        return 0

    lax.fori_loop(0, ROWS // TILE, step, 0)


def select_kernel(plan, canon, one, weight_out, src):
    index = position()
    src[...] = jnp.full(src.shape, -1, jnp.int32)
    weight_out[...] = jnp.zeros(weight_out.shape, F32)
    for slot in PLACES:
        at, length = SLOT_OFFSET[slot], LENGTH[slot]
        src[at : at + length, :] = pick(
            slot, index, lambda place, length=length: canon[CANON_OFFSET[place] : CANON_OFFSET[place] + length, :]
        )
        weight = jnp.float32(1.0)
        for d in range(3):
            if slot[d] == 0:
                weight = weight * 0.5
            elif slot[d] == 2 and plan.sizes[d] > 2:
                weight = weight * jnp.where(has_b(index[d], plan.sizes[d]), 0.5, 1.0)
        weight_out[at : at + length, :] = jnp.full((length, 128), 1.0, F32) * weight

    for t in range(0, ROWS, TILE):
        rows = slice(t, t + TILE)
        hit = src[rows, :] == lax.broadcasted_iota(jnp.int32, (TILE, IFACE), 1)
        one[rows, :] = jnp.where(hit, 1.0, 0.0).astype(BF16)


def spread_kernel(plan, cinv, out):
    nc = cinv.shape[1]
    row = lax.broadcasted_iota(jnp.int32, (nc, plan.wide), 0)
    col = lax.broadcasted_iota(jnp.int32, (nc, plan.wide), 1)
    spread = jnp.where(jnp.logical_and((col >> 3) * 6 + (col & 7) == row, (col & 7) < 6), 1.0, 0.0).astype(BF16)
    value = sum(dot(part, spread) for part in split(cinv[...], 3))
    out[...] = jnp.zeros(out.shape, F32)
    for i in range(plan.setup):
        out[8 * i : 8 * i + 6, :] = value[:, 128 * i : 128 * (i + 1)]


def turn_kernel(one, weight, basis, turned):
    turned[...] = jnp.zeros(turned.shape, F32)
    turned[:, :6] = dot_last(one[...], basis[...]) * weight[:, :6]


def left_tiles(one, matrix, start, stop, out):
    for t in range(start, stop):
        at = (t - start) * TILE
        out[at : at + TILE, :] = dot(one[t * TILE : (t + 1) * TILE, :], matrix[...]).astype(BF16)


def inverse_left_kernel(one, matrix, basis, mid, few):
    left_tiles(one, matrix, 0, CUT_INVERSE, mid)
    few[...] = jnp.zeros(few.shape, F32)
    few[:6, :] = basis[...].astype(F32)
    mid[COARSE_AT : COARSE_AT + 16, :] = few[...].astype(BF16)


def inverse_right_kernel(one, mid, matrix, weight, schur, out, schur_mid, more):
    left_tiles(one, matrix, CUT_INVERSE, TILES, more)
    right(one, (mid, more), weight, out)
    left_tiles(one, schur, 0, CUT_SCHUR, schur_mid)


def schur_right_kernel(one, mid, matrix, out, more):
    left_tiles(one, matrix, CUT_SCHUR, TILES, more)
    right(one, (mid, more), None, out)


def right(one, mids, weight, out):
    order = sorted(range(ROWS // TILE), key=lambda t: (t != COARSE_AT // TILE, t))

    def put(value, i, j):
        if weight is not None:
            scale = weight[i * TILE : (i + 1) * TILE, :1]
            if i == order[0]:
                row = lax.broadcasted_iota(jnp.int32, (TILE, 1), 0) + i * TILE
                inside = jnp.logical_and(row >= COARSE_AT, row < COARSE_AT + 16)
                scale = jnp.where(inside, 1.0, scale)
            value = value * scale
        out[i * TILE : (i + 1) * TILE, j * TILE : (j + 1) * TILE] = value.astype(BF16)

    for a, i in enumerate(order):
        cut = mids[0].shape[0] // TILE
        mid, at = (mids[0], i * TILE) if i < cut else (mids[1], (i - cut) * TILE)
        for j in order[a:]:
            value = dot_last(mid[at : at + TILE, :], one[j * TILE : (j + 1) * TILE, :])
            put(value, i, j)
            if i != j:
                put(value.T, j, i)


def fill(acc, parts):
    at = 0
    for part in parts:
        acc[at : at + part.shape[0], :] = part[...]
        at += part.shape[0]


def known_blocks(plan, kind, own, swapped, arrived, per):
    blocks = own + [ref[8 * i : 8 * (i + 1), :] for ref in swapped for i in range(per)]
    count = len(blocks)
    for message, ref in zip(plan.coarse[kind][0], arrived):
        if message.ride:
            blocks += [ref[message.rows + 8 * i : message.rows + 8 * (i + 1), :] for i in range(count)]
    return blocks


def first_kernel(plan, kind, *refs):
    refs = list(refs)
    base, own = refs.pop(0), refs.pop(0)
    swapped = [refs.pop(0) for _ in plan.before[kind]]
    per = plan.per(kind)
    pack = None
    if kind == "initial":
        turned = refs.pop(0)
        pack = packer(turned, refs.pop(-1), {})
    mine = [own[8 * i : 8 * (i + 1), :] for i in range(per)]
    write_payloads(plan.coarse[kind][0], refs, base, known_blocks(plan, kind, mine, swapped, [], per), pack)


def middle_kernel(plan, kind, count, after, *refs):
    first, second = plan.messages(kind)
    per = plan.per(kind)
    refs = list(refs)
    parts = [refs.pop(0) for _ in range(count)]
    if after:
        refs.pop(0)
    received = [refs.pop(0) for _ in first]
    blocks, pack = [], None
    if per:
        own = refs.pop(0)
        swapped = [refs.pop(0) for _ in plan.before[kind]]
        mine = [own[8 * i : 8 * (i + 1), :] for i in range(per)]
        blocks = known_blocks(plan, kind, mine, swapped, received, per)
    if per and kind == "initial":
        turned = refs.pop(0)
        stage = refs.pop(-1)
        kept = {m: refs.pop(-1) for m in reversed(first) if m.faces}
        for message, ref in zip(first, received):
            if message.faces:
                unpack(message, ref[ref.shape[0] - CHUNK :, :], kept[message])
        pack = packer(turned, stage, kept)
    acc = refs.pop(-1)
    fill(acc, parts)
    add_received(plan, position(), first, received, acc)
    write_payloads(second, refs, acc, blocks, pack)


def product_kernel(part, matrix, vector, out):
    start, stop = PARTS[part]
    size = (stop - start) // (4 if part == "all" else 2)
    for t in range(start, stop, size):
        out[t - start : t - start + size, :] = dot(matrix[t : t + size, :], vector[...])


def finish(plan, kind, parts, got, acc):
    first, second = plan.messages(kind)
    index = position()
    fill(acc, parts)
    add_received(plan, index, first, got[: len(first)], acc)
    add_received(plan, index, second, got[len(first) :], acc)


def residual_kernel(plan, opening, count, *refs):
    kind = "initial" if opening else "plain"
    refs = list(refs)
    parts = [refs.pop(0) for _ in range(count)]
    got = [refs.pop(0) for _ in range(sum(len(m) for m in plan.messages(kind)))]
    matrix, weight = refs.pop(0), refs.pop(0)
    before = None if opening else refs.pop(0)
    residual, rounded, restricted, acc = refs
    finish(plan, kind, parts, got, acc)
    value = acc[...] if opening else before[...] - acc[...]
    residual[...] = value
    rounded[...] = (weight[...] * value).astype(BF16)
    restricted[...] = dot(matrix[COARSE_AT : COARSE_AT + 16, :], rounded[...])[:8]


def lift_kernel(plan, base, turned, correction, out, *outs):
    lifted = turned[...].astype(BF16)
    out[...] = base[...] + sum(dot(lifted, part) for part in split(correction[...], 3))
    write_payloads(plan.plain[0], outs, out, [])


def collect(plan, kind, own, got, per, which, stack, at_column):
    first, second = plan.coarse[kind]
    index = position()
    me = (index[0] * plan.sizes[1] + index[1]) * plan.sizes[2] + index[2]

    def put(code, value):
        stack[pl.ds(pl.multiple_of((me ^ code) * 8, 8), 8), at_column : at_column + 128] = value

    put(0, own[8 * which : 8 * (which + 1), :])
    for m in plan.before[kind]:
        put(m.xor(), got[0][8 * which : 8 * (which + 1), :])
        got = got[1:]
    for stage, messages in enumerate((first, second)):
        for m, ref in zip(messages, got):
            if m.ride:
                for i, code in enumerate(plan.codes(kind, stage)):
                    at = m.rows + 8 * (per * i + which)
                    put(code ^ m.xor(), ref[at : at + 8, :])
        got = got[len(messages) :]


def lifting_kernel(plan, *refs):
    first, second = plan.coarse["initial"]
    turned, spread, *got, out, stack, many, unpacked = refs
    swapped, got = got[: len(plan.before["initial"])], got[len(plan.before["initial"]) :]
    per = plan.setup
    index = position()
    me = (index[0] * plan.sizes[1] + index[1]) * plan.sizes[2] + index[2]

    def place(code, value, to, ok):
        there = me ^ code
        value = pltpu.roll(value, (there & 15) * 8, 1)
        rows = value.shape[0]
        for half in range(per):
            here = both((there >> 4) == half, ok)
            many[to : to + rows, 128 * half : 128 * (half + 1)] += jnp.where(here, value, 0.0)

    many[...] = jnp.zeros(many.shape, F32)
    for t in range(ROWS // TILE):
        place(0, turned[t * TILE : (t + 1) * TILE, :], t * TILE, None)
    for m, ref in zip(first + second, got):
        if not m.faces:
            continue
        unpack(m, ref[ref.shape[0] - CHUNK :, :], unpacked)
        at, ok = 0, exists(plan, index, m)
        for source, slot in m.basis:
            code, fine = m.xor(), ok
            if source is not None:
                code ^= source.xor()
                fine = both(exists(plan, index, source), ok)
            place(code, unpacked[at : at + LENGTH[slot], :], SLOT_OFFSET[slot], fine)
            at += LENGTH[slot]
    for half in range(per):
        collect(plan, "initial", spread, swapped + got, per, half, stack, 128 * half)
    parts = jnp.concatenate(split(stack[...], 3), axis=0)

    def body(rows):
        basis = many[rows, :].astype(BF16)
        whole = dot(jnp.concatenate([basis] * 3, axis=1), parts)
        high, low = split(whole, 2)
        out[rows, :] = jnp.concatenate([high, low], axis=1)

    each_tile(body)


def update_kernel(plan, *refs):
    refs = list(refs)
    base = refs.pop(0)
    got = [refs.pop(0) for _ in range(sum(len(m) for m in plan.messages("update")))]
    matrix = refs.pop(0)
    if plan.ride:
        lift, own = refs.pop(0), refs.pop(0)
        swapped = [refs.pop(0) for _ in plan.before["update"]]
        stack = refs.pop(-1)
    acc = refs.pop(-1)
    update, rounded, early, *outs = refs
    finish(plan, "update", [base], got, acc)
    if plan.ride:
        collect(plan, "update", own, swapped + got, 1, 0, stack, 0)
        high, low = split(stack[...], 2)
        right = jnp.concatenate([high, low], axis=1)
        for t in range(0, ROWS, 320):
            both_parts = dot(lift[t : t + 320, : plan.wide], right)
            value = dot(lift[t : t + 320, plan.wide :], high) + both_parts[:, 128:]
            value = acc[t : t + 320, :] + (both_parts[:, :128] + value)
            update[t : t + 320, :] = value
            rounded[t : t + 320, :] = value.astype(BF16)
    else:
        update[...] = acc[...]
        rounded[...] = acc[...].astype(BF16)
    product_kernel("early", matrix, rounded, early)
    write_payloads(plan.plain[0], outs, early, [])


def later_kernel(opening, matrix, rounded, update, *refs):
    late, total = refs[-2:]
    product_kernel("late", matrix, rounded, late)
    total[...] = update[...] if opening else refs[0][...] + update[...]


def output_kernel(plan, canon, early, late, *refs):
    *got, residual, out, acc = refs
    finish(plan, "plain", [early, late], got, acc)
    acc[...] = residual[...] - acc[...]
    scatter_rows(position(), canon, acc, out)


def local(plan, load_cases, schur_matrix, local_inverse, coarse_basis, coarse_inverse, canon_rows):
    smem = pl.BlockSpec(memory_space=pltpu.SMEM)
    loads = load_cases.shape[-1]
    canon = canon_rows.reshape(1, IFACE)
    load = load_cases.reshape(IFACE, 1, loads)
    basis = coarse_basis[0, 0, 0]
    acc = pltpu.VMEM((ROWS, 128), F32)
    pieces = pltpu.VMEM((16 * CHUNK, 128), F32)
    early_rows, late_rows = SPLIT, ROWS - SPLIT

    def spread_out(kind, own):
        return [own] + transfer(plan.before[kind], [own] * len(plan.before[kind]))

    def first(kind, base, blocks, more):
        return call(
            functools.partial(first_kernel, plan, kind),
            plan.payload_shapes(kind, 0),
            [base] + blocks + more,
            scratch=[pieces] if kind == "initial" else [],
        )

    def assemble(kind, parts, payloads, blocks, more, after=()):
        messages = plan.messages(kind)
        got = transfer(messages[0], payloads)
        setup = kind == "initial" and plan.ride
        payloads = call(
            functools.partial(middle_kernel, plan, kind, len(parts), bool(after)),
            plan.payload_shapes(kind, 1),
            parts + list(after) + got + blocks + (more if setup else []),
            scratch=[acc] + ([pieces] * (1 + sum(m.faces for m in messages[0])) if setup else []),
        )
        return got + transfer(messages[1], payloads)

    one, weight = call(
        functools.partial(select_kernel, plan),
        [shape(ROWS, IFACE, BF16), shape(ROWS, 128)],
        [canon_rows.reshape(IFACE, 1)],
        scratch=[pltpu.VMEM((ROWS, 1), jnp.int32)],
        flops=ROWS * IFACE * 1158,
    )
    if plan.ride:
        (spread,) = call(
            functools.partial(spread_kernel, plan), [shape(8 * plan.setup, 128)], [coarse_inverse]
        )
    (turned,) = call(turn_kernel, [shape(ROWS, 128)], [one, weight, basis])
    (early,) = call(
        functools.partial(gather_kernel, EARLY, 0), [shape(early_rows, 128)], [canon, load], specs=[smem, vm()]
    )
    (late,) = call(
        functools.partial(gather_kernel, LATE, SPLIT), [shape(late_rows, 128)], [canon, load], specs=[smem, vm()]
    )
    flops = 2 * ROWS * IFACE * IFACE
    square = shape(ROWS, ROWS, BF16)

    matrix, other = local_inverse[0, 0, 0], schur_matrix[0, 0, 0]
    (half,) = call(
        inverse_left_kernel,
        [shape(CUT_INVERSE * TILE, IFACE, BF16)],
        [one, matrix, basis],
        scratch=[pltpu.VMEM((16, IFACE), F32)],
        flops=flops,
    )
    inverse, half = call(
        inverse_right_kernel,
        [square, shape(CUT_SCHUR * TILE, IFACE, BF16)],
        [one, half, matrix, weight, other],
        scratch=[pltpu.VMEM(((TILES - CUT_INVERSE) * TILE, IFACE), BF16)],
        limit=24,
        flops=2 * flops,
    )
    blocks = []
    if plan.ride:
        blocks = spread_out("initial", spread)
        payloads = first("initial", early, blocks, [turned])
    else:
        payloads = call(
            lambda base, *outs: write_payloads(plan.plain[0], outs, base, []),
            plan.payload_shapes("plain", 0),
            [early],
        )
    parts = [early, late]
    got = assemble("initial", parts, payloads, blocks, [turned])
    if plan.ride:
        (lift,) = call(
            functools.partial(lifting_kernel, plan),
            [shape(ROWS, 2 * plan.wide, BF16)],
            [turned] + blocks + got,
            scratch=[pltpu.VMEM((plan.wide, plan.wide), F32), pltpu.VMEM((ROWS, plan.wide), F32), pieces],
            flops=2 * ROWS * 3 * plan.wide * plan.wide,
        )
    (schur,) = call(
        schur_right_kernel,
        [square],
        [one, half, other],
        scratch=[pltpu.VMEM(((TILES - CUT_SCHUR) * TILE, IFACE), BF16)],
        flops=flops,
    )
    sol = residual = None
    flops = 2 * ROWS * ROWS * 128
    for iteration in range(ITERS):
        opening = iteration == 0
        residual, rounded, restricted = call(
            functools.partial(residual_kernel, plan, opening, len(parts)),
            [shape(ROWS, 128), shape(ROWS, 128, BF16), shape(8, 128)],
            parts + got + [inverse, weight] + ([] if opening else [residual]),
            scratch=[acc],
        )
        if plan.ride:
            blocks = spread_out("update", restricted)
        (base,) = call(
            functools.partial(product_kernel, "all"), [shape(ROWS, 128)], [inverse, rounded], flops=flops
        )
        if plan.ride:
            payloads = first("update", base, blocks, [])
        else:
            blocks = []
            rows = lax.all_gather(restricted[:6], AXES, axis=0, tiled=True)
            correction = jnp.dot(coarse_inverse, rows, precision=lax.Precision.HIGHEST, preferred_element_type=F32)
            base, *payloads = call(
                functools.partial(lift_kernel, plan),
                [shape(ROWS, 128)] + plan.payload_shapes("plain", 0),
                [base, turned, jnp.pad(correction, ((0, 122), (0, 0)))],
            )
        got = assemble("update", [base], payloads, blocks, [], [lift] if opening and plan.ride else [])
        update, rounded, early, *payloads = call(
            functools.partial(update_kernel, plan),
            [shape(ROWS, 128), shape(ROWS, 128, BF16), shape(early_rows, 128)] + plan.payload_shapes("plain", 0),
            [base] + got + [schur] + ([lift] + blocks if plan.ride else []),
            scratch=[acc] + ([pltpu.VMEM((plan.wide, 128), F32)] if plan.ride else []),
            flops=flops,
        )
        late, sol = call(
            functools.partial(later_kernel, opening),
            [shape(late_rows, 128), shape(ROWS, 128)],
            [schur, rounded, update] + ([] if opening else [sol]),
            flops=flops // 2,
        )
        parts = [early, late]
        got = assemble("plain", parts, payloads, [], [])
    out = jax.ShapeDtypeStruct((IFACE, 1, loads), F32)
    (sol_out,) = call(scatter_kernel, [out], [canon, sol], specs=[smem, vm()])
    (residual_out,) = call(
        functools.partial(output_kernel, plan),
        [out],
        [canon] + parts + got + [residual],
        specs=[smem] + [vm()] * (3 + len(got)),
        scratch=[acc],
    )
    return tuple(o.reshape(1, 1, 1, IFACE, loads) for o in (sol_out, residual_out))


def solution(mesh):
    plan = Plan(tuple(mesh.shape[a] for a in AXES))
    in_specs = (
        P("gx", "gy", "gz", None, None),
        P("gx", "gy", "gz", None, None),
        P("gx", "gy", "gz", None, None),
        P("gx", "gy", "gz", None, None),
        P(("gx", "gy", "gz"), None),
        P("gx", "gy", "gz", None),
    )
    out_specs = (P("gx", "gy", "gz", None, None), P("gx", "gy", "gz", None, None))
    return jax.shard_map(
        functools.partial(local, plan), mesh=mesh, in_specs=in_specs, out_specs=out_specs, check_vma=False
    )
```
